256 devices in a mesh: east: 16 (over x, z_hi), north: 16 (over y, z_lo, core).
Axes of the slice: x: 4, y: 4, z: 8 (z_hi: 4, z_lo: 2; z = z_hi * 2 + z_lo), core: 2. Of those that a mesh axis runs over, the one named last changes fastest.
Arguments:
- features: bfloat16 [96, 128, 2048], P(None, 'east', 'north'), may hold values from -6 to 6
- occupancy: int32 [16, 16, 2], P('east', 'north'), may hold values from 0 to 1, as said below
- weight_first: bfloat16 [27, 96, 96], replicated, may hold values from -0.125 to 0.125
- weight_second: bfloat16 [27, 96, 96], replicated, may hold values from -0.125 to 0.125
- cotangent: bfloat16 [96, 128, 2048], P(None, 'east', 'north'), may hold values from -6 to 6
Outputs:
- activated: bfloat16 [96, 128, 2048], P(None, 'east', 'north')
- feature_grad: bfloat16 [96, 128, 2048], P(None, 'east', 'north')
- grad_first: float32 [248832], P(('east', 'north'))
- grad_second: float32 [248832], P(('east', 'north'))
The draws below stay inside these ranges and needn't reach their ends.
Inputs may be any that keep to these rules, and one draw needn't show every extreme that they name: `occupancy`: every ground cell's column holds at least one occupied block; occupied blocks of a column lie in one run of consecutive heights.
All inputs are finite; a program needn't handle non-finite values.
Results may differ from the reference program's by a relative error of at most 0.0085.
Values may be sent and summed in bfloat16 or wider, within the bound.
No kernel may reach another device: no remote copies, remote signals or barrier semaphores. Data moves between devices by JAX's collectives and lax.ppermute only.
A program may use at most 64 MiB of HBM per device.

```python
import math
import jax
import jax.numpy as jnp
from jax import lax

CH = 96
EDGE = 8
ZH = 16
NX = 128
NY = 128


def draw_occupancy(key, part):
    key = jax.random.fold_in(key, 11)
    key_coarse, key_jitter, key_kind = jax.random.split(key, 3)
    east_blocks = NX // EDGE
    north_blocks = NY // EDGE
    levels = ZH // EDGE
    coarse = jax.random.randint(key_coarse, (east_blocks // 2 + 1, north_blocks // 2 + 1), 0, max(levels // 2, 1))
    ground = jnp.repeat(jnp.repeat(coarse, 2, 0), 2, 1)[:east_blocks, :north_blocks]
    ground = jnp.minimum(ground + jax.random.randint(key_jitter, (east_blocks, north_blocks), 0, 2), levels - 1)
    kind = jax.random.randint(key_kind, (east_blocks, north_blocks), 0, 4)
    top = jnp.where(kind == 3, levels - 1, jnp.where(kind == 2, jnp.minimum(ground + 1, levels - 1), ground))
    height = jnp.arange(levels, dtype=jnp.int32)[None, None, :]
    filled = (height >= ground[:, :, None]) & (height <= top[:, :, None])
    return filled.astype(jnp.int32)


def block_levels(own_key, shape, cuts, low, top_value):
    gain, own = 1.0, jax.random.fold_in(own_key, 6)
    for position, shards_of in cuts:
        heights = jnp.exp(jax.random.uniform(jax.random.fold_in(own, position), (shards_of,), jnp.float32, low / len(cuts), top_value / len(cuts)))
        gain = gain * jnp.repeat(heights, shape[position] // shards_of).reshape([-1 if axis == position else 1 for axis in range(len(shape))])
    return gain


def bell_draw(rng, extent, width, limit, pieces=(), kind=jnp.bfloat16):
    loudness = block_levels(rng, extent, pieces, -0.22, 0.18) if pieces else 1.0
    array = jax.random.normal(rng, extent, jnp.float32) * width * loudness
    return jnp.minimum(jnp.maximum(array, -limit), limit).astype(kind)


def setup_inputs(seed: int = 0) -> dict:
    streams_of = jax.random.split(jax.random.key(seed), 6)
    features = bell_draw(streams_of[0], (CH, NX, NY * ZH), 1.0, 6.0, ((1, 16), (2, 16)))
    occupancy = draw_occupancy(jax.random.fold_in(streams_of[5], 71), 0)
    weight_first = bell_draw(streams_of[2], (27, CH, CH), (27 * CH) ** -0.5, 0.125)
    weight_second = bell_draw(streams_of[3], (27, CH, CH), (27 * CH) ** -0.5, 0.125)
    cotangent = bell_draw(streams_of[4], (CH, NX, NY * ZH), 1.0, 6.0, ((1, 16), (2, 16)))
    return dict(features=features, occupancy=occupancy, weight_first=weight_first, weight_second=weight_second, cotangent=cotangent)


def shifted(window, offset, transposed, width_x, width_y, depth):
    start_x = offset // 9
    start_y = offset // 3 % 3
    start_z = offset % 3
    if transposed:
        start_x, start_y, start_z = (2 - start_x, 2 - start_y, 2 - start_z)
    piece = window[:, start_x:start_x + width_x, start_y:start_y + width_y, start_z:start_z + depth]
    return piece.reshape(piece.shape[0], -1)

def conv_window(window, weight, transposed):
    width_x = window.shape[1] - 2
    width_y = window.shape[2] - 2
    depth = window.shape[3] - 2
    total = jnp.zeros((weight.shape[2], width_x * width_y * depth), jnp.float32)
    for offset in range(27):
        matrix = weight[offset] if transposed else weight[offset].T
        total = total + jnp.dot(matrix, shifted(window, offset, transposed, width_x, width_y, depth), preferred_element_type=jnp.float32)
    return total.reshape(weight.shape[2], width_x, width_y, depth)

def grad_window(window, cotan):
    flat = cotan.reshape(cotan.shape[0], -1)
    parts = []
    for offset in range(27):
        piece = shifted(window, offset, False, cotan.shape[1], cotan.shape[2], cotan.shape[3])
        parts.append(lax.dot_general(piece, flat, (((1,), (1,)), ((), ())), preferred_element_type=jnp.float32))
    return jnp.stack(parts)

def silu_slope(value):
    sigma = jax.nn.sigmoid(value)
    return sigma * (1.0 + value * (1.0 - sigma))

def padded_grid(field):
    return jnp.pad(field, ((0, 0), (1, 1), (1, 1), (1, 1)))

def reference(features, occupancy, weight_first, weight_second, cotangent):
    grid = features.reshape(CH, NX, NY, ZH)
    cells = jnp.repeat(jnp.repeat(jnp.repeat(occupancy, EDGE, 0), EDGE, 1), EDGE, 2)
    voxel_mask = cells.astype(jnp.float32)[None]
    masked = (grid * voxel_mask).astype(jnp.bfloat16)
    first = voxel_mask * conv_window(padded_grid(masked), weight_first, False)
    hidden = jax.nn.silu(first).astype(jnp.bfloat16)
    second = voxel_mask * conv_window(padded_grid(hidden), weight_second, False)
    activated = jax.nn.silu(second).astype(jnp.bfloat16)
    upstream = cotangent.reshape(CH, NX, NY, ZH).astype(jnp.float32)
    grad_two = (upstream * silu_slope(second) * voxel_mask).astype(jnp.bfloat16)
    factor = 1.0 / math.sqrt(NX * NY * ZH)
    grad_second = (grad_window(padded_grid(hidden), grad_two) * factor).reshape(-1)
    back_hidden = conv_window(padded_grid(grad_two), weight_second, True)
    grad_one = (back_hidden * silu_slope(first) * voxel_mask).astype(jnp.bfloat16)
    grad_first = (grad_window(padded_grid(masked), grad_one) * factor).reshape(-1)
    feature_grad = (voxel_mask * conv_window(padded_grid(grad_one), weight_first, True)).astype(jnp.bfloat16)
    return (activated.reshape(CH, NX, NY * ZH), feature_grad.reshape(CH, NX, NY * ZH), grad_first, grad_second)
```

```python
import math

import jax
import jax.numpy as jnp
from jax import lax
from jax.experimental import pallas as pl
from jax.experimental.pallas import tpu as pltpu
from jax.sharding import PartitionSpec as P

BOTH = ("east", "north")
F32 = jnp.float32
BF16 = jnp.bfloat16
CH = 96
LN = 128
TAPS = 9 * LN


def flip_pad(value):
    wide = jnp.concatenate(
        [value.astype(F32), jnp.zeros((LN - value.shape[0], value.shape[1]), F32)], axis=0
    )
    return wide.T


def weights_kernel(first, second, fwd_one, fwd_two, back_two, back_one):
    for out in (fwd_one, fwd_two, back_two, back_one):
        out[...] = jnp.zeros_like(out)

    def body(tap, carry):
        plane = tap // 9
        row = pl.multiple_of((tap % 9) * LN, LN)
        for source, ahead, back in ((first, fwd_one, back_one), (second, fwd_two, back_two)):
            ahead[plane + 1, pl.ds(row, CH), 0:CH] = source[tap]
            turned = jnp.pad(source[26 - tap].astype(F32), ((0, LN - CH), (0, LN - CH))).T
            back[plane + 1, pl.ds(row, LN), :] = turned.astype(BF16)
        return carry

    lax.fori_loop(0, 27, body, 0)


def spread(taps, plane_hi, plane_lo, value, rows):
    count = rows + 32
    level = lax.broadcasted_iota(jnp.int32, (count, LN), 0) & 15
    below = jnp.where(level == 0, 0.0, pltpu.roll(value, 1, 0))
    above = jnp.where(level == 15, 0.0, pltpu.roll(value, count - 1, 0))
    for c, moved in enumerate((below, value, above)):
        short = moved.astype(BF16)
        for b in range(3):
            lane = (3 * b + c) * LN
            taps[plane_hi, plane_lo, 0:rows, lane : lane + LN] = short[16 * b : 16 * b + rows]


def convolve(taps, weight, total, pairs, rows):
    size = pairs * rows
    for j in range(4):
        left = taps[j // 2 : j // 2 + pairs, j % 2, 0:rows, :].reshape(size, TAPS)
        right = jnp.concatenate([weight[j + 1], weight[j]], axis=1)
        part = jnp.dot(left, right, preferred_element_type=F32)
        if j == 0:
            total[0:size, :] = part
        else:
            total[0:size, :] += part


def kernel_grad(turned, planes, shift, scale, result):
    def piece(k):
        a, b = k // 3, k % 3
        start = (shift + 1 - b) * 16
        return planes[shift + 1 - a : shift + 9 - a, start : start + 128, :].reshape(1024, LN)

    for k in range(0, 9, 2):
        right = jnp.concatenate([piece(k), piece(min(k + 1, 8))], axis=1)
        part = jnp.dot(turned[...], right, preferred_element_type=F32) * scale
        result[k * 288 : k * 288 + 288, :] = part[:, 0:LN]
        if k < 8:
            result[(k + 1) * 288 : (k + 1) * 288 + 288, :] = part[:, LN : 2 * LN]


def turn_own(taps, first_plane, first_row, turned):
    for x in range(8):
        p = first_plane + x
        for c in range(3):
            lane = (3 + c) * LN
            block = taps[p // 2, p % 2, first_row : first_row + 128, lane : lane + LN]
            turned[c * CH : (c + 1) * CH, x * 128 : x * 128 + 128] = (
                block.astype(F32).T[0:CH].astype(BF16)
            )


def main_kernel(
    scale,
    place,
    feat,
    cot,
    west,
    east,
    south,
    north,
    own_mask,
    fwd_one,
    fwd_two,
    back_two,
    back_one,
    activated,
    feature_grad,
    keep,
    send,
    taps,
    grid,
    upstream,
    total,
    slope_one,
    planes,
    turned_one,
    turned_two,
    masks,
    grad_one_sum,
    grad_two_sum,
):
    has = [place[k].astype(F32) for k in range(4)]

    def mask_rows(ref, row):
        tile = ref[row : row + 16, :].astype(F32)
        return jnp.concatenate([tile] * 8, axis=0).T

    middle = [mask_rows(west, 576) * has[0], mask_rows(own_mask, 0), mask_rows(east, 576) * has[1]]
    for bx in range(3):
        side = 1.0 if bx == 1 else has[0] if bx == 0 else has[1]
        masks[bx, 0:64, :] = mask_rows(south, 1056 + 16 * bx)[0:64] * (has[2] * side)
        masks[bx, 64:192, :] = middle[bx]
        masks[bx, 192:256, :] = mask_rows(north, 1056 + 16 * bx)[0:64] * (has[3] * side)

    for p in range(16):
        if p < 4:
            block = west[p * CH : (p + 1) * CH, :]
        elif p < 12:
            block = feat[p - 4]
        else:
            block = east[(p - 12) * CH : (p - 11) * CH, :]
        grid[p, 64:192, :] = flip_pad(block)
    for k in range(8):
        for ref, row in ((south, 0), (north, 192)):
            both = flip_pad(ref[k * CH : (k + 1) * CH, :])
            grid[k, row : row + 64, :] = both[0:64]
            grid[k + 8, row : row + 64, :] = both[64:128]
    for p in range(12):
        if p < 2:
            block = west[384 + p * CH : 384 + (p + 1) * CH, :]
        elif p < 10:
            block = cot[p - 2]
        else:
            block = east[384 + (p - 10) * CH : 384 + (p - 9) * CH, :]
        upstream[p, 32:160, :] = flip_pad(block)
    for k in range(3):
        for ref, row in ((south, 0), (north, 160)):
            four = flip_pad(ref[768 + k * CH : 768 + (k + 1) * CH, :])
            for q in range(4):
                upstream[k + 3 * q, row : row + 32, :] = four[32 * q : 32 * q + 32]

    def band(p, low, high):
        return (p >= low).astype(jnp.int32) + (p >= high).astype(jnp.int32)

    def start(p, carry):
        spread(taps, p // 2, p % 2, grid[p] * masks[band(p, 4, 12)], 224)
        return carry

    lax.fori_loop(0, 16, start, 0)
    turn_own(taps, 4, 48, turned_one)
    convolve(taps, fwd_one, total, 7, 224)

    def after_one(i, carry):
        for half in range(2):
            p = 2 * i + half
            value = total[pl.ds(pl.multiple_of(i * 224, 16), 224), half * LN : half * LN + LN]
            value = value * masks[band(p, 3, 11), 16:240, :]
            sigma = jax.nn.sigmoid(value)
            slope_one[p] = (sigma * (1.0 + value * (1.0 - sigma)))[32:192]
            spread(taps, i, half, value * sigma, 192)
        return carry

    lax.fori_loop(0, 7, after_one, 0)
    turn_own(taps, 3, 32, turned_two)
    convolve(taps, fwd_two, total, 6, 192)

    def after_two(i, carry):
        for half in range(2):
            p = 2 * i + half
            value = total[pl.ds(pl.multiple_of(i * 192, 16), 192), half * LN : half * LN + LN]
            mask = masks[band(p, 2, 10), 32:224, :]
            value = value * mask
            sigma = jax.nn.sigmoid(value)

            @pl.when((p >= 2) & (p < 10))
            def _():
                activated[p - 2] = (value * sigma)[32:160].T[0:CH].astype(BF16)

            slope = sigma * (1.0 + value * (1.0 - sigma))
            grad = upstream[p] * slope * mask
            planes[p] = grad.astype(BF16)
            spread(taps, i, half, grad, 160)
        return carry

    lax.fori_loop(0, 6, after_two, 0)
    kernel_grad(turned_two, planes, 2, scale, grad_two_sum)
    convolve(taps, back_two, total, 5, 160)

    def after_three(i, carry):
        for half in range(2):
            p = 2 * i + half
            value = total[pl.ds(pl.multiple_of(i * 160, 16), 160), half * LN : half * LN + LN]
            grad = value * slope_one[p + 2] * masks[band(p, 1, 9), 48:208, :]
            planes[p, 0:160, :] = grad.astype(BF16)
            spread(taps, i, half, grad, 128)
        return carry

    lax.fori_loop(0, 5, after_three, 0)
    kernel_grad(turned_one, planes, 1, scale, grad_one_sum)
    convolve(taps, back_one, total, 4, 128)
    for p in range(8):
        i, half = p // 2, p % 2
        value = total[i * 128 : i * 128 + 128, half * LN : half * LN + LN] * masks[1, 64:192, :]
        feature_grad[p] = value.T[0:CH].astype(BF16)

    me = place[4]
    for out, low in ((keep, 0), (send, 1)):
        for e in range(4):
            j = jnp.bitwise_xor(me, 2 * e + low)

            def pack(g, carry):
                row = 81 * g + 10 * j
                one = grad_one_sum[pl.ds(row, 16), 0:CH]
                two = grad_two_sum[pl.ds(row, 16), 0:CH]
                out[e, g, 0:16, :] = one.astype(BF16)
                out[e, g, 16:32, :] = two.astype(BF16)
                return carry

            lax.fori_loop(0, 32, pack, 0)


def shift_by(step, axis):
    count = lax.axis_size(axis)
    return [(i, (i + step) % count) for i in range(count)]


def swap(value, bits):
    count = lax.axis_size("east") * lax.axis_size("north")
    return lax.ppermute(value, BOTH, [(i, i ^ bits) for i in range(count)])


def local(features, occupancy, weight_first, weight_second, cotangent):
    column = lax.axis_index("east")
    row = lax.axis_index("north")
    position = column * 16 + row
    voxel_total = 16 * 8 * 16 * 8 * 16
    scale = 1.0 / math.sqrt(voxel_total)

    feat = jnp.transpose(features, (1, 0, 2))
    cot = jnp.transpose(cotangent, (1, 0, 2))
    levels = jnp.repeat(occupancy.reshape(-1), 8).astype(BF16)
    own_mask = jnp.broadcast_to(jnp.tile(levels, 8)[None, :], (16, LN))

    def strip(f, c):
        return jnp.concatenate([f.reshape(-1, LN), c.reshape(-1, LN), own_mask], axis=0)

    west = lax.ppermute(strip(feat[4:8], cot[6:8]), "east", shift_by(1, "east"))
    east = lax.ppermute(strip(feat[0:4], cot[0:2]), "east", shift_by(-1, "east"))

    vmem = pl.BlockSpec(memory_space=pltpu.VMEM)
    packed = jax.ShapeDtypeStruct((5, TAPS, LN), BF16)
    weights = pl.pallas_call(
        weights_kernel,
        out_shape=[packed] * 4,
        in_specs=[vmem] * 2,
        out_specs=[vmem] * 4,
        compiler_params=pltpu.CompilerParams(vmem_limit_bytes=32 << 20),
        cost_estimate=pl.CostEstimate(flops=1 << 20, bytes_accessed=8 << 20, transcendentals=0),
        name="weights",
    )(weight_first, weight_second)

    all_feat = jnp.concatenate(
        [west[0:384].reshape(4, CH, LN), feat, east[0:384].reshape(4, CH, LN)], axis=0
    )
    all_cot = jnp.concatenate(
        [west[384:576].reshape(2, CH, LN), cot, east[384:576].reshape(2, CH, LN)], axis=0
    )
    all_mask = [west[576:592], own_mask, east[576:592]]

    def edge(at_feat, at_cot):
        f = all_feat[:, :, at_feat : at_feat + 64]
        f = jnp.concatenate([f[0:8], f[8:16]], axis=2)
        c = all_cot[:, :, at_cot : at_cot + 32]
        c = jnp.concatenate([c[0:3], c[3:6], c[6:9], c[9:12]], axis=2)
        return jnp.concatenate([f.reshape(-1, LN), c.reshape(-1, LN)] + all_mask, axis=0)

    south = lax.ppermute(edge(64, 96), "north", shift_by(1, "north"))
    north = lax.ppermute(edge(0, 0), "north", shift_by(-1, "north"))

    place = jnp.stack(
        [column > 0, column < 15, row > 0, row < 15, position % 8]
    ).astype(jnp.int32)
    image = jax.ShapeDtypeStruct((8, CH, LN), BF16)
    pieces = jax.ShapeDtypeStruct((4, 32, 32, CH), BF16)
    activated, feature_grad, keep, send = pl.pallas_call(
        lambda *refs: main_kernel(scale, *refs),
        out_shape=[image, image, pieces, pieces],
        in_specs=[pl.BlockSpec(memory_space=pltpu.SMEM)] + [vmem] * 11,
        out_specs=[vmem] * 4,
        scratch_shapes=[
            pltpu.VMEM((8, 2, 224, TAPS), BF16),
            pltpu.VMEM((16, 256, LN), F32),
            pltpu.VMEM((12, 192, LN), F32),
            pltpu.VMEM((7 * 224, 2 * LN), F32),
            pltpu.VMEM((14, 160, LN), F32),
            pltpu.VMEM((12, 192, LN), BF16),
            pltpu.VMEM((288, 1024), BF16),
            pltpu.VMEM((288, 1024), BF16),
            pltpu.VMEM((3, 256, LN), F32),
            pltpu.VMEM((2592 + 16, LN), F32),
            pltpu.VMEM((2592 + 16, LN), F32),
        ],
        compiler_params=pltpu.CompilerParams(vmem_limit_bytes=56 << 20),
        name="level",
    )(place, feat, cot, west, east, south, north, own_mask, *weights)

    def add(*terms):
        return sum(t.astype(F32) for t in terms).astype(BF16)

    part = add(keep, swap(send, 1))
    others = [swap(part[k], 2 * k) for k in (1, 2, 3)]
    part = add(part[0], *others)
    block = position // 8
    for bit in (1, 8, 16, 2, 4):
        count = part.shape[0]
        inner = {1: 1, 8: 4, 16: 4, 2: 1, 4: 1}[bit]
        half = part.reshape((count // (2 * inner), 2, inner) + part.shape[1:])
        mine = (block // bit) % 2
        held = lax.dynamic_index_in_dim(half, mine, 1, keepdims=False)
        given = lax.dynamic_index_in_dim(half, 1 - mine, 1, keepdims=False)
        part = add(held, swap(given, 8 * bit)).reshape((count // 2,) + part.shape[1:])
    flat = part[0].astype(F32)

    def own_share(rows):
        return lax.dynamic_slice_in_dim(rows[0:12].reshape(-1), 12 * (position % 8), 972)

    return (
        jnp.transpose(activated, (1, 0, 2)).reshape(CH, 8, LN),
        jnp.transpose(feature_grad, (1, 0, 2)).reshape(CH, 8, LN),
        own_share(flat[0:16]),
        own_share(flat[16:32]),
    )


def solution(mesh):
    return jax.shard_map(
        local,
        mesh=mesh,
        in_specs=(
            P(None, "east", "north"),
            P("east", "north", None),
            P(),
            P(),
            P(None, "east", "north"),
        ),
        out_specs=(
            P(None, "east", "north"),
            P(None, "east", "north"),
            P(BOTH),
            P(BOTH),
        ),
        check_vma=False,
    )
```

```python
import math

import jax
import jax.numpy as jnp
from jax import lax
from jax.experimental import pallas as pl
from jax.experimental.pallas import tpu as pltpu
from jax.sharding import PartitionSpec as P

BOTH = ("east", "north")
F32 = jnp.float32
BF16 = jnp.bfloat16
CH = 96
LN = 128
TAPS = 9 * LN
STRIP = 6 * CH + 16
VMEM = pl.BlockSpec(memory_space=pltpu.VMEM)
SMEM = pl.BlockSpec(memory_space=pltpu.SMEM)


def lanes(rows):
    return lax.broadcasted_iota(jnp.int32, (rows, LN), 1)


def flip_pad(value):
    wide = jnp.concatenate(
        [value.astype(F32), jnp.zeros((LN - value.shape[0], value.shape[1]), F32)], axis=0
    )
    return wide.T


def mask_column(ref, row):
    tile = ref[row : row + 16, :].astype(F32)
    return jnp.concatenate([tile] * 8, axis=0).T


def strips_kernel(
    occupied, features, cotangent, feat, cot, to_west, to_east, own_mask, wide_feat, wide_cot
):
    wide_feat[...] = features[...].astype(F32).reshape(CH * 8, LN)
    wide_cot[...] = cotangent[...].astype(F32).reshape(CH * 8, LN)
    for x in range(8):
        feat[x] = wide_feat[pl.ds(x, CH, stride=8), :].astype(BF16)
        cot[x] = wide_cot[pl.ds(x, CH, stride=8), :].astype(BF16)
    low = occupied[0, 0].astype(F32)
    high = occupied[0, 1].astype(F32)
    own_mask[...] = jnp.where((lanes(16) & 15) < 8, low, high).astype(BF16)
    for out, first, second in ((to_west, 0, 0), (to_east, 4, 6)):
        for k in range(4):
            out[k * CH : (k + 1) * CH, :] = feat[first + k]
        for k in range(2):
            out[(4 + k) * CH : (5 + k) * CH, :] = cot[second + k]
        out[6 * CH : STRIP, :] = own_mask[...]


def turn_levels(value, x, turned):
    lane = lanes(CH) & 15
    below = jnp.where(lane == 0, 0.0, pltpu.roll(value, 1, 1))
    above = jnp.where(lane == 15, 0.0, pltpu.roll(value, LN - 1, 1))
    start = x * LN if isinstance(x, int) else pl.multiple_of(x * LN, LN)
    for c, moved in enumerate((below, value, above)):
        turned[c * CH : (c + 1) * CH, pl.ds(start, LN)] = moved.astype(BF16)


def prepare_kernel(
    first,
    second,
    feat,
    cot,
    own_mask,
    fwd_one,
    fwd_two,
    back_two,
    back_one,
    turned_one,
    own_grid,
    own_cot,
):
    for out in (fwd_one, fwd_two, back_two, back_one):
        out[...] = jnp.zeros_like(out)

    def body(tap, carry):
        plane = tap // 9
        row = pl.multiple_of((tap % 9) * LN, LN)
        for source, ahead, back in ((first, fwd_one, back_one), (second, fwd_two, back_two)):
            ahead[plane + 1, pl.ds(row, CH), 0:CH] = source[tap]
            turned = jnp.pad(source[26 - tap].astype(F32), ((0, LN - CH), (0, LN - CH))).T
            back[plane + 1, pl.ds(row, LN), :] = turned.astype(BF16)
        return carry

    lax.fori_loop(0, 27, body, 0)
    mask = jnp.concatenate([own_mask[...].astype(F32)] * 6, axis=0)
    for x in range(8):
        value = feat[x].astype(F32) * mask
        turn_levels(value, x, turned_one)
        own_grid[x] = flip_pad(value).astype(BF16)
        own_cot[x] = flip_pad(cot[x]).astype(BF16)


def sides_kernel(place, own_mask, west, east, side_grid, side_cot, middle):
    middle[0] = mask_column(west, 6 * CH) * place[0].astype(F32)
    middle[1] = mask_column(own_mask, 0)
    middle[2] = mask_column(east, 6 * CH) * place[1].astype(F32)
    for side, ref in ((0, west), (1, east)):
        for k in range(4):
            block = flip_pad(ref[k * CH : (k + 1) * CH, :]) * middle[2 * side]
            side_grid[4 * side + k] = block.astype(BF16)
        for k in range(2):
            side_cot[2 * side + k] = flip_pad(ref[(4 + k) * CH : (5 + k) * CH, :]).astype(BF16)


def spread(taps, plane_hi, plane_lo, value, rows):
    count = rows + 32
    level = lax.broadcasted_iota(jnp.int32, (count, LN), 0) & 15
    below = jnp.where(level == 0, 0.0, pltpu.roll(value, 1, 0))
    above = jnp.where(level == 15, 0.0, pltpu.roll(value, count - 1, 0))
    for c, moved in enumerate((below, value, above)):
        short = moved.astype(BF16)
        for b in range(3):
            lane = (3 * b + c) * LN
            taps[plane_hi, plane_lo, 0:rows, lane : lane + LN] = short[16 * b : 16 * b + rows]


def convolve(taps, weight, total, pairs, rows):
    size = pairs * rows
    left = jnp.concatenate(
        [
            taps[j // 2 : j // 2 + pairs, j % 2, 0:rows, :].reshape(size, TAPS)
            for j in range(4)
        ],
        axis=1,
    )
    right = jnp.concatenate(
        [jnp.concatenate([weight[j + 1], weight[j]], axis=1) for j in range(4)], axis=0
    )
    total[0:size, :] = jnp.dot(left, right, preferred_element_type=F32)


def kernel_grad(turned, planes, shift, scale, result):
    def piece(k):
        a, b = k // 3, k % 3
        start = (shift + 1 - b) * 16
        return planes[shift + 1 - a : shift + 9 - a, start : start + 128, :].reshape(1024, LN)

    for k in range(0, 9, 2):
        right = jnp.concatenate([piece(k), piece(min(k + 1, 8))], axis=1)
        part = jnp.dot(turned[...], right, preferred_element_type=F32) * scale
        result[k * 288 : k * 288 + 288, :] = part[:, 0:LN]
        if k < 8:
            result[(k + 1) * 288 : (k + 1) * 288 + 288, :] = part[:, LN : 2 * LN]


def band(p, low, high):
    return (p >= low).astype(jnp.int32) + (p >= high).astype(jnp.int32)


def level_kernel(
    scale,
    place,
    own_grid,
    side_grid,
    own_cot,
    side_cot,
    middle,
    south,
    north,
    fwd_one,
    fwd_two,
    back_two,
    turned_one,
    activated,
    grad_one,
    masks,
    keep,
    send,
    taps,
    edge,
    upstream,
    total,
    slope_one,
    grad_two,
    turned_two,
    grad_one_sum,
    grad_two_sum,
    packed,
):
    for ref, flag, row in ((south, place[2], 0), (north, place[3], 192)):
        tile = ref[11 * CH : 11 * CH + 48, :].astype(F32) * flag.astype(F32)
        turned = jnp.concatenate([tile, jnp.zeros((80, LN), F32)], axis=0).T[0:64]
        for bx in range(3):
            side = place[bx // 2].astype(F32) if bx != 1 else 1.0
            column = turned[:, 16 * bx : 16 * bx + 1] * side
            masks[bx, row : row + 64, :] = jnp.broadcast_to(column, (64, LN))
    masks[:, 64:192, :] = middle[...]

    for k in range(8):
        for ref, row in ((south, 0), (north, 64)):
            both = flip_pad(ref[k * CH : (k + 1) * CH, :])
            edge[k, row : row + 64, :] = both[0:64]
            edge[k + 8, row : row + 64, :] = both[64:128]
    for k in range(3):
        for ref, row in ((south, 0), (north, 160)):
            four = flip_pad(ref[(8 + k) * CH : (9 + k) * CH, :])
            for q in range(4):
                upstream[k + 3 * q, row : row + 32, :] = four[32 * q : 32 * q + 32]
    for k in range(2):
        upstream[k, 32:160, :] = side_cot[k].astype(F32)
        upstream[10 + k, 32:160, :] = side_cot[2 + k].astype(F32)
    for k in range(8):
        upstream[2 + k, 32:160, :] = own_cot[k].astype(F32)

    def begin(p, value, bx):
        low = edge[p, 0:64, :] * masks[bx, 0:64, :]
        high = edge[p, 64:128, :] * masks[bx, 192:256, :]
        whole = jnp.concatenate([low, value.astype(F32), high], axis=0)
        spread(taps, p // 2, p % 2, whole, 224)

    def begin_west(p, carry):
        begin(p, side_grid[p], 0)
        return carry

    def begin_own(p, carry):
        begin(p + 4, own_grid[p], 1)
        return carry

    def begin_east(p, carry):
        begin(p + 12, side_grid[p + 4], 2)
        return carry

    lax.fori_loop(0, 4, begin_west, 0)
    lax.fori_loop(0, 8, begin_own, 0)
    lax.fori_loop(0, 4, begin_east, 0)
    convolve(taps, fwd_one, total, 7, 224)

    def after_one(i, carry):
        for half in range(2):
            p = 2 * i + half
            value = total[pl.ds(pl.multiple_of(i * 224, 16), 224), half * LN : half * LN + LN]
            value = value * masks[band(p, 3, 11), 16:240, :]
            sigma = jax.nn.sigmoid(value)
            slope_one[p] = (sigma * (1.0 + value * (1.0 - sigma)))[32:192]
            hidden = (value * sigma).astype(BF16).astype(F32)
            spread(taps, i, half, hidden, 192)

            @pl.when((p >= 3) & (p < 11))
            def _():
                turn_levels(hidden[48:176].T[0:CH], p - 3, turned_two)

        return carry

    lax.fori_loop(0, 7, after_one, 0)
    convolve(taps, fwd_two, total, 6, 192)

    def after_two(i, carry):
        for half in range(2):
            p = 2 * i + half
            value = total[pl.ds(pl.multiple_of(i * 192, 16), 192), half * LN : half * LN + LN]
            mask = masks[band(p, 2, 10), 32:224, :]
            value = value * mask
            sigma = jax.nn.sigmoid(value)

            @pl.when((p >= 2) & (p < 10))
            def _():
                activated[p - 2] = (value * sigma)[32:160].T[0:CH].astype(BF16)

            slope = sigma * (1.0 + value * (1.0 - sigma))
            grad = upstream[p] * slope * mask
            grad_two[p] = grad.astype(BF16)
            spread(taps, i, half, grad, 160)
        return carry

    lax.fori_loop(0, 6, after_two, 0)
    kernel_grad(turned_two, grad_two, 2, scale, grad_two_sum)
    convolve(taps, back_two, total, 5, 160)

    def after_three(i, carry):
        for half in range(2):
            p = 2 * i + half
            value = total[pl.ds(pl.multiple_of(i * 160, 16), 160), half * LN : half * LN + LN]
            grad = value * slope_one[p + 2] * masks[band(p, 1, 9), 48:208, :]
            grad_one[p] = grad.astype(BF16)
        return carry

    lax.fori_loop(0, 5, after_three, 0)
    kernel_grad(turned_one, grad_one, 1, scale, grad_one_sum)

    me = place[4]
    tail = lanes(CH) < CH
    for out, low in ((keep, 0), (send, 1)):
        for e in range(4):
            j = jnp.bitwise_xor(me, 2 * e + low)
            for grad, source in ((0, grad_one_sum), (1, grad_two_sum)):

                def gather(g, carry):
                    packed[pl.ds(12 * g, 16), :] = source[pl.ds(81 * g + 10 * j, 16), :]
                    return carry

                lax.fori_loop(0, 32, gather, 0, unroll=8)
                last = packed[288:384, :]
                for k in range(3):
                    block = jnp.where(
                        tail, packed[CH * k : CH * k + CH, :], pltpu.roll(last, CH - 32 * k, 1)
                    )
                    start = 288 * grad + CH * k
                    out[e, start : start + CH, :] = block.astype(BF16)


def final_kernel(grad_one, masks, back_one, feature_grad, taps, total):
    def begin(i, carry):
        for half in range(2):
            spread(taps, i, half, grad_one[2 * i + half].astype(F32), 128)
        return carry

    lax.fori_loop(0, 5, begin, 0)
    convolve(taps, back_one, total, 4, 128)
    for p in range(8):
        i, half = p // 2, p % 2
        value = total[i * 128 : i * 128 + 128, half * LN : half * LN + LN] * masks[1, 64:192, :]
        feature_grad[p] = value.T[0:CH].astype(BF16)


def combine_kernel(place, a0, a1, a2, a3, hold, give, rows, ordered):
    bit = place[5]
    lane = lanes(CH)
    for grad in range(2):
        blocks = []
        for k in range(3):
            start = 288 * grad + CH * k
            blocks.append(
                sum(ref[start : start + CH, :].astype(F32) for ref in (a0, a1, a2, a3))
            )
        a, b, c = blocks
        last = jnp.where(
            lane < 32,
            pltpu.roll(a, 32, 1),
            jnp.where(lane < 64, pltpu.roll(b, 64, 1), pltpu.roll(c, 96, 1)),
        )
        for k, block in enumerate((a, b, c, last)):
            rows[grad, CH * k : CH * k + CH, :] = block
    for out, want in ((hold, bit), (give, 1 - bit)):
        for m in range(16):
            for grad in range(2):
                start = 24 * m + 12 * grad
                ordered[start : start + 12, :] = rows[grad, pl.ds(24 * m + 12 * want, 12), :]
        out[...] = ordered[...].astype(BF16)


def finish_kernel(place, held, got, out_one, out_two):
    j = place[4]
    lane = lanes(1)
    value = held[...] + got[...]
    for grad, out in ((0, out_one), (1, out_two)):
        flat = []
        for m in range(3):
            r = [value[12 * grad + 4 * m + q : 12 * grad + 4 * m + q + 1] for q in range(4)]
            flat.append(jnp.where(lane < 96, r[0], pltpu.roll(r[1], 96, 1)))
            flat.append(jnp.where(lane < 64, pltpu.roll(r[1], 96, 1), pltpu.roll(r[2], 64, 1)))
            flat.append(jnp.where(lane < 32, pltpu.roll(r[2], 64, 1), pltpu.roll(r[3], 32, 1)))
        low = jnp.concatenate(flat[0:8], axis=0)
        high = jnp.concatenate(flat[1:9], axis=0)
        turn = lax.rem(LN - 12 * j, LN)
        out[...] = jnp.where(
            lanes(8) < LN - 12 * j, pltpu.roll(low, turn, 1), pltpu.roll(high, turn, 1)
        )


def call(kernel, name, outs, scratch, limit, flops, specs, *args):
    return pl.pallas_call(
        kernel,
        out_shape=outs,
        in_specs=specs,
        out_specs=[VMEM] * len(outs),
        scratch_shapes=scratch,
        compiler_params=pltpu.CompilerParams(vmem_limit_bytes=limit << 20),
        cost_estimate=pl.CostEstimate(flops=flops, bytes_accessed=1 << 20, transcendentals=0),
        name=name,
    )(*args)


def shape(*dims, dtype=BF16):
    return jax.ShapeDtypeStruct(dims, dtype)


def shift_by(step, axis):
    count = lax.axis_size(axis)
    return [(i, (i + step) % count) for i in range(count)]


def swap(value, bits):
    count = lax.axis_size("east") * lax.axis_size("north")
    return lax.ppermute(value, BOTH, [(i, i ^ bits) for i in range(count)])


def local(features, occupancy, weight_first, weight_second, cotangent):
    column = lax.axis_index("east")
    row = lax.axis_index("north")
    position = column * 16 + row
    block = position // 8
    scale = 1.0 / math.sqrt(128 * 128 * 16)
    place = jnp.stack(
        [column > 0, column < 15, row > 0, row < 15, position % 8, block % 2]
    ).astype(jnp.int32)

    feat, cot, to_west, to_east, own_mask = call(
        strips_kernel,
        "strips",
        [shape(8, CH, LN), shape(8, CH, LN), shape(STRIP, LN), shape(STRIP, LN), shape(16, LN)],
        [pltpu.VMEM((CH * 8, LN), F32), pltpu.VMEM((CH * 8, LN), F32)],
        8,
        1 << 20,
        [SMEM, VMEM, VMEM],
        occupancy.reshape(1, 2),
        features,
        cotangent,
    )
    west = lax.ppermute(to_east, "east", shift_by(1, "east"))
    east = lax.ppermute(to_west, "east", shift_by(-1, "east"))

    weight = shape(5, TAPS, LN)
    tile = shape(8, LN, LN)
    prepared = call(
        prepare_kernel,
        "prepare",
        [weight, weight, weight, weight, shape(288, 1024), tile, tile],
        [],
        16,
        1 << 33,
        [VMEM] * 5,
        weight_first,
        weight_second,
        feat,
        cot,
        own_mask,
    )
    (west, east), prepared = lax.optimization_barrier(((west, east), prepared))
    fwd_one, fwd_two, back_two, back_one, turned_one, own_grid, own_cot = prepared

    all_feat = jnp.concatenate(
        [west[0:384].reshape(4, CH, LN), feat, east[0:384].reshape(4, CH, LN)], axis=0
    )
    all_cot = jnp.concatenate(
        [west[384:576].reshape(2, CH, LN), cot, east[384:576].reshape(2, CH, LN)], axis=0
    )
    all_mask = [west[576:592], own_mask, east[576:592]]

    def rim(at_feat, at_cot):
        f = all_feat[:, :, at_feat : at_feat + 64]
        f = jnp.concatenate([f[0:8], f[8:16]], axis=2)
        c = all_cot[:, :, at_cot : at_cot + 32]
        c = jnp.concatenate([c[0:3], c[3:6], c[6:9], c[9:12]], axis=2)
        return jnp.concatenate([f.reshape(-1, LN), c.reshape(-1, LN)] + all_mask, axis=0)

    south = lax.ppermute(rim(64, 96), "north", shift_by(1, "north"))
    north = lax.ppermute(rim(0, 0), "north", shift_by(-1, "north"))
    sides = call(
        sides_kernel,
        "sides",
        [tile, shape(4, LN, LN), shape(3, LN, LN, dtype=F32)],
        [],
        8,
        1 << 31,
        [SMEM] + [VMEM] * 3,
        place,
        own_mask,
        west,
        east,
    )
    (south, north), sides = lax.optimization_barrier(((south, north), sides))
    side_grid, side_cot, middle = sides

    activated, grad_one, masks, keep, send = call(
        lambda *refs: level_kernel(scale, *refs),
        "level",
        [
            shape(8, CH, LN),
            shape(10, 160, LN),
            shape(3, 256, LN, dtype=F32),
            shape(4, 576, LN),
            shape(4, 576, LN),
        ],
        [
            pltpu.VMEM((8, 2, 224, TAPS), BF16),
            pltpu.VMEM((16, 128, LN), F32),
            pltpu.VMEM((12, 192, LN), F32),
            pltpu.VMEM((7 * 224, 2 * LN), F32),
            pltpu.VMEM((14, 160, LN), F32),
            pltpu.VMEM((12, 192, LN), BF16),
            pltpu.VMEM((288, 1024), BF16),
            pltpu.VMEM((2592 + 16, LN), F32),
            pltpu.VMEM((2592 + 16, LN), F32),
            pltpu.VMEM((400, LN), F32),
        ],
        36,
        1 << 34,
        [SMEM] + [VMEM] * 11,
        place,
        own_grid,
        side_grid,
        own_cot,
        side_cot,
        middle,
        south,
        north,
        fwd_one,
        fwd_two,
        back_two,
        turned_one,
    )

    def add(*terms):
        return sum(t.astype(F32) for t in terms)

    part = add(keep, swap(send, 1)).astype(BF16)
    others = [swap(part[k], 2 * k) for k in (1, 2, 3)]
    (feature_grad,) = call(
        final_kernel,
        "final",
        [shape(8, CH, LN)],
        [pltpu.VMEM((5, 2, 128, TAPS), BF16), pltpu.VMEM((512, 2 * LN), F32)],
        16,
        1 << 32,
        [VMEM] * 3,
        grad_one,
        masks,
        back_one,
    )
    others, feature_grad = lax.optimization_barrier((others, feature_grad))
    hold, give = call(
        combine_kernel,
        "combine",
        [shape(384, LN), shape(384, LN)],
        [pltpu.VMEM((2, 384, LN), F32), pltpu.VMEM((384, LN), F32)],
        8,
        1 << 20,
        [SMEM] + [VMEM] * 4,
        place,
        part[0],
        *others,
    )
    part = add(hold, swap(give, 8)).reshape(16, 24, LN)
    for bit, kind in ((8, BF16), (4, F32), (2, F32)):
        half = part.reshape((2, -1, 24, LN)).astype(kind)
        mine = (block // (2 * bit)) % 2
        held = lax.dynamic_index_in_dim(half, mine, 0, keepdims=False)
        given = lax.dynamic_index_in_dim(half, 1 - mine, 0, keepdims=False)
        part = add(held, swap(given, 16 * bit))
    mine = (block // 2) % 2
    held = lax.dynamic_index_in_dim(part, mine, 0, keepdims=False)
    given = lax.dynamic_index_in_dim(part, 1 - mine, 0, keepdims=False)
    one, two = call(
        finish_kernel,
        "finish",
        [shape(8, LN, dtype=F32), shape(8, LN, dtype=F32)],
        [],
        8,
        1 << 20,
        [SMEM] + [VMEM] * 2,
        place,
        held,
        swap(given, 16),
    )

    return (
        jnp.transpose(activated, (1, 0, 2)),
        jnp.transpose(feature_grad, (1, 0, 2)),
        one.reshape(-1)[0:972],
        two.reshape(-1)[0:972],
    )


def solution(mesh):
    return jax.shard_map(
        local,
        mesh=mesh,
        in_specs=(
            P(None, "east", "north"),
            P("east", "north", None),
            P(),
            P(),
            P(None, "east", "north"),
        ),
        out_specs=(
            P(None, "east", "north"),
            P(None, "east", "north"),
            P(BOTH),
            P(BOTH),
        ),
        check_vma=False,
    )
```

```python
import math

import jax
import jax.numpy as jnp
from jax import lax
from jax.experimental import pallas as pl
from jax.experimental.pallas import tpu as pltpu
from jax.sharding import PartitionSpec as P

BOTH = ("east", "north")
F32 = jnp.float32
BF16 = jnp.bfloat16
CH = 96
LN = 128
TAPS = 7 * LN
WHOLE = (0, 2, 3, 5, 6, 7, 8)
SPLIT = (1, 1, 1, 4, 4, 4)
STRIP = 6 * CH + 16
RIM = 11 * CH + 48
VMEM = pl.BlockSpec(memory_space=pltpu.VMEM)
SMEM = pl.BlockSpec(memory_space=pltpu.SMEM)


def lanes(rows):
    return lax.broadcasted_iota(jnp.int32, (rows, LN), 1)


def flip_pad(value):
    wide = jnp.concatenate(
        [value.astype(F32), jnp.zeros((LN - value.shape[0], value.shape[1]), F32)], axis=0
    )
    return wide.T


def mask_column(ref, row):
    tile = ref[row : row + 16, :].astype(F32)
    return jnp.concatenate([tile] * 8, axis=0).T


def strips_kernel(
    occupied,
    features,
    cotangent,
    feat,
    cot,
    to_west,
    to_east,
    own_mask,
    near_feat,
    near_cot,
    near_occupied,
    wide_feat,
    wide_cot,
    sems,
):
    copies = [
        pltpu.make_async_copy(features, near_feat, sems.at[0]),
        pltpu.make_async_copy(cotangent, near_cot, sems.at[1]),
        pltpu.make_async_copy(occupied, near_occupied, sems.at[2]),
    ]
    for copy in copies:
        copy.start()
    for copy, near, wide, out in (
        (copies[0], near_feat, wide_feat, feat),
        (copies[1], near_cot, wide_cot, cot),
    ):
        copy.wait()
        wide[...] = near[...].astype(F32).reshape(CH * 8, LN)
        for x in range(8):
            out[x] = wide[pl.ds(x, CH, stride=8), :].astype(BF16)
    copies[2].wait()
    levels = near_occupied[...].astype(F32)
    own_mask[...] = jnp.where((lanes(16) & 15) < 8, levels[:, 0:1], levels[:, 1:2]).astype(BF16)
    for out, first, second in ((to_west, 0, 0), (to_east, 4, 6)):
        for k in range(4):
            out[k * CH : (k + 1) * CH, :] = feat[first + k]
        for k in range(2):
            out[(4 + k) * CH : (5 + k) * CH, :] = cot[second + k]
        out[6 * CH : STRIP, :] = own_mask[...]


def turn_levels(value, x, turned):
    lane = lanes(CH) & 15
    below = jnp.where(lane == 0, 0.0, pltpu.roll(value, 1, 1))
    above = jnp.where(lane == 15, 0.0, pltpu.roll(value, LN - 1, 1))
    start = x * LN if isinstance(x, int) else pl.multiple_of(x * LN, LN)
    for c, moved in enumerate((below, value, above)):
        turned[c * CH : (c + 1) * CH, pl.ds(start, LN)] = moved.astype(BF16)


def prepare_kernel(
    first,
    second,
    feat,
    cot,
    own_mask,
    fwd_one,
    fwd_two,
    back_two,
    back_one,
    turned_one,
    own_grid,
    own_cot,
    token,
):
    token[...] = jnp.zeros_like(token)
    for out in (fwd_one, fwd_two, back_two, back_one):
        out[...] = jnp.zeros_like(out)

    def body(plane, carry):
        for source, ahead, back in ((first, fwd_one, back_one), (second, fwd_two, back_two)):
            for k in range(9):
                straight = source[9 * plane + k]
                turned = jnp.pad(
                    source[26 - 9 * plane - k].astype(F32), ((0, LN - CH), (0, LN - CH))
                ).T.astype(BF16)
                if k in WHOLE:
                    row = WHOLE.index(k) * LN
                    ahead[plane + 1, row : row + CH, 0:CH] = straight
                    back[plane + 1, row : row + CH, :] = turned[0:CH]
                else:
                    for q in range(3):
                        row = (SPLIT.index(k) + q) * LN + CH
                        ahead[plane + 1, row : row + 32, 0:CH] = straight[32 * q : 32 * q + 32]
                        back[plane + 1, row : row + 32, :] = turned[32 * q : 32 * q + 32]
        return carry

    lax.fori_loop(0, 3, body, 0)
    mask = jnp.concatenate([own_mask[...].astype(F32)] * 6, axis=0)
    for x in range(8):
        value = feat[x].astype(F32) * mask
        turn_levels(value, x, turned_one)
        own_grid[x] = flip_pad(value).astype(BF16)
        own_cot[x] = flip_pad(cot[x]).astype(BF16)


def rims_kernel(west, east, feat, cot, own_mask, to_south, to_north):
    half = lanes(CH) < 64
    quarter = lanes(CH) // 32

    def feat_plane(p):
        if p < 4:
            return west[p * CH : (p + 1) * CH, :].astype(F32)
        if p < 12:
            return feat[p - 4].astype(F32)
        return east[(p - 12) * CH : (p - 11) * CH, :].astype(F32)

    def cot_plane(p):
        if p < 2:
            return west[(4 + p) * CH : (5 + p) * CH, :].astype(F32)
        if p < 10:
            return cot[p - 2].astype(F32)
        return east[(p - 6) * CH : (p - 5) * CH, :].astype(F32)

    for k in range(8):
        one, two = feat_plane(k), feat_plane(k + 8)
        rows = slice(k * CH, (k + 1) * CH)
        to_south[rows, :] = jnp.where(half, one, pltpu.roll(two, 64, 1)).astype(BF16)
        to_north[rows, :] = jnp.where(half, pltpu.roll(one, 64, 1), two).astype(BF16)
    for k in range(3):
        four = [cot_plane(k + 3 * q) for q in range(4)]
        rows = slice((8 + k) * CH, (9 + k) * CH)
        for out, shift in ((to_south, 0), (to_north, 32)):
            moved = [
                pltpu.roll(four[q], (32 * q + shift) % LN, 1) if (32 * q + shift) % LN else four[q]
                for q in range(4)
            ]
            packed = jnp.where(
                quarter < 2,
                jnp.where(quarter == 0, moved[0], moved[1]),
                jnp.where(quarter == 2, moved[2], moved[3]),
            )
            out[rows, :] = packed.astype(BF16)
    for out in (to_south, to_north):
        out[11 * CH : 11 * CH + 16, :] = west[6 * CH : STRIP, :]
        out[11 * CH + 16 : 11 * CH + 32, :] = own_mask[...]
        out[11 * CH + 32 : RIM, :] = east[6 * CH : STRIP, :]


def sides_kernel(place, own_mask, west, east, side_grid, side_cot, middle, token):
    token[...] = jnp.zeros_like(token)
    middle[0] = mask_column(west, 6 * CH) * place[0].astype(F32)
    middle[1] = mask_column(own_mask, 0)
    middle[2] = mask_column(east, 6 * CH) * place[1].astype(F32)
    for side, ref in ((0, west), (1, east)):
        for k in range(4):
            block = flip_pad(ref[k * CH : (k + 1) * CH, :]) * middle[2 * side]
            side_grid[4 * side + k] = block.astype(BF16)
        for k in range(2):
            side_cot[2 * side + k] = flip_pad(ref[(4 + k) * CH : (5 + k) * CH, :]).astype(BF16)


def spread(taps, plane, value, rows):
    count = rows + 32
    level = lax.broadcasted_iota(jnp.int32, (count, LN), 0) & 15
    below = jnp.where(level == 0, 0.0, pltpu.roll(value, 1, 0))
    above = jnp.where(level == 15, 0.0, pltpu.roll(value, count - 1, 0))
    spare = lanes(count) >= CH
    short = [moved.astype(BF16) for moved in (below, value, above)]
    rest = [
        jnp.where(spare, pltpu.roll(value, CH - 32 * q, 1), 0.0).astype(BF16) for q in range(3)
    ]
    for n, k in enumerate(WHOLE):
        start = 16 * (k // 3)
        block = short[k % 3][start : start + rows]
        if n < 6:
            start = 16 * (SPLIT[n] // 3)
            block = block + rest[n % 3][start : start + rows]
        taps[plane // 2, plane % 2, 0:rows, n * LN : (n + 1) * LN] = block


def convolve(taps, weight, pair, rows):
    left = jnp.concatenate(
        [taps[pair + j // 2, j % 2, 0:rows, :] for j in range(4)], axis=1
    )
    right = jnp.concatenate(
        [jnp.concatenate([weight[j + 1], weight[j]], axis=1) for j in range(4)], axis=0
    )
    return jnp.dot(left, right, preferred_element_type=F32)


def pipeline(taps, weight, total, pairs, rows, after):
    for i in range(pairs + 1):
        if i < pairs:
            total[i * rows : (i + 1) * rows, :] = convolve(taps, weight, i, rows)
        if i > 0:
            for half in range(2):
                value = total[(i - 1) * rows : i * rows, half * LN : half * LN + LN]
                after(2 * (i - 1) + half, value)


def kernel_grad(turned, planes, shift, scale, result):
    def piece(k):
        a, b = k // 3, k % 3
        start = (shift + 1 - b) * 16
        return planes[shift + 1 - a : shift + 9 - a, start : start + 128, :].reshape(1024, LN)

    for k in range(0, 9, 2):
        right = jnp.concatenate([piece(k), piece(min(k + 1, 8))], axis=1)
        part = jnp.dot(turned[...], right, preferred_element_type=F32) * scale
        result[k * 288 : k * 288 + 288, :] = part[:, 0:LN]
        if k < 8:
            result[(k + 1) * 288 : (k + 1) * 288 + 288, :] = part[:, LN : 2 * LN]


def band(p, low, high):
    return int(p >= low) + int(p >= high)


def level_kernel(
    scale,
    place,
    own_grid,
    side_grid,
    own_cot,
    side_cot,
    middle,
    south,
    north,
    fwd_one,
    fwd_two,
    back_two,
    turned_one,
    activated,
    grad_one,
    masks,
    keep,
    send,
    taps,
    more_taps,
    edge,
    upstream,
    total,
    slope_one,
    grad_two,
    turned_two,
    grad_one_sum,
    grad_two_sum,
    packed,
):
    for ref, flag, row in ((south, place[2], 0), (north, place[3], 192)):
        tile = ref[11 * CH : 11 * CH + 48, :].astype(F32) * flag.astype(F32)
        turned = jnp.concatenate([tile, jnp.zeros((80, LN), F32)], axis=0).T[0:64]
        for bx in range(3):
            side = place[bx // 2].astype(F32) if bx != 1 else 1.0
            column = turned[:, 16 * bx : 16 * bx + 1] * side
            masks[bx, row : row + 64, :] = jnp.broadcast_to(column, (64, LN))
    masks[:, 64:192, :] = middle[...]

    for k in range(8):
        for ref, row in ((south, 0), (north, 64)):
            both = flip_pad(ref[k * CH : (k + 1) * CH, :])
            edge[k, row : row + 64, :] = both[0:64]
            edge[k + 8, row : row + 64, :] = both[64:128]
    for k in range(3):
        for ref, row in ((south, 0), (north, 160)):
            four = flip_pad(ref[(8 + k) * CH : (9 + k) * CH, :])
            for q in range(4):
                upstream[k + 3 * q, row : row + 32, :] = four[32 * q : 32 * q + 32]
    for k in range(2):
        upstream[k, 32:160, :] = side_cot[k].astype(F32)
        upstream[10 + k, 32:160, :] = side_cot[2 + k].astype(F32)
    for k in range(8):
        upstream[2 + k, 32:160, :] = own_cot[k].astype(F32)

    for p in range(16):
        bx = band(p, 4, 12)
        value = own_grid[p - 4] if bx == 1 else side_grid[p % 8]
        low = edge[p, 0:64, :] * masks[bx, 0:64, :]
        high = edge[p, 64:128, :] * masks[bx, 192:256, :]
        spread(taps, p, jnp.concatenate([low, value.astype(F32), high], axis=0), 224)

    def after_one(p, value):
        value = value * masks[band(p, 3, 11), 16:240, :]
        sigma = jax.nn.sigmoid(value)
        if 2 <= p < 12:
            slope_one[p - 2] = (sigma * (1.0 + value * (1.0 - sigma)))[32:192]
        hidden = (value * sigma).astype(BF16).astype(F32)
        spread(more_taps, p, hidden, 192)
        if 3 <= p < 11:
            turn_levels(hidden[48:176].T[0:CH], p - 3, turned_two)

    pipeline(taps, fwd_one, total, 7, 224, after_one)

    def after_two(p, value):
        mask = masks[band(p, 2, 10), 32:224, :]
        value = value * mask
        sigma = jax.nn.sigmoid(value)
        if 2 <= p < 10:
            activated[p - 2] = (value * sigma)[32:160].T[0:CH].astype(BF16)
        slope = sigma * (1.0 + value * (1.0 - sigma))
        grad = upstream[p] * slope * mask
        grad_two[p] = grad.astype(BF16)
        spread(taps, p, grad, 160)

    pipeline(more_taps, fwd_two, total, 6, 192, after_two)
    kernel_grad(turned_two, grad_two, 2, scale, grad_two_sum)

    def after_three(p, value):
        grad = value * slope_one[p] * masks[band(p, 1, 9), 48:208, :]
        grad_one[p] = grad.astype(BF16)

    pipeline(taps, back_two, total, 5, 160, after_three)
    kernel_grad(turned_one, grad_one, 1, scale, grad_one_sum)

    me = place[4]
    bit = place[5]
    tail = lanes(CH) < CH
    for out, low in ((keep, 0), (send, 1)):
        for e in range(4):
            near, far = e % 2, e // 2
            for grad, source in ((0, grad_one_sum), (1, grad_two_sum)):
                for turn in range(2):
                    j = jnp.bitwise_xor(me, 4 * (turn ^ far) + 2 * near + low)
                    first = 10 * j + 81 * jnp.bitwise_xor(bit, far)

                    def gather(m, carry):
                        packed[pl.ds(192 * turn + 12 * m, 16), :] = source[
                            pl.ds(first + 162 * m, 16), :
                        ]
                        return carry

                    lax.fori_loop(0, 16, gather, 0, unroll=8)
                last = packed[288:384, :]
                for k in range(3):
                    block = jnp.where(
                        tail, packed[CH * k : CH * k + CH, :], pltpu.roll(last, CH - 32 * k, 1)
                    )
                    start = 288 * grad + CH * k
                    out[e, start : start + CH, :] = block.astype(BF16)


def final_kernel(grad_one, masks, back_one, feature_grad, token, taps, total):
    token[...] = jnp.zeros_like(token)
    for p in range(10):
        spread(taps, p, grad_one[p].astype(F32), 128)

    def after_four(p, value):
        feature_grad[p] = (value * masks[1, 64:192, :]).T[0:CH].astype(BF16)

    pipeline(taps, back_one, total, 4, 128, after_four)


def combine_kernel(a0, a1, a2, a3, hold, give, ordered):
    lane = lanes(CH)
    for grad in range(2):
        blocks = []
        for k in range(3):
            start = 288 * grad + CH * k
            blocks.append(
                sum(ref[start : start + CH, :].astype(F32) for ref in (a0, a1, a2, a3))
            )
        a, b, c = blocks
        last = jnp.where(
            lane < 32,
            pltpu.roll(a, 32, 1),
            jnp.where(lane < 64, pltpu.roll(b, 64, 1), pltpu.roll(c, 96, 1)),
        )
        for k, block in enumerate((a, b, c, last)):
            for m in range(8):
                start = 192 * k + 24 * m + 12 * grad
                ordered[start : start + 12, :] = block[12 * m : 12 * m + 12]
    hold[...] = ordered[0:384, :].astype(BF16)
    give[...] = ordered[384:768, :].astype(BF16)


def finish_kernel(place, held, got, out_one, out_two):
    j = place[4]
    lane = lanes(1)
    value = held[...] + got[...]
    for grad, out in ((0, out_one), (1, out_two)):
        flat = []
        for m in range(3):
            r = [value[12 * grad + 4 * m + q : 12 * grad + 4 * m + q + 1] for q in range(4)]
            flat.append(jnp.where(lane < 96, r[0], pltpu.roll(r[1], 96, 1)))
            flat.append(jnp.where(lane < 64, pltpu.roll(r[1], 96, 1), pltpu.roll(r[2], 64, 1)))
            flat.append(jnp.where(lane < 32, pltpu.roll(r[2], 64, 1), pltpu.roll(r[3], 32, 1)))
        low = jnp.concatenate(flat[0:8], axis=0)
        high = jnp.concatenate(flat[1:9], axis=0)
        turn = lax.rem(LN - 12 * j, LN)
        out[...] = jnp.where(
            lanes(8) < LN - 12 * j, pltpu.roll(low, turn, 1), pltpu.roll(high, turn, 1)
        )


def call(kernel, name, outs, scratch, limit, flops, specs, *args):
    return pl.pallas_call(
        kernel,
        out_shape=outs,
        in_specs=specs,
        out_specs=[VMEM] * len(outs),
        scratch_shapes=scratch,
        compiler_params=pltpu.CompilerParams(vmem_limit_bytes=limit << 20),
        cost_estimate=pl.CostEstimate(flops=flops, bytes_accessed=1 << 20, transcendentals=0),
        name=name,
    )(*args)


def shape(*dims, dtype=BF16):
    return jax.ShapeDtypeStruct(dims, dtype)


def shift_by(step, axis):
    count = lax.axis_size(axis)
    return [(i, (i + step) % count) for i in range(count)]


def swap(value, bits):
    count = lax.axis_size("east") * lax.axis_size("north")
    return lax.ppermute(value, BOTH, [(i, i ^ bits) for i in range(count)])


def local(features, occupancy, weight_first, weight_second, cotangent):
    column = lax.axis_index("east")
    row = lax.axis_index("north")
    position = column * 16 + row
    block = position // 8
    scale = 1.0 / math.sqrt(128 * 128 * 16)
    place = jnp.stack(
        [column > 0, column < 15, row > 0, row < 15, position % 8, block % 2]
    ).astype(jnp.int32)

    feat, cot, to_west, to_east, own_mask = call(
        strips_kernel,
        "strips",
        [shape(8, CH, LN), shape(8, CH, LN), shape(STRIP, LN), shape(STRIP, LN), shape(16, LN)],
        [
            pltpu.VMEM((CH, 8, LN), BF16),
            pltpu.VMEM((CH, 8, LN), BF16),
            pltpu.VMEM((1, 2), jnp.int32),
            pltpu.VMEM((CH * 8, LN), F32),
            pltpu.VMEM((CH * 8, LN), F32),
            pltpu.SemaphoreType.DMA((3,)),
        ],
        60,
        1 << 20,
        [pl.BlockSpec(memory_space=pltpu.HBM)] * 3,
        occupancy.reshape(1, 2),
        features,
        cotangent,
    )
    west = lax.ppermute(to_east, "east", shift_by(1, "east"))
    east = lax.ppermute(to_west, "east", shift_by(-1, "east"))

    weight = shape(5, TAPS, LN)
    tile = shape(8, LN, LN)
    mark = shape(8, LN, dtype=F32)
    prepared = call(
        prepare_kernel,
        "prepare",
        [weight, weight, weight, weight, shape(288, 1024), tile, tile, mark],
        [],
        16,
        1 << 33,
        [VMEM] * 5,
        weight_first,
        weight_second,
        feat,
        cot,
        own_mask,
    )
    fwd_one, fwd_two, back_two, back_one, turned_one, own_grid, own_cot, token = prepared
    west, east, token = lax.optimization_barrier((west, east, token))
    to_south, to_north = call(
        rims_kernel,
        "rims",
        [shape(RIM, LN), shape(RIM, LN)],
        [],
        8,
        1 << 20,
        [VMEM] * 5,
        west,
        east,
        feat,
        cot,
        own_mask,
    )
    south = lax.ppermute(to_north, "north", shift_by(1, "north"))
    north = lax.ppermute(to_south, "north", shift_by(-1, "north"))
    side_grid, side_cot, middle, token = call(
        sides_kernel,
        "sides",
        [tile, shape(4, LN, LN), shape(3, LN, LN, dtype=F32), mark],
        [],
        8,
        1 << 31,
        [SMEM] + [VMEM] * 3,
        place,
        own_mask,
        west,
        east,
    )
    south, north, token = lax.optimization_barrier((south, north, token))

    activated, grad_one, masks, keep, send = call(
        lambda *refs: level_kernel(scale, *refs),
        "level",
        [
            shape(8, CH, LN),
            shape(10, 160, LN),
            shape(3, 256, LN, dtype=F32),
            shape(4, 576, LN),
            shape(4, 576, LN),
        ],
        [
            pltpu.VMEM((8, 2, 224, TAPS), BF16),
            pltpu.VMEM((7, 2, 192, TAPS), BF16),
            pltpu.VMEM((16, 128, LN), F32),
            pltpu.VMEM((12, 192, LN), F32),
            pltpu.VMEM((7 * 224, 2 * LN), F32),
            pltpu.VMEM((10, 160, LN), F32),
            pltpu.VMEM((12, 192, LN), BF16),
            pltpu.VMEM((288, 1024), BF16),
            pltpu.VMEM((2592 + 16, LN), F32),
            pltpu.VMEM((2592 + 16, LN), F32),
            pltpu.VMEM((400, LN), F32),
        ],
        36,
        1 << 34,
        [SMEM] + [VMEM] * 11,
        place,
        own_grid,
        side_grid,
        own_cot,
        side_cot,
        middle,
        south,
        north,
        fwd_one,
        fwd_two,
        back_two,
        turned_one,
    )

    def add(*terms):
        return sum(t.astype(F32) for t in terms)

    part = add(keep, swap(send, 1)).astype(BF16)
    others = [swap(part[k], bits) for k, bits in ((1, 2), (2, 12), (3, 14))]
    feature_grad, token = call(
        final_kernel,
        "final",
        [shape(8, CH, LN), mark],
        [pltpu.VMEM((5, 2, 128, TAPS), BF16), pltpu.VMEM((512, 2 * LN), F32)],
        16,
        1 << 32,
        [VMEM] * 3,
        grad_one,
        masks,
        back_one,
    )
    others, token = lax.optimization_barrier((others, token))
    hold, give = call(
        combine_kernel,
        "combine",
        [shape(384, LN), shape(384, LN)],
        [pltpu.VMEM((768, LN), F32)],
        8,
        1 << 20,
        [VMEM] * 4,
        part[0],
        *others,
    )
    part = add(hold, swap(give, 4)).reshape(16, 24, LN)
    for bit, kind, partner in ((8, BF16, 192), (4, F32, 64), (2, F32, 48)):
        half = part.reshape((2, -1, 24, LN)).astype(kind)
        mine = (block // (2 * bit)) % 2
        held = lax.dynamic_index_in_dim(half, mine, 0, keepdims=False)
        given = lax.dynamic_index_in_dim(half, 1 - mine, 0, keepdims=False)
        part = add(held, swap(given, partner))
    mine = (block // 2) % 2
    held = lax.dynamic_index_in_dim(part, mine, 0, keepdims=False)
    given = lax.dynamic_index_in_dim(part, 1 - mine, 0, keepdims=False)
    one, two = call(
        finish_kernel,
        "finish",
        [shape(8, LN, dtype=F32), shape(8, LN, dtype=F32)],
        [],
        8,
        1 << 20,
        [SMEM] + [VMEM] * 2,
        place,
        held,
        swap(given, 16),
    )

    return (
        jnp.transpose(activated, (1, 0, 2)),
        jnp.transpose(feature_grad, (1, 0, 2)),
        one.reshape(-1)[0:972],
        two.reshape(-1)[0:972],
    )


def solution(mesh):
    return jax.shard_map(
        local,
        mesh=mesh,
        in_specs=(
            P(None, "east", "north"),
            P("east", "north", None),
            P(),
            P(),
            P(None, "east", "north"),
        ),
        out_specs=(
            P(None, "east", "north"),
            P(None, "east", "north"),
            P(BOTH),
            P(BOTH),
        ),
        check_vma=False,
    )
```

```python
import math

import jax
import jax.numpy as jnp
from jax import lax
from jax.experimental import pallas as pl
from jax.experimental.pallas import tpu as pltpu
from jax.sharding import PartitionSpec as P

BOTH = ("east", "north")
F32 = jnp.float32
BF16 = jnp.bfloat16
CH = 96
LN = 128
TAPS = 7 * LN
WHOLE = (0, 2, 3, 5, 6, 7, 8)
SPLIT = (1, 1, 1, 4, 4, 4)
STRIP = 6 * CH + 16
RIM = 11 * CH + 48
VMEM = pl.BlockSpec(memory_space=pltpu.VMEM)
SMEM = pl.BlockSpec(memory_space=pltpu.SMEM)


def lanes(rows):
    return lax.broadcasted_iota(jnp.int32, (rows, LN), 1)


def flip_pad(value):
    wide = jnp.concatenate(
        [value.astype(F32), jnp.zeros((LN - value.shape[0], value.shape[1]), F32)], axis=0
    )
    return wide.T


def mask_column(ref, row):
    tile = ref[row : row + 16, :].astype(F32)
    return jnp.concatenate([tile] * 8, axis=0).T


def here():
    return lax.axis_index("east"), lax.axis_index("north")


def as_float(flag):
    return flag.astype(jnp.int32).astype(F32)


def neighbours():
    column, row = here()
    last_column, last_row = lax.axis_size("east") - 1, lax.axis_size("north") - 1
    flags = (column > 0, column < last_column, row > 0, row < last_row)
    return [as_float(flag) for flag in flags]


def mask_tile(occupied):
    levels = occupied[...].astype(F32)
    return jnp.where((lanes(16) & 15) < 8, levels[:, 0:1], levels[:, 1:2]).astype(BF16)


def strips_kernel(
    occupied,
    features,
    cotangent,
    to_west,
    to_east,
    near_feat,
    near_cot,
    near_occupied,
    wide_feat,
    wide_cot,
    sems,
):
    copies = [
        pltpu.make_async_copy(features, near_feat, sems.at[0]),
        pltpu.make_async_copy(cotangent, near_cot, sems.at[1]),
        pltpu.make_async_copy(occupied, near_occupied, sems.at[2]),
    ]
    for copy in copies:
        copy.start()
    for copy, near, wide, start, count in (
        (copies[0], near_feat, wide_feat, 0, 4),
        (copies[1], near_cot, wide_cot, 4, 2),
    ):
        copy.wait()
        wide[...] = near[...].astype(F32).reshape(CH * 8, LN)
        for k in range(count):
            rows = slice((start + k) * CH, (start + k + 1) * CH)
            to_west[rows, :] = wide[pl.ds(k, CH, stride=8), :].astype(BF16)
            to_east[rows, :] = wide[pl.ds(8 - count + k, CH, stride=8), :].astype(BF16)
    copies[2].wait()
    mask = mask_tile(near_occupied)
    to_west[6 * CH : STRIP, :] = mask
    to_east[6 * CH : STRIP, :] = mask


def turn_levels(value, x, turned):
    lane = lanes(CH) & 15
    below = jnp.where(lane == 0, 0.0, pltpu.roll(value, 1, 1))
    above = jnp.where(lane == 15, 0.0, pltpu.roll(value, LN - 1, 1))
    start = x * LN if isinstance(x, int) else pl.multiple_of(x * LN, LN)
    for c, moved in enumerate((below, value, above)):
        turned[c * CH : (c + 1) * CH, pl.ds(start, LN)] = moved.astype(BF16)


def prepare_kernel(
    first,
    second,
    features,
    cotangent,
    occupied,
    fwd_one,
    fwd_two,
    back_two,
    back_one,
    turned_one,
    own_grid,
    own_cot,
    feat,
    cot,
    own_mask,
    wide_feat,
    wide_cot,
):
    wide_feat[...] = features[...].astype(F32).reshape(CH * 8, LN)
    wide_cot[...] = cotangent[...].astype(F32).reshape(CH * 8, LN)
    own_mask[...] = mask_tile(occupied)
    for out in (fwd_one, fwd_two, back_two, back_one):
        out[...] = jnp.zeros_like(out)

    def body(plane, carry):
        for source, ahead, back in ((first, fwd_one, back_one), (second, fwd_two, back_two)):
            for k in range(9):
                straight = source[9 * plane + k]
                turned = jnp.pad(
                    source[26 - 9 * plane - k].astype(F32), ((0, LN - CH), (0, LN - CH))
                ).T.astype(BF16)
                if k in WHOLE:
                    row = WHOLE.index(k) * LN
                    ahead[plane + 1, row : row + CH, 0:CH] = straight
                    back[plane + 1, row : row + CH, :] = turned[0:CH]
                else:
                    for q in range(3):
                        row = (SPLIT.index(k) + q) * LN + CH
                        ahead[plane + 1, row : row + 32, 0:CH] = straight[32 * q : 32 * q + 32]
                        back[plane + 1, row : row + 32, :] = turned[32 * q : 32 * q + 32]
        return carry

    lax.fori_loop(0, 3, body, 0)
    mask = jnp.concatenate([own_mask[...].astype(F32)] * 6, axis=0)
    for x in range(8):
        plain = wide_feat[pl.ds(x, CH, stride=8), :]
        feat[x] = plain.astype(BF16)
        value = plain * mask
        turn_levels(value, x, turned_one)
        own_grid[x] = flip_pad(value).astype(BF16)
        plain = wide_cot[pl.ds(x, CH, stride=8), :]
        cot[x] = plain.astype(BF16)
        own_cot[x] = flip_pad(plain).astype(BF16)


def rims_kernel(west, east, feat, cot, own_mask, to_south, to_north):
    half = lanes(CH) < 64
    quarter = lanes(CH) // 32

    def feat_plane(p):
        if p < 4:
            return west[p * CH : (p + 1) * CH, :].astype(F32)
        if p < 12:
            return feat[p - 4].astype(F32)
        return east[(p - 12) * CH : (p - 11) * CH, :].astype(F32)

    def cot_plane(p):
        if p < 2:
            return west[(4 + p) * CH : (5 + p) * CH, :].astype(F32)
        if p < 10:
            return cot[p - 2].astype(F32)
        return east[(p - 6) * CH : (p - 5) * CH, :].astype(F32)

    for k in range(8):
        one, two = feat_plane(k), feat_plane(k + 8)
        rows = slice(k * CH, (k + 1) * CH)
        to_south[rows, :] = jnp.where(half, one, pltpu.roll(two, 64, 1)).astype(BF16)
        to_north[rows, :] = jnp.where(half, pltpu.roll(one, 64, 1), two).astype(BF16)
    for k in range(3):
        four = [cot_plane(k + 3 * q) for q in range(4)]
        rows = slice((8 + k) * CH, (9 + k) * CH)
        for out, shift in ((to_south, 0), (to_north, 32)):
            moved = [
                pltpu.roll(four[q], (32 * q + shift) % LN, 1) if (32 * q + shift) % LN else four[q]
                for q in range(4)
            ]
            packed = jnp.where(
                quarter < 2,
                jnp.where(quarter == 0, moved[0], moved[1]),
                jnp.where(quarter == 2, moved[2], moved[3]),
            )
            out[rows, :] = packed.astype(BF16)
    for out in (to_south, to_north):
        out[11 * CH : 11 * CH + 16, :] = west[6 * CH : STRIP, :]
        out[11 * CH + 16 : 11 * CH + 32, :] = own_mask[...]
        out[11 * CH + 32 : RIM, :] = east[6 * CH : STRIP, :]


def sides_kernel(own_mask, west, east, side_grid, side_cot, middle):
    has = neighbours()
    middle[0] = mask_column(west, 6 * CH) * has[0]
    middle[1] = mask_column(own_mask, 0)
    middle[2] = mask_column(east, 6 * CH) * has[1]
    for side, ref in ((0, west), (1, east)):
        for k in range(4):
            block = flip_pad(ref[k * CH : (k + 1) * CH, :]) * middle[2 * side]
            side_grid[4 * side + k] = block.astype(BF16)
        for k in range(2):
            side_cot[2 * side + k] = flip_pad(ref[(4 + k) * CH : (5 + k) * CH, :]).astype(BF16)


def spread(taps, plane, value, rows):
    count = rows + 32
    level = lax.broadcasted_iota(jnp.int32, (count, LN), 0) & 15
    below = jnp.where(level == 0, 0.0, pltpu.roll(value, 1, 0))
    above = jnp.where(level == 15, 0.0, pltpu.roll(value, count - 1, 0))
    spare = lanes(count) >= CH
    short = [moved.astype(BF16) for moved in (below, value, above)]
    rest = [
        jnp.where(spare, pltpu.roll(value, CH - 32 * q, 1), 0.0).astype(BF16) for q in range(3)
    ]
    for n, k in enumerate(WHOLE):
        start = 16 * (k // 3)
        block = short[k % 3][start : start + rows]
        if n < 6:
            start = 16 * (SPLIT[n] // 3)
            block = block + rest[n % 3][start : start + rows]
        taps[plane // 2, plane % 2, 0:rows, n * LN : (n + 1) * LN] = block


def convolve(taps, weight, pair, rows):
    left = jnp.concatenate(
        [taps[pair + j // 2, j % 2, 0:rows, :] for j in range(4)], axis=1
    )
    right = jnp.concatenate(
        [jnp.concatenate([weight[j + 1], weight[j]], axis=1) for j in range(4)], axis=0
    )
    return jnp.dot(left, right, preferred_element_type=F32)


def pipeline(taps, weight, total, pairs, rows, after):
    for i in range(pairs + 1):
        if i < pairs:
            total[i * rows : (i + 1) * rows, :] = convolve(taps, weight, i, rows)
        if i > 0:
            for half in range(2):
                value = total[(i - 1) * rows : i * rows, half * LN : half * LN + LN]
                after(2 * (i - 1) + half, value)


def kernel_grad(turned, planes, shift, scale, result):
    def piece(k):
        a, b = k // 3, k % 3
        start = (shift + 1 - b) * 16
        return planes[shift + 1 - a : shift + 9 - a, start : start + 128, :].reshape(1024, LN)

    for k in range(0, 9, 2):
        right = jnp.concatenate([piece(k), piece(min(k + 1, 8))], axis=1)
        part = jnp.dot(turned[...], right, preferred_element_type=F32) * scale
        result[k * 288 : k * 288 + 288, :] = part[:, 0:LN]
        if k < 8:
            result[(k + 1) * 288 : (k + 1) * 288 + 288, :] = part[:, LN : 2 * LN]


def band(p, low, high):
    return int(p >= low) + int(p >= high)


def level_kernel(
    scale,
    own_grid,
    side_grid,
    own_cot,
    side_cot,
    middle,
    south,
    north,
    fwd_one,
    fwd_two,
    back_two,
    turned_one,
    activated,
    grad_one,
    masks,
    keep,
    send,
    taps,
    more_taps,
    edge,
    upstream,
    total,
    slope_one,
    grad_two,
    turned_two,
    grad_one_sum,
    grad_two_sum,
    packed,
    rows,
):
    has = neighbours()
    for ref, flag, row in ((south, has[2], 0), (north, has[3], 192)):
        tile = ref[11 * CH : 11 * CH + 48, :].astype(F32) * flag
        turned = jnp.concatenate([tile, jnp.zeros((80, LN), F32)], axis=0).T[0:64]
        for bx in range(3):
            side = has[bx // 2] if bx != 1 else 1.0
            column = turned[:, 16 * bx : 16 * bx + 1] * side
            masks[bx, row : row + 64, :] = jnp.broadcast_to(column, (64, LN))
    masks[:, 64:192, :] = middle[...]

    for k in range(8):
        for ref, row in ((south, 0), (north, 64)):
            both = flip_pad(ref[k * CH : (k + 1) * CH, :])
            edge[k, row : row + 64, :] = both[0:64]
            edge[k + 8, row : row + 64, :] = both[64:128]
    for k in range(3):
        for ref, row in ((south, 0), (north, 160)):
            four = flip_pad(ref[(8 + k) * CH : (9 + k) * CH, :])
            for q in range(4):
                upstream[k + 3 * q, row : row + 32, :] = four[32 * q : 32 * q + 32]
    for k in range(2):
        upstream[k, 32:160, :] = side_cot[k].astype(F32)
        upstream[10 + k, 32:160, :] = side_cot[2 + k].astype(F32)
    for k in range(8):
        upstream[2 + k, 32:160, :] = own_cot[k].astype(F32)

    for p in range(16):
        bx = band(p, 4, 12)
        value = own_grid[p - 4] if bx == 1 else side_grid[p % 8]
        low = edge[p, 0:64, :] * masks[bx, 0:64, :]
        high = edge[p, 64:128, :] * masks[bx, 192:256, :]
        spread(taps, p, jnp.concatenate([low, value.astype(F32), high], axis=0), 224)

    def after_one(p, value):
        value = value * masks[band(p, 3, 11), 16:240, :]
        sigma = jax.nn.sigmoid(value)
        if 2 <= p < 12:
            slope_one[p - 2] = (sigma * (1.0 + value * (1.0 - sigma)))[32:192]
        hidden = (value * sigma).astype(BF16).astype(F32)
        spread(more_taps, p, hidden, 192)
        if 3 <= p < 11:
            turn_levels(hidden[48:176].T[0:CH], p - 3, turned_two)

    pipeline(taps, fwd_one, total, 7, 224, after_one)

    def after_two(p, value):
        mask = masks[band(p, 2, 10), 32:224, :]
        value = value * mask
        sigma = jax.nn.sigmoid(value)
        if 2 <= p < 10:
            rows[pl.ds(p - 2, CH, stride=8), :] = (value * sigma)[32:160].T[0:CH]
        slope = sigma * (1.0 + value * (1.0 - sigma))
        grad = upstream[p] * slope * mask
        grad_two[p] = grad.astype(BF16)
        spread(taps, p, grad, 160)

    pipeline(more_taps, fwd_two, total, 6, 192, after_two)
    activated[...] = rows[...].reshape(CH, 8, LN).astype(BF16)
    kernel_grad(turned_two, grad_two, 2, scale, grad_two_sum)

    def after_three(p, value):
        grad = value * slope_one[p] * masks[band(p, 1, 9), 48:208, :]
        grad_one[p] = grad.astype(BF16)

    pipeline(taps, back_two, total, 5, 160, after_three)
    kernel_grad(turned_one, grad_one, 1, scale, grad_one_sum)

    row = lax.axis_index("north")
    me = row & 7
    bit = row >> 3
    tail = lanes(CH) < CH
    for out, low in ((keep, 0), (send, 1)):
        for e in range(4):
            near, far = e % 2, e // 2
            for grad, source in ((0, grad_one_sum), (1, grad_two_sum)):
                for turn in range(2):
                    j = jnp.bitwise_xor(me, 4 * (turn ^ far) + 2 * near + low)
                    first = 10 * j + 81 * jnp.bitwise_xor(bit, far)

                    def gather(m, carry):
                        packed[pl.ds(192 * turn + 12 * m, 16), :] = source[
                            pl.ds(first + 162 * m, 16), :
                        ]
                        return carry

                    lax.fori_loop(0, 16, gather, 0, unroll=8)
                last = packed[288:384, :]
                for k in range(3):
                    block = jnp.where(
                        tail, packed[CH * k : CH * k + CH, :], pltpu.roll(last, CH - 32 * k, 1)
                    )
                    start = 288 * grad + CH * k
                    out[e, start : start + CH, :] = block.astype(BF16)


def final_kernel(grad_one, masks, back_one, feature_grad, token, taps, total, rows):
    token[...] = jnp.zeros_like(token)
    for p in range(10):
        spread(taps, p, grad_one[p].astype(F32), 128)

    def after_four(p, value):
        rows[pl.ds(p, CH, stride=8), :] = (value * masks[1, 64:192, :]).T[0:CH]

    pipeline(taps, back_one, total, 4, 128, after_four)
    feature_grad[...] = rows[...].reshape(CH, 8, LN).astype(BF16)


def combine_kernel(a0, a1, a2, a3, token, hold, give, ordered):
    lane = lanes(CH)
    for grad in range(2):
        blocks = []
        for k in range(3):
            start = 288 * grad + CH * k
            blocks.append(
                sum(ref[start : start + CH, :].astype(F32) for ref in (a0, a1, a2, a3))
            )
        a, b, c = blocks
        last = jnp.where(
            lane < 32,
            pltpu.roll(a, 32, 1),
            jnp.where(lane < 64, pltpu.roll(b, 64, 1), pltpu.roll(c, 96, 1)),
        )
        for k, block in enumerate((a, b, c, last)):
            for m in range(8):
                start = 192 * k + 24 * m + 12 * grad
                ordered[start : start + 12, :] = block[12 * m : 12 * m + 12]
    hold[...] = ordered[0:384, :].astype(BF16)
    give[...] = ordered[384:768, :].astype(BF16)


def step_kernel(shift, held, got, hold, give):
    bit = (lax.axis_index("east") >> shift) & 1
    for out, want in ((hold, bit), (give, 1 - bit)):
        out[...] = (held[want].astype(F32) + got[want].astype(F32)).astype(out.dtype)


def finish_kernel(held, got, out_one, out_two):
    j = lax.axis_index("north") & 7
    lane = lanes(1)
    value = held[...] + got[...]
    for grad, out in ((0, out_one), (1, out_two)):
        flat = []
        for m in range(3):
            r = [value[12 * grad + 4 * m + q : 12 * grad + 4 * m + q + 1] for q in range(4)]
            flat.append(jnp.where(lane < 96, r[0], pltpu.roll(r[1], 96, 1)))
            flat.append(jnp.where(lane < 64, pltpu.roll(r[1], 96, 1), pltpu.roll(r[2], 64, 1)))
            flat.append(jnp.where(lane < 32, pltpu.roll(r[2], 64, 1), pltpu.roll(r[3], 32, 1)))
        low = jnp.concatenate(flat[0:8], axis=0)
        high = jnp.concatenate(flat[1:9], axis=0)
        turn = lax.rem(LN - 12 * j, LN)
        out[...] = jnp.where(
            lanes(8) < LN - 12 * j, pltpu.roll(low, turn, 1), pltpu.roll(high, turn, 1)
        )


def call(kernel, name, outs, scratch, limit, flops, specs, *args):
    return pl.pallas_call(
        kernel,
        out_shape=outs,
        in_specs=specs,
        out_specs=[VMEM] * len(outs),
        scratch_shapes=scratch,
        compiler_params=pltpu.CompilerParams(vmem_limit_bytes=limit << 20),
        cost_estimate=pl.CostEstimate(flops=flops, bytes_accessed=1 << 20, transcendentals=0),
        name=name,
    )(*args)


def shape(*dims, dtype=BF16):
    return jax.ShapeDtypeStruct(dims, dtype)


def shift_by(step, axis):
    count = lax.axis_size(axis)
    return [(i, (i + step) % count) for i in range(count)]


def swap(value, bits):
    count = lax.axis_size("east") * lax.axis_size("north")
    return lax.ppermute(value, BOTH, [(i, i ^ bits) for i in range(count)])


def local(features, occupancy, weight_first, weight_second, cotangent):
    scale = 1.0 / math.sqrt(128 * 128 * 16)
    occupied = occupancy.reshape(1, 2)
    wide = pltpu.VMEM((CH * 8, LN), F32)
    near = pltpu.VMEM((CH, 8, LN), BF16)

    to_west, to_east = call(
        strips_kernel,
        "strips",
        [shape(STRIP, LN), shape(STRIP, LN)],
        [near, near, pltpu.VMEM((1, 2), jnp.int32), wide, wide, pltpu.SemaphoreType.DMA((3,))],
        60,
        1 << 20,
        [pl.BlockSpec(memory_space=pltpu.HBM)] * 3,
        occupied,
        features,
        cotangent,
    )
    west = lax.ppermute(to_east, "east", shift_by(1, "east"))
    east = lax.ppermute(to_west, "east", shift_by(-1, "east"))

    weight = shape(5, TAPS, LN)
    tile = shape(8, LN, LN)
    image = shape(CH, 8, LN)
    planes = shape(8, CH, LN)
    fwd_one, fwd_two, back_two, back_one, turned_one, own_grid, own_cot, feat, cot, own_mask = call(
        prepare_kernel,
        "prepare",
        [weight] * 4 + [shape(288, 1024), tile, tile, planes, planes, shape(16, LN)],
        [wide, wide],
        12,
        1 << 33,
        [VMEM] * 5,
        weight_first,
        weight_second,
        features,
        cotangent,
        occupied,
    )
    to_south, to_north = call(
        rims_kernel,
        "rims",
        [shape(RIM, LN), shape(RIM, LN)],
        [],
        8,
        1 << 20,
        [VMEM] * 5,
        west,
        east,
        feat,
        cot,
        own_mask,
    )
    south = lax.ppermute(to_north, "north", shift_by(1, "north"))
    north = lax.ppermute(to_south, "north", shift_by(-1, "north"))
    side_grid, side_cot, middle = call(
        sides_kernel,
        "sides",
        [tile, shape(4, LN, LN), shape(3, LN, LN, dtype=F32)],
        [],
        8,
        1 << 31,
        [VMEM] * 3,
        own_mask,
        west,
        east,
    )

    activated, grad_one, masks, keep, send = call(
        lambda *refs: level_kernel(scale, *refs),
        "level",
        [
            image,
            shape(10, 160, LN),
            shape(3, 256, LN, dtype=F32),
            shape(4, 576, LN),
            shape(4, 576, LN),
        ],
        [
            pltpu.VMEM((8, 2, 224, TAPS), BF16),
            pltpu.VMEM((7, 2, 192, TAPS), BF16),
            pltpu.VMEM((16, 128, LN), F32),
            pltpu.VMEM((12, 192, LN), F32),
            pltpu.VMEM((7 * 224, 2 * LN), F32),
            pltpu.VMEM((10, 160, LN), F32),
            pltpu.VMEM((12, 192, LN), BF16),
            pltpu.VMEM((288, 1024), BF16),
            pltpu.VMEM((2592 + 16, LN), F32),
            pltpu.VMEM((2592 + 16, LN), F32),
            pltpu.VMEM((400, LN), F32),
            wide,
        ],
        32,
        1 << 34,
        [VMEM] * 11,
        own_grid,
        side_grid,
        own_cot,
        side_cot,
        middle,
        south,
        north,
        fwd_one,
        fwd_two,
        back_two,
        turned_one,
    )

    part = (keep.astype(F32) + swap(send, 1).astype(F32)).astype(BF16)
    others = [swap(part[k], bits) for k, bits in ((1, 2), (2, 12), (3, 14))]
    feature_grad, token = call(
        final_kernel,
        "final",
        [image, shape(8, LN, dtype=F32)],
        [pltpu.VMEM((5, 2, 128, TAPS), BF16), pltpu.VMEM((512, 2 * LN), F32), wide],
        12,
        1 << 32,
        [VMEM] * 3,
        grad_one,
        masks,
        back_one,
    )
    held, given = call(
        combine_kernel,
        "combine",
        [shape(384, LN), shape(384, LN)],
        [pltpu.VMEM((768, LN), F32)],
        8,
        1 << 20,
        [VMEM] * 5,
        part[0],
        *others,
        token,
    )
    partner, size = 4, 384
    for shift, after, kind in ((3, 192, BF16), (2, 64, BF16), (1, 48, F32), (0, 16, F32)):
        got = swap(given, partner)
        partner, size = after, size // 2
        held, given = call(
            lambda *refs: step_kernel(shift, *refs),
            "step",
            [shape(size, LN, dtype=kind)] * 2,
            [],
            8,
            1 << 20,
            [VMEM] * 2,
            held.reshape(2, size, LN),
            got.reshape(2, size, LN),
        )
    one, two = call(
        finish_kernel,
        "finish",
        [shape(8, LN, dtype=F32), shape(8, LN, dtype=F32)],
        [],
        8,
        1 << 20,
        [VMEM] * 2,
        held,
        swap(given, partner),
    )
    return activated, feature_grad, one.reshape(-1)[0:972], two.reshape(-1)[0:972]


def solution(mesh):
    return jax.shard_map(
        local,
        mesh=mesh,
        in_specs=(
            P(None, "east", "north"),
            P("east", "north", None),
            P(),
            P(),
            P(None, "east", "north"),
        ),
        out_specs=(
            P(None, "east", "north"),
            P(None, "east", "north"),
            P(BOTH),
            P(BOTH),
        ),
        check_vma=False,
    )
```

```python
import math

import jax
import jax.numpy as jnp
from jax import lax
from jax.experimental import pallas as pl
from jax.experimental.pallas import tpu as pltpu
from jax.sharding import PartitionSpec as P

BOTH = ("east", "north")
F32 = jnp.float32
BF16 = jnp.bfloat16
CH = 96
LN = 128
TAPS = 7 * LN
WHOLE = (0, 2, 3, 5, 6, 7, 8)
SPLIT = (1, 1, 1, 4, 4, 4)
STRIP = 6 * CH + 16
RIM = 11 * CH + 48
VMEM = pl.BlockSpec(memory_space=pltpu.VMEM)
SMEM = pl.BlockSpec(memory_space=pltpu.SMEM)


def lanes(rows):
    return lax.broadcasted_iota(jnp.int32, (rows, LN), 1)


def flip_pad(value):
    wide = jnp.concatenate(
        [value.astype(F32), jnp.zeros((LN - value.shape[0], value.shape[1]), F32)], axis=0
    )
    return wide.T


def mask_column(ref, row):
    tile = ref[row : row + 16, :].astype(F32)
    return jnp.concatenate([tile] * 8, axis=0).T


def here():
    return lax.axis_index("east"), lax.axis_index("north")


def as_float(flag):
    return flag.astype(jnp.int32).astype(F32)


def neighbours():
    column, row = here()
    last_column, last_row = lax.axis_size("east") - 1, lax.axis_size("north") - 1
    flags = (column > 0, column < last_column, row > 0, row < last_row)
    return [as_float(flag) for flag in flags]


def mask_tile(occupied):
    levels = occupied[...].astype(F32)
    return jnp.where((lanes(16) & 15) < 8, levels[:, 0:1], levels[:, 1:2]).astype(BF16)


def strips_kernel(
    occupied,
    features,
    cotangent,
    to_west,
    to_east,
    near_feat,
    near_cot,
    near_occupied,
    wide_feat,
    wide_cot,
    sems,
):
    copies = [
        pltpu.make_async_copy(features, near_feat, sems.at[0]),
        pltpu.make_async_copy(cotangent, near_cot, sems.at[1]),
        pltpu.make_async_copy(occupied, near_occupied, sems.at[2]),
    ]
    for copy in copies:
        copy.start()
    for copy, near, wide, start, count in (
        (copies[0], near_feat, wide_feat, 0, 4),
        (copies[1], near_cot, wide_cot, 4, 2),
    ):
        copy.wait()
        wide[...] = near[...].astype(F32).reshape(CH * 8, LN)
        for k in range(count):
            rows = slice((start + k) * CH, (start + k + 1) * CH)
            to_west[rows, :] = wide[pl.ds(k, CH, stride=8), :].astype(BF16)
            to_east[rows, :] = wide[pl.ds(8 - count + k, CH, stride=8), :].astype(BF16)
    copies[2].wait()
    mask = mask_tile(near_occupied)
    to_west[6 * CH : STRIP, :] = mask
    to_east[6 * CH : STRIP, :] = mask


def turn_levels(value, x, turned):
    lane = lanes(CH) & 15
    below = jnp.where(lane == 0, 0.0, pltpu.roll(value, 1, 1))
    above = jnp.where(lane == 15, 0.0, pltpu.roll(value, LN - 1, 1))
    start = x * LN if isinstance(x, int) else pl.multiple_of(x * LN, LN)
    for c, moved in enumerate((below, value, above)):
        turned[c * CH : (c + 1) * CH, pl.ds(start, LN)] = moved.astype(BF16)


def prepare_kernel(
    first,
    second,
    features,
    cotangent,
    occupied,
    fwd_one,
    fwd_two,
    back_two,
    back_one,
    turned_one,
    own_grid,
    own_cot,
    feat,
    cot,
    own_mask,
    wide_feat,
    wide_cot,
):
    wide_feat[...] = features[...].astype(F32).reshape(CH * 8, LN)
    wide_cot[...] = cotangent[...].astype(F32).reshape(CH * 8, LN)
    own_mask[...] = mask_tile(occupied)
    for out in (fwd_one, fwd_two, back_two, back_one):
        out[...] = jnp.zeros_like(out)

    def body(plane, carry):
        for source, ahead, back in ((first, fwd_one, back_one), (second, fwd_two, back_two)):
            for k in range(9):
                straight = source[9 * plane + k]
                turned = jnp.pad(
                    source[26 - 9 * plane - k].astype(F32), ((0, LN - CH), (0, LN - CH))
                ).T.astype(BF16)
                if k in WHOLE:
                    row = WHOLE.index(k) * LN
                    ahead[plane + 1, row : row + CH, 0:CH] = straight
                    back[plane + 1, row : row + CH, :] = turned[0:CH]
                else:
                    for q in range(3):
                        row = (SPLIT.index(k) + q) * LN + CH
                        ahead[plane + 1, row : row + 32, 0:CH] = straight[32 * q : 32 * q + 32]
                        back[plane + 1, row : row + 32, :] = turned[32 * q : 32 * q + 32]
        return carry

    lax.fori_loop(0, 3, body, 0)
    mask = jnp.concatenate([own_mask[...].astype(F32)] * 6, axis=0)
    for x in range(8):
        plain = wide_feat[pl.ds(x, CH, stride=8), :]
        feat[x] = plain.astype(BF16)
        value = plain * mask
        turn_levels(value, x, turned_one)
        own_grid[x] = flip_pad(value).astype(BF16)
        plain = wide_cot[pl.ds(x, CH, stride=8), :]
        cot[x] = plain.astype(BF16)
        own_cot[x] = flip_pad(plain).astype(BF16)


def rims_kernel(west, east, feat, cot, own_mask, to_south, to_north):
    half = lanes(CH) < 64
    quarter = lanes(CH) // 32

    def feat_plane(p):
        if p < 4:
            return west[p * CH : (p + 1) * CH, :].astype(F32)
        if p < 12:
            return feat[p - 4].astype(F32)
        return east[(p - 12) * CH : (p - 11) * CH, :].astype(F32)

    def cot_plane(p):
        if p < 2:
            return west[(4 + p) * CH : (5 + p) * CH, :].astype(F32)
        if p < 10:
            return cot[p - 2].astype(F32)
        return east[(p - 6) * CH : (p - 5) * CH, :].astype(F32)

    for k in range(8):
        one, two = feat_plane(k), feat_plane(k + 8)
        rows = slice(k * CH, (k + 1) * CH)
        to_south[rows, :] = jnp.where(half, one, pltpu.roll(two, 64, 1)).astype(BF16)
        to_north[rows, :] = jnp.where(half, pltpu.roll(one, 64, 1), two).astype(BF16)
    for k in range(3):
        four = [cot_plane(k + 3 * q) for q in range(4)]
        rows = slice((8 + k) * CH, (9 + k) * CH)
        for out, shift in ((to_south, 0), (to_north, 32)):
            moved = [
                pltpu.roll(four[q], (32 * q + shift) % LN, 1) if (32 * q + shift) % LN else four[q]
                for q in range(4)
            ]
            packed = jnp.where(
                quarter < 2,
                jnp.where(quarter == 0, moved[0], moved[1]),
                jnp.where(quarter == 2, moved[2], moved[3]),
            )
            out[rows, :] = packed.astype(BF16)
    for out in (to_south, to_north):
        out[11 * CH : 11 * CH + 16, :] = west[6 * CH : STRIP, :]
        out[11 * CH + 16 : 11 * CH + 32, :] = own_mask[...]
        out[11 * CH + 32 : RIM, :] = east[6 * CH : STRIP, :]


def sides_kernel(own_mask, west, east, side_grid, side_cot, middle):
    has = neighbours()
    middle[0] = mask_column(west, 6 * CH) * has[0]
    middle[1] = mask_column(own_mask, 0)
    middle[2] = mask_column(east, 6 * CH) * has[1]
    for side, ref in ((0, west), (1, east)):
        for k in range(4):
            block = flip_pad(ref[k * CH : (k + 1) * CH, :]) * middle[2 * side]
            side_grid[4 * side + k] = block.astype(BF16)
        for k in range(2):
            side_cot[2 * side + k] = flip_pad(ref[(4 + k) * CH : (5 + k) * CH, :]).astype(BF16)


def spread(taps, plane, value, rows):
    count = rows + 32
    level = lax.broadcasted_iota(jnp.int32, (count, LN), 0) & 15
    below = jnp.where(level == 0, 0.0, pltpu.roll(value, 1, 0))
    above = jnp.where(level == 15, 0.0, pltpu.roll(value, count - 1, 0))
    spare = lanes(count) >= CH
    short = [moved.astype(BF16) for moved in (below, value, above)]
    rest = [
        jnp.where(spare, pltpu.roll(value, CH - 32 * q, 1), 0.0).astype(BF16) for q in range(3)
    ]
    for n, k in enumerate(WHOLE):
        start = 16 * (k // 3)
        block = short[k % 3][start : start + rows]
        if n < 6:
            start = 16 * (SPLIT[n] // 3)
            block = block + rest[n % 3][start : start + rows]
        taps[plane // 2, plane % 2, 0:rows, n * LN : (n + 1) * LN] = block


def convolve(taps, weight, total, pair, rows):
    left = jnp.concatenate(
        [taps[pair + j // 2, j % 2, 0:rows, :] for j in range(4)], axis=1
    )
    right = jnp.concatenate(
        [jnp.concatenate([weight[j + 1], weight[j]], axis=1) for j in range(4)], axis=0
    )
    total[pair * rows : (pair + 1) * rows, :] = jnp.dot(left, right, preferred_element_type=F32)


def half_of(total, p, rows):
    start = p % 2 * LN
    return total[p // 2 * rows : (p // 2 + 1) * rows, start : start + LN]


HOPS = (1, 12, 192, 64, 4, 48, 16, 2)


def path(code):
    mask = 0
    for k, hop in enumerate(HOPS):
        if code >> (7 - k) & 1:
            mask ^= hop
    return mask


def kernel_grad(turned, planes, shift, scale, result):
    def piece(k):
        a, b = k // 3, k % 3
        start = (shift + 1 - b) * 16
        return planes[shift + 1 - a : shift + 9 - a, start : start + 128, :].reshape(1024, LN)

    for k in range(0, 9, 2):
        right = jnp.concatenate([piece(k), piece(min(k + 1, 8))], axis=1)
        part = jnp.dot(turned[...], right, preferred_element_type=F32) * scale
        result[k * 288 : k * 288 + 288, :] = part[:, 0:LN]
        if k < 8:
            result[(k + 1) * 288 : (k + 1) * 288 + 288, :] = part[:, LN : 2 * LN]


def band(p, low, high):
    return int(p >= low) + int(p >= high)


def level_kernel(
    scale,
    own_grid,
    side_grid,
    own_cot,
    side_cot,
    middle,
    south,
    north,
    fwd_one,
    fwd_two,
    back_two,
    turned_one,
    activated,
    grad_one,
    masks,
    keep,
    send,
    taps_one,
    taps_two,
    taps_three,
    total_one,
    total_two,
    total_three,
    edge,
    upstream,
    slope_one,
    grad_two,
    turned_two,
    grad_one_sum,
    grad_two_sum,
    packed,
    rows,
):
    has = neighbours()
    for ref, flag, row in ((south, has[2], 0), (north, has[3], 192)):
        tile = ref[11 * CH : 11 * CH + 48, :].astype(F32) * flag
        turned = jnp.concatenate([tile, jnp.zeros((80, LN), F32)], axis=0).T[0:64]
        for bx in range(3):
            side = has[bx // 2] if bx != 1 else 1.0
            column = turned[:, 16 * bx : 16 * bx + 1] * side
            masks[bx, row : row + 64, :] = jnp.broadcast_to(column, (64, LN))
    masks[:, 64:192, :] = middle[...]

    for k in range(8):
        for ref, row in ((south, 0), (north, 64)):
            both = flip_pad(ref[k * CH : (k + 1) * CH, :])
            edge[k, row : row + 64, :] = both[0:64]
            edge[k + 8, row : row + 64, :] = both[64:128]
    for k in range(3):
        for ref, row in ((south, 0), (north, 160)):
            four = flip_pad(ref[(8 + k) * CH : (9 + k) * CH, :])
            for q in range(4):
                upstream[k + 3 * q, row : row + 32, :] = four[32 * q : 32 * q + 32]
    for k in range(2):
        upstream[k, 32:160, :] = side_cot[k].astype(F32)
        upstream[10 + k, 32:160, :] = side_cot[2 + k].astype(F32)
    for k in range(8):
        upstream[2 + k, 32:160, :] = own_cot[k].astype(F32)

    def begin(p):
        bx = band(p, 4, 12)
        value = own_grid[p - 4] if bx == 1 else side_grid[p % 8]
        low = edge[p, 0:64, :] * masks[bx, 0:64, :]
        high = edge[p, 64:128, :] * masks[bx, 192:256, :]
        spread(taps_one, p, jnp.concatenate([low, value.astype(F32), high], axis=0), 224)

    def after_one(p):
        value = half_of(total_one, p, 224) * masks[band(p, 3, 11), 16:240, :]
        sigma = jax.nn.sigmoid(value)
        if 2 <= p < 12:
            slope_one[p - 2] = (sigma * (1.0 + value * (1.0 - sigma)))[32:192]
        hidden = (value * sigma).astype(BF16).astype(F32)
        spread(taps_two, p, hidden, 192)
        if 3 <= p < 11:
            turn_levels(hidden[48:176].T[0:CH], p - 3, turned_two)

    def after_two(p):
        mask = masks[band(p, 2, 10), 32:224, :]
        value = half_of(total_two, p, 192) * mask
        sigma = jax.nn.sigmoid(value)
        if 2 <= p < 10:
            rows[pl.ds(p - 2, CH, stride=8), :] = (value * sigma)[32:160].T[0:CH]
        slope = sigma * (1.0 + value * (1.0 - sigma))
        grad = upstream[p] * slope * mask
        grad_two[p] = grad.astype(BF16)
        spread(taps_three, p, grad, 160)

    def after_three(p):
        grad = half_of(total_three, p, 160) * slope_one[p] * masks[band(p, 1, 9), 48:208, :]
        grad_one[p] = grad.astype(BF16)

    for p in range(4):
        begin(p)
    for t in range(12):
        if t < 7:
            convolve(taps_one, fwd_one, total_one, t, 224)
        if t < 6:
            begin(2 * t + 4)
            begin(2 * t + 5)
        if 1 <= t < 8:
            after_one(2 * t - 2)
            after_one(2 * t - 1)
        if 3 <= t < 9:
            convolve(taps_two, fwd_two, total_two, t - 3, 192)
        if 4 <= t < 10:
            after_two(2 * t - 8)
            after_two(2 * t - 7)
        if 6 <= t < 11:
            convolve(taps_three, back_two, total_three, t - 6, 160)
        if 7 <= t < 12:
            after_three(2 * t - 14)
            after_three(2 * t - 13)
        if t == 10:
            kernel_grad(turned_two, grad_two, 2, scale, grad_two_sum)
    activated[...] = rows[...].reshape(CH, 8, LN).astype(BF16)
    kernel_grad(turned_one, grad_one, 1, scale, grad_one_sum)

    column, row = here()
    position = column * 16 + row
    spare = lanes(48) >= CH
    for grad, source in ((1, grad_two_sum), (0, grad_one_sum)):
        for code in range(256):
            owner = jnp.bitwise_xor(position, path(code))
            start = 81 * (owner >> 3) + 10 * (owner & 7)
            packed[24 * code + 12 * grad : 24 * code + 12 * grad + 12, :] = source[
                pl.ds(start, 12), :
            ]
    for code in range(0, 256, 8):
        block = [packed[24 * code + 48 * k : 24 * code + 48 * k + 48, :] for k in range(4)]
        out = keep if code < 128 else send
        first = 144 * (code // 8 % 4)
        for k in range(3):
            mixed = jnp.where(spare, pltpu.roll(block[3], CH - 32 * k, 1), block[k])
            out[code // 32 % 4, first + 48 * k : first + 48 * k + 48, :] = mixed.astype(BF16)


def final_kernel(grad_one, masks, back_one, feature_grad, token, taps, total, rows):
    token[...] = jnp.zeros_like(token)
    for p in range(10):
        spread(taps, p, grad_one[p].astype(F32), 128)

    def after_four(p):
        value = half_of(total, p, 128)
        rows[pl.ds(p, CH, stride=8), :] = (value * masks[1, 64:192, :]).T[0:CH]

    for t in range(5):
        if t < 4:
            convolve(taps, back_one, total, t, 128)
        if t > 0:
            after_four(2 * t - 2)
            after_four(2 * t - 1)
    feature_grad[...] = rows[...].reshape(CH, 8, LN).astype(BF16)


def gather_kernel(a0, a1, a2, a3, token, *outs):
    for k, out in enumerate(outs):
        piece = slice(144 * k, 144 * k + 144)
        out[...] = sum(ref[piece, :].astype(F32) for ref in (a0, a1, a2, a3)).astype(BF16)


def unpack_kernel(a0, a1, a2, a3, hold, give):
    lane = lanes(48)
    a, b, c = (
        sum(ref[48 * k : 48 * k + 48, :].astype(F32) for ref in (a0, a1, a2, a3))
        for k in range(3)
    )
    last = jnp.where(
        lane < 32,
        pltpu.roll(a, 32, 1),
        jnp.where(lane < 64, pltpu.roll(b, 64, 1), pltpu.roll(c, 96, 1)),
    )
    for out, pair in ((hold, (a, b)), (give, (c, last))):
        out[...] = jnp.concatenate(pair, axis=0).astype(BF16)


def step_kernel(held, got, hold, give):
    size = hold.shape[0]
    total = held[...].astype(F32) + got[...].astype(F32)
    hold[...] = total[0:size].astype(hold.dtype)
    give[...] = total[size : 2 * size].astype(give.dtype)


def finish_kernel(held, got, out_one, out_two):
    j = lax.axis_index("north") & 7
    lane = lanes(1)
    value = held[...] + got[...]
    for grad, out in ((0, out_one), (1, out_two)):
        flat = []
        for m in range(3):
            r = [value[12 * grad + 4 * m + q : 12 * grad + 4 * m + q + 1] for q in range(4)]
            flat.append(jnp.where(lane < 96, r[0], pltpu.roll(r[1], 96, 1)))
            flat.append(jnp.where(lane < 64, pltpu.roll(r[1], 96, 1), pltpu.roll(r[2], 64, 1)))
            flat.append(jnp.where(lane < 32, pltpu.roll(r[2], 64, 1), pltpu.roll(r[3], 32, 1)))
        low = jnp.concatenate(flat[0:8], axis=0)
        high = jnp.concatenate(flat[1:9], axis=0)
        turn = lax.rem(LN - 12 * j, LN)
        out[...] = jnp.where(
            lanes(8) < LN - 12 * j, pltpu.roll(low, turn, 1), pltpu.roll(high, turn, 1)
        )


def call(kernel, name, outs, scratch, limit, flops, specs, *args):
    return pl.pallas_call(
        kernel,
        out_shape=outs,
        in_specs=specs,
        out_specs=[VMEM] * len(outs),
        scratch_shapes=scratch,
        compiler_params=pltpu.CompilerParams(vmem_limit_bytes=limit << 20),
        cost_estimate=pl.CostEstimate(flops=flops, bytes_accessed=1 << 20, transcendentals=0),
        name=name,
    )(*args)


def shape(*dims, dtype=BF16):
    return jax.ShapeDtypeStruct(dims, dtype)


def shift_by(step, axis):
    count = lax.axis_size(axis)
    return [(i, (i + step) % count) for i in range(count)]


def swap(value, bits):
    count = lax.axis_size("east") * lax.axis_size("north")
    return lax.ppermute(value, BOTH, [(i, i ^ bits) for i in range(count)])


def local(features, occupancy, weight_first, weight_second, cotangent):
    scale = 1.0 / math.sqrt(128 * 128 * 16)
    occupied = occupancy.reshape(1, 2)
    wide = pltpu.VMEM((CH * 8, LN), F32)
    near = pltpu.VMEM((CH, 8, LN), BF16)

    to_west, to_east = call(
        strips_kernel,
        "strips",
        [shape(STRIP, LN), shape(STRIP, LN)],
        [near, near, pltpu.VMEM((1, 2), jnp.int32), wide, wide, pltpu.SemaphoreType.DMA((3,))],
        60,
        1 << 20,
        [pl.BlockSpec(memory_space=pltpu.HBM)] * 3,
        occupied,
        features,
        cotangent,
    )
    west = lax.ppermute(to_east, "east", shift_by(1, "east"))
    east = lax.ppermute(to_west, "east", shift_by(-1, "east"))

    weight = shape(5, TAPS, LN)
    tile = shape(8, LN, LN)
    image = shape(CH, 8, LN)
    planes = shape(8, CH, LN)
    fwd_one, fwd_two, back_two, back_one, turned_one, own_grid, own_cot, feat, cot, own_mask = call(
        prepare_kernel,
        "prepare",
        [weight] * 4 + [shape(288, 1024), tile, tile, planes, planes, shape(16, LN)],
        [wide, wide],
        12,
        1 << 33,
        [VMEM] * 5,
        weight_first,
        weight_second,
        features,
        cotangent,
        occupied,
    )
    to_south, to_north = call(
        rims_kernel,
        "rims",
        [shape(RIM, LN), shape(RIM, LN)],
        [],
        8,
        1 << 20,
        [VMEM] * 5,
        west,
        east,
        feat,
        cot,
        own_mask,
    )
    south = lax.ppermute(to_north, "north", shift_by(1, "north"))
    north = lax.ppermute(to_south, "north", shift_by(-1, "north"))
    side_grid, side_cot, middle = call(
        sides_kernel,
        "sides",
        [tile, shape(4, LN, LN), shape(3, LN, LN, dtype=F32)],
        [],
        8,
        1 << 31,
        [VMEM] * 3,
        own_mask,
        west,
        east,
    )

    activated, grad_one, masks, keep, send = call(
        lambda *refs: level_kernel(scale, *refs),
        "level",
        [
            image,
            shape(10, 160, LN),
            shape(3, 256, LN, dtype=F32),
            shape(4, 576, LN),
            shape(4, 576, LN),
        ],
        [
            pltpu.VMEM((8, 2, 224, TAPS), BF16),
            pltpu.VMEM((7, 2, 192, TAPS), BF16),
            pltpu.VMEM((6, 2, 160, TAPS), BF16),
            pltpu.VMEM((7 * 224, 2 * LN), F32),
            pltpu.VMEM((6 * 192, 2 * LN), F32),
            pltpu.VMEM((5 * 160, 2 * LN), F32),
            pltpu.VMEM((16, 128, LN), F32),
            pltpu.VMEM((12, 192, LN), F32),
            pltpu.VMEM((10, 160, LN), F32),
            pltpu.VMEM((12, 192, LN), BF16),
            pltpu.VMEM((288, 1024), BF16),
            pltpu.VMEM((2592 + 16, LN), F32),
            pltpu.VMEM((2592 + 16, LN), F32),
            pltpu.VMEM((256 * 24, LN), F32),
            wide,
        ],
        40,
        1 << 34,
        [VMEM] * 11,
        own_grid,
        side_grid,
        own_cot,
        side_cot,
        middle,
        south,
        north,
        fwd_one,
        fwd_two,
        back_two,
        turned_one,
    )

    part = (keep.astype(F32) + swap(send, 1).astype(F32)).astype(BF16)
    others = [swap(part[k], bits) for k, bits in ((2, 12), (1, 192), (3, 204))]
    feature_grad, token = call(
        final_kernel,
        "final",
        [image, shape(8, LN, dtype=F32)],
        [pltpu.VMEM((5, 2, 128, TAPS), BF16), pltpu.VMEM((512, 2 * LN), F32), wide],
        12,
        1 << 32,
        [VMEM] * 3,
        grad_one,
        masks,
        back_one,
    )
    pieces = call(
        gather_kernel,
        "gather",
        [shape(144, LN)] * 4,
        [],
        8,
        1 << 20,
        [VMEM] * 5,
        part[0],
        *others,
        token,
    )
    others = [swap(pieces[k], bits) for k, bits in ((2, 64), (1, 4), (3, 68))]
    held, given = call(
        unpack_kernel,
        "unpack",
        [shape(96, LN), shape(96, LN)],
        [],
        8,
        1 << 20,
        [VMEM] * 4,
        pieces[0],
        *others,
    )
    for partner, size, kind in ((48, 48, BF16), (16, 24, F32)):
        held, given = call(
            step_kernel,
            "step",
            [shape(size, LN, dtype=kind)] * 2,
            [],
            8,
            1 << 20,
            [VMEM] * 2,
            held,
            swap(given, partner),
        )
    one, two = call(
        finish_kernel,
        "finish",
        [shape(8, LN, dtype=F32), shape(8, LN, dtype=F32)],
        [],
        8,
        1 << 20,
        [VMEM] * 2,
        held,
        swap(given, 2),
    )
    return activated, feature_grad, one.reshape(-1)[0:972], two.reshape(-1)[0:972]


def solution(mesh):
    return jax.shard_map(
        local,
        mesh=mesh,
        in_specs=(
            P(None, "east", "north"),
            P("east", "north", None),
            P(),
            P(),
            P(None, "east", "north"),
        ),
        out_specs=(
            P(None, "east", "north"),
            P(None, "east", "north"),
            P(BOTH),
            P(BOTH),
        ),
        check_vma=False,
    )
```

```python
import math

import jax
import jax.numpy as jnp
from jax import lax
from jax.experimental import pallas as pl
from jax.experimental.pallas import tpu as pltpu
from jax.sharding import PartitionSpec as P

BOTH = ("east", "north")
F32 = jnp.float32
BF16 = jnp.bfloat16
CH = 96
LN = 128
TAPS = 7 * LN
WHOLE = (0, 2, 3, 5, 6, 7, 8)
SPLIT = (1, 1, 1, 4, 4, 4)
STRIP = 6 * CH + 16
RIM = 11 * CH + 48
VMEM = pl.BlockSpec(memory_space=pltpu.VMEM)
SMEM = pl.BlockSpec(memory_space=pltpu.SMEM)


def lanes(rows):
    return lax.broadcasted_iota(jnp.int32, (rows, LN), 1)


def flip_pad(value):
    wide = jnp.concatenate(
        [value.astype(F32), jnp.zeros((LN - value.shape[0], value.shape[1]), F32)], axis=0
    )
    return wide.T


def mask_column(ref, row):
    tile = ref[row : row + 16, :].astype(F32)
    return jnp.concatenate([tile] * 8, axis=0).T


def here():
    return lax.axis_index("east"), lax.axis_index("north")


def as_float(flag):
    return flag.astype(jnp.int32).astype(F32)


def neighbours():
    column, row = here()
    last_column, last_row = lax.axis_size("east") - 1, lax.axis_size("north") - 1
    flags = (column > 0, column < last_column, row > 0, row < last_row)
    return [as_float(flag) for flag in flags]


def mask_tile(occupied):
    levels = occupied[...].astype(F32)
    return jnp.where((lanes(16) & 15) < 8, levels[:, 0:1], levels[:, 1:2]).astype(BF16)


def strips_kernel(
    occupied,
    features,
    cotangent,
    to_west,
    to_east,
    near_feat,
    near_cot,
    near_occupied,
    wide_feat,
    wide_cot,
    sems,
):
    copies = [
        pltpu.make_async_copy(features, near_feat, sems.at[0]),
        pltpu.make_async_copy(cotangent, near_cot, sems.at[1]),
        pltpu.make_async_copy(occupied, near_occupied, sems.at[2]),
    ]
    for copy in copies:
        copy.start()
    for copy, near, wide, start, count in (
        (copies[0], near_feat, wide_feat, 0, 4),
        (copies[1], near_cot, wide_cot, 4, 2),
    ):
        copy.wait()
        wide[...] = near[...].astype(F32).reshape(CH * 8, LN)
        for k in range(count):
            rows = slice((start + k) * CH, (start + k + 1) * CH)
            to_west[rows, :] = wide[pl.ds(k, CH, stride=8), :].astype(BF16)
            to_east[rows, :] = wide[pl.ds(8 - count + k, CH, stride=8), :].astype(BF16)
    copies[2].wait()
    mask = mask_tile(near_occupied)
    to_west[6 * CH : STRIP, :] = mask
    to_east[6 * CH : STRIP, :] = mask


def turn_levels(value, x, turned):
    lane = lanes(CH) & 15
    below = jnp.where(lane == 0, 0.0, pltpu.roll(value, 1, 1))
    above = jnp.where(lane == 15, 0.0, pltpu.roll(value, LN - 1, 1))
    start = x * LN if isinstance(x, int) else pl.multiple_of(x * LN, LN)
    for c, moved in enumerate((below, value, above)):
        turned[c * CH : (c + 1) * CH, pl.ds(start, LN)] = moved.astype(BF16)


def prepare_kernel(
    first,
    second,
    features,
    cotangent,
    occupied,
    fwd_one,
    fwd_two,
    back_two,
    back_one,
    turned_one,
    own_grid,
    own_cot,
    feat,
    cot,
    own_mask,
    wide_feat,
    wide_cot,
):
    wide_feat[...] = features[...].astype(F32).reshape(CH * 8, LN)
    wide_cot[...] = cotangent[...].astype(F32).reshape(CH * 8, LN)
    own_mask[...] = mask_tile(occupied)
    for out in (fwd_one, fwd_two, back_two, back_one):
        out[...] = jnp.zeros_like(out)

    def body(plane, carry):
        for source, ahead, back in ((first, fwd_one, back_one), (second, fwd_two, back_two)):
            for k in range(9):
                straight = source[9 * plane + k]
                turned = jnp.pad(
                    source[26 - 9 * plane - k].astype(F32), ((0, LN - CH), (0, LN - CH))
                ).T.astype(BF16)
                if k in WHOLE:
                    row = WHOLE.index(k) * LN
                    ahead[plane + 1, row : row + CH, 0:CH] = straight
                    back[plane + 1, row : row + CH, :] = turned[0:CH]
                else:
                    for q in range(3):
                        row = (SPLIT.index(k) + q) * LN + CH
                        ahead[plane + 1, row : row + 32, 0:CH] = straight[32 * q : 32 * q + 32]
                        back[plane + 1, row : row + 32, :] = turned[32 * q : 32 * q + 32]
        return carry

    lax.fori_loop(0, 3, body, 0)
    mask = jnp.concatenate([own_mask[...].astype(F32)] * 6, axis=0)
    for x in range(8):
        plain = wide_feat[pl.ds(x, CH, stride=8), :]
        feat[x] = plain.astype(BF16)
        value = plain * mask
        turn_levels(value, x, turned_one)
        own_grid[x] = flip_pad(value).astype(BF16)
        plain = wide_cot[pl.ds(x, CH, stride=8), :]
        cot[x] = plain.astype(BF16)
        own_cot[x] = flip_pad(plain).astype(BF16)


def northern(row):
    return (row & 1) == 0


def rims_kernel(west, east, feat, cot, own_mask, first, second):
    even = northern(lax.axis_index("north"))
    half = lanes(CH) < 64
    quarter = lanes(CH) // 32

    def feat_plane(p):
        if p < 4:
            return west[p * CH : (p + 1) * CH, :].astype(F32)
        if p < 12:
            return feat[p - 4].astype(F32)
        return east[(p - 12) * CH : (p - 11) * CH, :].astype(F32)

    def cot_plane(p):
        if p < 2:
            return west[(4 + p) * CH : (5 + p) * CH, :].astype(F32)
        if p < 10:
            return cot[p - 2].astype(F32)
        return east[(p - 6) * CH : (p - 5) * CH, :].astype(F32)

    for k in range(8):
        one, two = feat_plane(k), feat_plane(k + 8)
        rows = slice(k * CH, (k + 1) * CH)
        low = jnp.where(half, one, pltpu.roll(two, 64, 1))
        high = jnp.where(half, pltpu.roll(one, 64, 1), two)
        first[rows, :] = jnp.where(even, high, low).astype(BF16)
        second[rows, :] = jnp.where(even, low, high).astype(BF16)
    for k in range(3):
        four = [cot_plane(k + 3 * q) for q in range(4)]
        rows = slice((8 + k) * CH, (9 + k) * CH)
        packs = []
        for shift in (0, 32):
            moved = [
                pltpu.roll(four[q], (32 * q + shift) % LN, 1) if (32 * q + shift) % LN else four[q]
                for q in range(4)
            ]
            packed = jnp.where(
                quarter < 2,
                jnp.where(quarter == 0, moved[0], moved[1]),
                jnp.where(quarter == 2, moved[2], moved[3]),
            )
            packs.append(packed)
        low, high = packs
        first[rows, :] = jnp.where(even, high, low).astype(BF16)
        second[rows, :] = jnp.where(even, low, high).astype(BF16)
    for out in (first, second):
        out[11 * CH : 11 * CH + 16, :] = west[6 * CH : STRIP, :]
        out[11 * CH + 16 : 11 * CH + 32, :] = own_mask[...]
        out[11 * CH + 32 : RIM, :] = east[6 * CH : STRIP, :]


def sides_kernel(own_mask, west, east, side_grid, side_cot, middle):
    has = neighbours()
    middle[0] = mask_column(west, 6 * CH) * has[0]
    middle[1] = mask_column(own_mask, 0)
    middle[2] = mask_column(east, 6 * CH) * has[1]
    for side, ref in ((0, west), (1, east)):
        for k in range(4):
            block = flip_pad(ref[k * CH : (k + 1) * CH, :]) * middle[2 * side]
            side_grid[4 * side + k] = block.astype(BF16)
        for k in range(2):
            side_cot[2 * side + k] = flip_pad(ref[(4 + k) * CH : (5 + k) * CH, :]).astype(BF16)


def spread(taps, plane, value, rows):
    count = rows + 32
    level = lax.broadcasted_iota(jnp.int32, (count, LN), 0) & 15
    below = jnp.where(level == 0, 0.0, pltpu.roll(value, 1, 0))
    above = jnp.where(level == 15, 0.0, pltpu.roll(value, count - 1, 0))
    spare = lanes(count) >= CH
    short = [moved.astype(BF16) for moved in (below, value, above)]
    rest = [
        jnp.where(spare, pltpu.roll(value, CH - 32 * q, 1), 0.0).astype(BF16) for q in range(3)
    ]
    for n, k in enumerate(WHOLE):
        start = 16 * (k // 3)
        block = short[k % 3][start : start + rows]
        if n < 6:
            start = 16 * (SPLIT[n] // 3)
            block = block + rest[n % 3][start : start + rows]
        taps[plane // 2, plane % 2, 0:rows, n * LN : (n + 1) * LN] = block


def convolve(taps, weight, total, pair, rows):
    left = jnp.concatenate(
        [taps[pair + j // 2, j % 2, 0:rows, :] for j in range(4)], axis=1
    )
    right = jnp.concatenate(
        [jnp.concatenate([weight[j + 1], weight[j]], axis=1) for j in range(4)], axis=0
    )
    total[pair * rows : (pair + 1) * rows, :] = jnp.dot(left, right, preferred_element_type=F32)


def half_of(total, p, rows):
    start = p % 2 * LN
    return total[p // 2 * rows : (p // 2 + 1) * rows, start : start + LN]


HOPS = (1, 12, 192, 64, 4, 48, 16, 2)


def path(code):
    mask = 0
    for k, hop in enumerate(HOPS):
        if code >> (7 - k) & 1:
            mask ^= hop
    return mask


def kernel_grad(turned, planes, shift, scale, result, part):
    def piece(k):
        first = shift + 1 - k // 3 + 4 * part
        start = (shift + 1 - k % 3) * 16
        return planes[first : first + 4, start : start + 128, :].reshape(512, LN)

    left = turned[:, 512 * part : 512 * part + 512]
    for k in range(0, 9, 2):
        right = jnp.concatenate([piece(k), piece(min(k + 1, 8))], axis=1)
        value = jnp.dot(left, right, preferred_element_type=F32) * scale
        for q in range(min(2, 9 - k)):
            rows = slice((k + q) * 288, (k + q + 1) * 288)
            if part:
                result[rows, :] += value[:, q * LN : (q + 1) * LN]
            else:
                result[rows, :] = value[:, q * LN : (q + 1) * LN]


def band(p, low, high):
    return int(p >= low) + int(p >= high)


def level_kernel(
    scale,
    own_grid,
    side_grid,
    own_cot,
    side_cot,
    middle,
    first,
    second,
    fwd_one,
    fwd_two,
    back_two,
    turned_one,
    activated,
    grad_one,
    masks,
    keep,
    send,
    taps_one,
    taps_two,
    taps_three,
    total_one,
    total_two,
    total_three,
    edge,
    upstream,
    slope_one,
    grad_two,
    turned_two,
    grad_one_sum,
    grad_two_sum,
    packed,
    rows,
):
    has = neighbours()
    even = northern(lax.axis_index("north"))

    def halos(start, count):
        a = first[start : start + count, :].astype(F32)
        b = second[start : start + count, :].astype(F32)
        return jnp.where(even, b, a), jnp.where(even, a, b)

    for tile, flag, row in zip(halos(11 * CH, 48), has[2:], (0, 192)):
        turned = jnp.concatenate([tile * flag, jnp.zeros((80, LN), F32)], axis=0).T[0:64]
        for bx in range(3):
            side = has[bx // 2] if bx != 1 else 1.0
            column = turned[:, 16 * bx : 16 * bx + 1] * side
            masks[bx, row : row + 64, :] = jnp.broadcast_to(column, (64, LN))
    masks[:, 64:192, :] = middle[...]

    for k in range(8):
        for block, row in zip(halos(k * CH, CH), (0, 64)):
            both = flip_pad(block)
            edge[k, row : row + 64, :] = both[0:64]
            edge[k + 8, row : row + 64, :] = both[64:128]
    for k in range(3):
        for block, row in zip(halos((8 + k) * CH, CH), (0, 160)):
            four = flip_pad(block)
            for q in range(4):
                upstream[k + 3 * q, row : row + 32, :] = four[32 * q : 32 * q + 32]
    for k in range(2):
        upstream[k, 32:160, :] = side_cot[k].astype(F32)
        upstream[10 + k, 32:160, :] = side_cot[2 + k].astype(F32)
    for k in range(8):
        upstream[2 + k, 32:160, :] = own_cot[k].astype(F32)

    def begin(p):
        bx = band(p, 4, 12)
        value = own_grid[p - 4] if bx == 1 else side_grid[p % 8]
        low = edge[p, 0:64, :] * masks[bx, 0:64, :]
        high = edge[p, 64:128, :] * masks[bx, 192:256, :]
        spread(taps_one, p, jnp.concatenate([low, value.astype(F32), high], axis=0), 224)

    def after_one(p):
        value = half_of(total_one, p, 224) * masks[band(p, 3, 11), 16:240, :]
        sigma = jax.nn.sigmoid(value)
        if 2 <= p < 12:
            slope_one[p - 2] = (sigma * (1.0 + value * (1.0 - sigma)))[32:192]
        hidden = (value * sigma).astype(BF16).astype(F32)
        spread(taps_two, p, hidden, 192)
        if 3 <= p < 11:
            turn_levels(hidden[48:176].T[0:CH], p - 3, turned_two)

    def after_two(p):
        mask = masks[band(p, 2, 10), 32:224, :]
        value = half_of(total_two, p, 192) * mask
        sigma = jax.nn.sigmoid(value)
        if 2 <= p < 10:
            rows[pl.ds(p - 2, CH, stride=8), :] = (value * sigma)[32:160].T[0:CH]
        slope = sigma * (1.0 + value * (1.0 - sigma))
        grad = upstream[p] * slope * mask
        grad_two[p] = grad.astype(BF16)
        spread(taps_three, p, grad, 160)

    def after_three(p):
        grad = half_of(total_three, p, 160) * slope_one[p] * masks[band(p, 1, 9), 48:208, :]
        grad_one[p] = grad.astype(BF16)

    for p in range(4):
        begin(p)
    for t in range(12):
        if t < 7:
            convolve(taps_one, fwd_one, total_one, t, 224)
        if t < 6:
            begin(2 * t + 4)
            begin(2 * t + 5)
        if 1 <= t < 8:
            after_one(2 * t - 2)
            after_one(2 * t - 1)
        if 3 <= t < 9:
            convolve(taps_two, fwd_two, total_two, t - 3, 192)
        if 4 <= t < 10:
            after_two(2 * t - 8)
            after_two(2 * t - 7)
        if 6 <= t < 11:
            convolve(taps_three, back_two, total_three, t - 6, 160)
        if 7 <= t < 12:
            after_three(2 * t - 14)
            after_three(2 * t - 13)
        if t == 8:
            kernel_grad(turned_two, grad_two, 2, scale, grad_two_sum, 0)
        if t == 9:
            activated[...] = rows[...].reshape(CH, 8, LN).astype(BF16)
            kernel_grad(turned_two, grad_two, 2, scale, grad_two_sum, 1)
        if t == 10:
            kernel_grad(turned_one, grad_one, 1, scale, grad_one_sum, 0)
    kernel_grad(turned_one, grad_one, 1, scale, grad_one_sum, 1)

    column, row = here()
    position = column * 16 + row
    spare = lanes(48) >= CH
    for grad, source in ((1, grad_two_sum), (0, grad_one_sum)):
        for code in range(256):
            owner = jnp.bitwise_xor(position, path(code))
            start = 81 * (owner >> 3) + 10 * (owner & 7)
            packed[24 * code + 12 * grad : 24 * code + 12 * grad + 12, :] = source[
                pl.ds(start, 12), :
            ]
    for code in range(0, 256, 8):
        block = [packed[24 * code + 48 * k : 24 * code + 48 * k + 48, :] for k in range(4)]
        out = keep if code < 128 else send
        first = 144 * (code // 8 % 4)
        for k in range(3):
            mixed = jnp.where(spare, pltpu.roll(block[3], CH - 32 * k, 1), block[k])
            out[code // 32 % 4, first + 48 * k : first + 48 * k + 48, :] = mixed.astype(BF16)


def final_kernel(grad_one, masks, back_one, feature_grad, token, taps, total, rows):
    token[...] = jnp.zeros_like(token)
    for p in range(10):
        spread(taps, p, grad_one[p].astype(F32), 128)

    def after_four(p):
        value = half_of(total, p, 128)
        rows[pl.ds(p, CH, stride=8), :] = (value * masks[1, 64:192, :]).T[0:CH]

    for t in range(5):
        if t < 4:
            convolve(taps, back_one, total, t, 128)
        if t > 0:
            after_four(2 * t - 2)
            after_four(2 * t - 1)
    feature_grad[...] = rows[...].reshape(CH, 8, LN).astype(BF16)


def gather_kernel(a0, a1, a2, a3, token, *outs):
    for k, out in enumerate(outs):
        piece = slice(144 * k, 144 * k + 144)
        out[...] = sum(ref[piece, :].astype(F32) for ref in (a0, a1, a2, a3)).astype(BF16)


def unpack_kernel(a0, a1, a2, a3, hold, give):
    lane = lanes(48)
    a, b, c = (
        sum(ref[48 * k : 48 * k + 48, :].astype(F32) for ref in (a0, a1, a2, a3))
        for k in range(3)
    )
    last = jnp.where(
        lane < 32,
        pltpu.roll(a, 32, 1),
        jnp.where(lane < 64, pltpu.roll(b, 64, 1), pltpu.roll(c, 96, 1)),
    )
    for out, pair in ((hold, (a, b)), (give, (c, last))):
        out[...] = jnp.concatenate(pair, axis=0).astype(BF16)


def step_kernel(held, got, hold, give):
    size = hold.shape[0]
    total = held[...].astype(F32) + got[...].astype(F32)
    hold[...] = total[0:size].astype(hold.dtype)
    give[...] = total[size : 2 * size].astype(give.dtype)


def finish_kernel(held, got, out_one, out_two):
    j = lax.axis_index("north") & 7
    lane = lanes(1)
    value = held[...] + got[...]
    for grad, out in ((0, out_one), (1, out_two)):
        flat = []
        for m in range(3):
            r = [value[12 * grad + 4 * m + q : 12 * grad + 4 * m + q + 1] for q in range(4)]
            flat.append(jnp.where(lane < 96, r[0], pltpu.roll(r[1], 96, 1)))
            flat.append(jnp.where(lane < 64, pltpu.roll(r[1], 96, 1), pltpu.roll(r[2], 64, 1)))
            flat.append(jnp.where(lane < 32, pltpu.roll(r[2], 64, 1), pltpu.roll(r[3], 32, 1)))
        low = jnp.concatenate(flat[0:8], axis=0)
        high = jnp.concatenate(flat[1:9], axis=0)
        turn = lax.rem(LN - 12 * j, LN)
        out[...] = jnp.where(
            lanes(8) < LN - 12 * j, pltpu.roll(low, turn, 1), pltpu.roll(high, turn, 1)
        )


def call(kernel, name, outs, scratch, limit, flops, specs, *args):
    return pl.pallas_call(
        kernel,
        out_shape=outs,
        in_specs=specs,
        out_specs=[VMEM] * len(outs),
        scratch_shapes=scratch,
        compiler_params=pltpu.CompilerParams(vmem_limit_bytes=limit << 20),
        cost_estimate=pl.CostEstimate(flops=flops, bytes_accessed=1 << 20, transcendentals=0),
        name=name,
    )(*args)


def shape(*dims, dtype=BF16):
    return jax.ShapeDtypeStruct(dims, dtype)


def shift_by(step, axis):
    count = lax.axis_size(axis)
    return [(i, (i + step) % count) for i in range(count)]


def mirror(phase, axis):
    count = lax.axis_size(axis)
    return [(i, (i + (1 if i % 2 == phase else -1)) % count) for i in range(count)]


def swap(value, bits):
    count = lax.axis_size("east") * lax.axis_size("north")
    return lax.ppermute(value, BOTH, [(i, i ^ bits) for i in range(count)])


def local(features, occupancy, weight_first, weight_second, cotangent):
    scale = 1.0 / math.sqrt(128 * 128 * 16)
    occupied = occupancy.reshape(1, 2)
    wide = pltpu.VMEM((CH * 8, LN), F32)
    near = pltpu.VMEM((CH, 8, LN), BF16)

    to_west, to_east = call(
        strips_kernel,
        "strips",
        [shape(STRIP, LN), shape(STRIP, LN)],
        [near, near, pltpu.VMEM((1, 2), jnp.int32), wide, wide, pltpu.SemaphoreType.DMA((3,))],
        60,
        1 << 20,
        [pl.BlockSpec(memory_space=pltpu.HBM)] * 3,
        occupied,
        features,
        cotangent,
    )
    west = lax.ppermute(to_east, "east", shift_by(1, "east"))
    east = lax.ppermute(to_west, "east", shift_by(-1, "east"))

    weight = shape(5, TAPS, LN)
    tile = shape(8, LN, LN)
    image = shape(CH, 8, LN)
    planes = shape(8, CH, LN)
    fwd_one, fwd_two, back_two, back_one, turned_one, own_grid, own_cot, feat, cot, own_mask = call(
        prepare_kernel,
        "prepare",
        [weight] * 4 + [shape(288, 1024), tile, tile, planes, planes, shape(16, LN)],
        [wide, wide],
        12,
        1 << 33,
        [VMEM] * 5,
        weight_first,
        weight_second,
        features,
        cotangent,
        occupied,
    )
    first, second = call(
        rims_kernel,
        "rims",
        [shape(RIM, LN), shape(RIM, LN)],
        [],
        8,
        1 << 20,
        [VMEM] * 5,
        west,
        east,
        feat,
        cot,
        own_mask,
    )
    first = lax.ppermute(first, "north", mirror(0, "north"))
    second = lax.ppermute(second, "north", mirror(1, "north"))
    side_grid, side_cot, middle = call(
        sides_kernel,
        "sides",
        [tile, shape(4, LN, LN), shape(3, LN, LN, dtype=F32)],
        [],
        8,
        1 << 31,
        [VMEM] * 3,
        own_mask,
        west,
        east,
    )

    activated, grad_one, masks, keep, send = call(
        lambda *refs: level_kernel(scale, *refs),
        "level",
        [
            image,
            shape(10, 160, LN),
            shape(3, 256, LN, dtype=F32),
            shape(4, 576, LN),
            shape(4, 576, LN),
        ],
        [
            pltpu.VMEM((8, 2, 224, TAPS), BF16),
            pltpu.VMEM((7, 2, 192, TAPS), BF16),
            pltpu.VMEM((6, 2, 160, TAPS), BF16),
            pltpu.VMEM((7 * 224, 2 * LN), F32),
            pltpu.VMEM((6 * 192, 2 * LN), F32),
            pltpu.VMEM((5 * 160, 2 * LN), F32),
            pltpu.VMEM((16, 128, LN), F32),
            pltpu.VMEM((12, 192, LN), F32),
            pltpu.VMEM((10, 160, LN), F32),
            pltpu.VMEM((12, 192, LN), BF16),
            pltpu.VMEM((288, 1024), BF16),
            pltpu.VMEM((2592 + 16, LN), F32),
            pltpu.VMEM((2592 + 16, LN), F32),
            pltpu.VMEM((256 * 24, LN), F32),
            wide,
        ],
        40,
        1 << 34,
        [VMEM] * 11,
        own_grid,
        side_grid,
        own_cot,
        side_cot,
        middle,
        first,
        second,
        fwd_one,
        fwd_two,
        back_two,
        turned_one,
    )

    part = (keep.astype(F32) + swap(send, 1).astype(F32)).astype(BF16)
    others = [swap(part[k], bits) for k, bits in ((2, 12), (1, 192), (3, 204))]
    feature_grad, token = call(
        final_kernel,
        "final",
        [image, shape(8, LN, dtype=F32)],
        [pltpu.VMEM((5, 2, 128, TAPS), BF16), pltpu.VMEM((512, 2 * LN), F32), wide],
        12,
        1 << 32,
        [VMEM] * 3,
        grad_one,
        masks,
        back_one,
    )
    pieces = call(
        gather_kernel,
        "gather",
        [shape(144, LN)] * 4,
        [],
        8,
        1 << 20,
        [VMEM] * 5,
        part[0],
        *others,
        token,
    )
    others = [swap(pieces[k], bits) for k, bits in ((2, 64), (1, 4), (3, 68))]
    held, given = call(
        unpack_kernel,
        "unpack",
        [shape(96, LN), shape(96, LN)],
        [],
        8,
        1 << 20,
        [VMEM] * 4,
        pieces[0],
        *others,
    )
    for partner, size, kind in ((48, 48, BF16), (16, 24, F32)):
        held, given = call(
            step_kernel,
            "step",
            [shape(size, LN, dtype=kind)] * 2,
            [],
            8,
            1 << 20,
            [VMEM] * 2,
            held,
            swap(given, partner),
        )
    one, two = call(
        finish_kernel,
        "finish",
        [shape(8, LN, dtype=F32), shape(8, LN, dtype=F32)],
        [],
        8,
        1 << 20,
        [VMEM] * 2,
        held,
        swap(given, 2),
    )
    return activated, feature_grad, one.reshape(-1)[0:972], two.reshape(-1)[0:972]


def solution(mesh):
    return jax.shard_map(
        local,
        mesh=mesh,
        in_specs=(
            P(None, "east", "north"),
            P("east", "north", None),
            P(),
            P(),
            P(None, "east", "north"),
        ),
        out_specs=(
            P(None, "east", "north"),
            P(None, "east", "north"),
            P(BOTH),
            P(BOTH),
        ),
        check_vma=False,
    )
```

```python
import math

import jax
import jax.numpy as jnp
from jax import lax
from jax.experimental import pallas as pl
from jax.experimental.pallas import tpu as pltpu
from jax.sharding import PartitionSpec as P

BOTH = ("east", "north")
F32 = jnp.float32
BF16 = jnp.bfloat16
CH = 96
LN = 128
TAPS = 7 * LN
WHOLE = (0, 2, 3, 5, 6, 7, 8)
SPLIT = (1, 1, 1, 4, 4, 4)
STRIP = 6 * CH + 16
RIM = 11 * CH + 48
VMEM = pl.BlockSpec(memory_space=pltpu.VMEM)
SMEM = pl.BlockSpec(memory_space=pltpu.SMEM)


def lanes(rows):
    return lax.broadcasted_iota(jnp.int32, (rows, LN), 1)


def flip_pad(value):
    wide = jnp.concatenate(
        [value.astype(F32), jnp.zeros((LN - value.shape[0], value.shape[1]), F32)], axis=0
    )
    return wide.T


def mask_column(ref, row):
    tile = ref[row : row + 16, :].astype(F32)
    return jnp.concatenate([tile] * 8, axis=0).T


def here():
    return lax.axis_index("east"), lax.axis_index("north")


def as_float(flag):
    return flag.astype(jnp.int32).astype(F32)


def neighbours():
    column, row = here()
    last_column, last_row = lax.axis_size("east") - 1, lax.axis_size("north") - 1
    flags = (column > 0, column < last_column, row > 0, row < last_row)
    return [as_float(flag) for flag in flags]


def mask_tile(occupied):
    levels = occupied[...].astype(F32)
    return jnp.where((lanes(16) & 15) < 8, levels[:, 0:1], levels[:, 1:2]).astype(BF16)


def strips_kernel(
    occupied,
    features,
    cotangent,
    to_west,
    to_east,
    near_feat,
    near_cot,
    near_occupied,
    wide_feat,
    wide_cot,
    sems,
):
    copies = [
        pltpu.make_async_copy(features, near_feat, sems.at[0]),
        pltpu.make_async_copy(cotangent, near_cot, sems.at[1]),
        pltpu.make_async_copy(occupied, near_occupied, sems.at[2]),
    ]
    for copy in copies:
        copy.start()
    for copy, near, wide, start, count in (
        (copies[0], near_feat, wide_feat, 0, 4),
        (copies[1], near_cot, wide_cot, 4, 2),
    ):
        copy.wait()
        wide[...] = near[...].astype(F32).reshape(CH * 8, LN)
        for k in range(count):
            rows = slice((start + k) * CH, (start + k + 1) * CH)
            to_west[rows, :] = wide[pl.ds(k, CH, stride=8), :].astype(BF16)
            to_east[rows, :] = wide[pl.ds(8 - count + k, CH, stride=8), :].astype(BF16)
    copies[2].wait()
    mask = mask_tile(near_occupied)
    to_west[6 * CH : STRIP, :] = mask
    to_east[6 * CH : STRIP, :] = mask


def turn_levels(value, x, turned):
    lane = lanes(CH) & 15
    below = jnp.where(lane == 0, 0.0, pltpu.roll(value, 1, 1))
    above = jnp.where(lane == 15, 0.0, pltpu.roll(value, LN - 1, 1))
    start = x * LN if isinstance(x, int) else pl.multiple_of(x * LN, LN)
    for c, moved in enumerate((below, value, above)):
        turned[c * CH : (c + 1) * CH, pl.ds(start, LN)] = moved.astype(BF16)


def prepare_kernel(
    first,
    second,
    features,
    cotangent,
    occupied,
    fwd_one,
    fwd_two,
    back_two,
    back_one,
    turned_one,
    own_grid,
    own_cot,
    feat,
    cot,
    own_mask,
    wide_feat,
    wide_cot,
):
    wide_feat[...] = features[...].astype(F32).reshape(CH * 8, LN)
    wide_cot[...] = cotangent[...].astype(F32).reshape(CH * 8, LN)
    own_mask[...] = mask_tile(occupied)
    for out in (fwd_one, fwd_two, back_two, back_one):
        out[...] = jnp.zeros_like(out)

    def body(plane, carry):
        for source, ahead, back in ((first, fwd_one, back_one), (second, fwd_two, back_two)):
            for k in range(9):
                straight = source[9 * plane + k]
                turned = jnp.pad(
                    source[26 - 9 * plane - k].astype(F32), ((0, LN - CH), (0, LN - CH))
                ).T.astype(BF16)
                if k in WHOLE:
                    row = WHOLE.index(k) * LN
                    ahead[plane + 1, row : row + CH, 0:CH] = straight
                    back[plane + 1, row : row + CH, :] = turned[0:CH]
                else:
                    for q in range(3):
                        row = (SPLIT.index(k) + q) * LN + CH
                        ahead[plane + 1, row : row + 32, 0:CH] = straight[32 * q : 32 * q + 32]
                        back[plane + 1, row : row + 32, :] = turned[32 * q : 32 * q + 32]
        return carry

    lax.fori_loop(0, 3, body, 0)
    mask = jnp.concatenate([own_mask[...].astype(F32)] * 6, axis=0)
    for x in range(8):
        plain = wide_feat[pl.ds(x, CH, stride=8), :]
        feat[x] = plain.astype(BF16)
        value = plain * mask
        turn_levels(value, x, turned_one)
        own_grid[x] = flip_pad(value).astype(BF16)
        plain = wide_cot[pl.ds(x, CH, stride=8), :]
        cot[x] = plain.astype(BF16)
        own_cot[x] = flip_pad(plain).astype(BF16)


def rims_kernel(west, east, feat, cot, own_mask, to_south, to_north):
    half = lanes(CH) < 64
    quarter = lanes(CH) // 32

    def feat_plane(p):
        if p < 4:
            return west[p * CH : (p + 1) * CH, :].astype(F32)
        if p < 12:
            return feat[p - 4].astype(F32)
        return east[(p - 12) * CH : (p - 11) * CH, :].astype(F32)

    def cot_plane(p):
        if p < 2:
            return west[(4 + p) * CH : (5 + p) * CH, :].astype(F32)
        if p < 10:
            return cot[p - 2].astype(F32)
        return east[(p - 6) * CH : (p - 5) * CH, :].astype(F32)

    for k in range(8):
        one, two = feat_plane(k), feat_plane(k + 8)
        rows = slice(k * CH, (k + 1) * CH)
        to_south[rows, :] = jnp.where(half, one, pltpu.roll(two, 64, 1)).astype(BF16)
        to_north[rows, :] = jnp.where(half, pltpu.roll(one, 64, 1), two).astype(BF16)
    for k in range(3):
        four = [cot_plane(k + 3 * q) for q in range(4)]
        rows = slice((8 + k) * CH, (9 + k) * CH)
        for out, shift in ((to_south, 0), (to_north, 32)):
            moved = [
                pltpu.roll(four[q], (32 * q + shift) % LN, 1) if (32 * q + shift) % LN else four[q]
                for q in range(4)
            ]
            packed = jnp.where(
                quarter < 2,
                jnp.where(quarter == 0, moved[0], moved[1]),
                jnp.where(quarter == 2, moved[2], moved[3]),
            )
            out[rows, :] = packed.astype(BF16)
    for out in (to_south, to_north):
        out[11 * CH : 11 * CH + 16, :] = west[6 * CH : STRIP, :]
        out[11 * CH + 16 : 11 * CH + 32, :] = own_mask[...]
        out[11 * CH + 32 : RIM, :] = east[6 * CH : STRIP, :]


def sides_kernel(own_mask, west, east, side_grid, side_cot, middle):
    has = neighbours()
    middle[0] = mask_column(west, 6 * CH) * has[0]
    middle[1] = mask_column(own_mask, 0)
    middle[2] = mask_column(east, 6 * CH) * has[1]
    for side, ref in ((0, west), (1, east)):
        for k in range(4):
            block = flip_pad(ref[k * CH : (k + 1) * CH, :]) * middle[2 * side]
            side_grid[4 * side + k] = block.astype(BF16)
        for k in range(2):
            side_cot[2 * side + k] = flip_pad(ref[(4 + k) * CH : (5 + k) * CH, :]).astype(BF16)


def spread(taps, plane, value, rows, first=0):
    count = rows + 32
    level = lax.broadcasted_iota(jnp.int32, (count, LN), 0) & 15
    below = jnp.where(level == 0, 0.0, pltpu.roll(value, 1, 0))
    above = jnp.where(level == 15, 0.0, pltpu.roll(value, count - 1, 0))
    spare = lanes(count) >= CH
    short = [moved.astype(BF16) for moved in (below, value, above)]
    rest = [
        jnp.where(spare, pltpu.roll(short[1], CH - 32 * q, 1), jnp.bfloat16(0)) for q in range(3)
    ]
    for n, k in enumerate(WHOLE):
        start = 16 * (k // 3)
        block = short[k % 3][start : start + rows]
        if n < 6:
            start = 16 * (SPLIT[n] // 3)
            block = block + rest[n % 3][start : start + rows]
        taps[plane // 2, plane % 2, first : first + rows, n * LN : (n + 1) * LN] = block


def convolve(taps, weight, total, pair, rows):
    left = jnp.concatenate(
        [taps[pair + j // 2, j % 2, 0:rows, :] for j in range(4)], axis=1
    )
    right = jnp.concatenate(
        [jnp.concatenate([weight[j + 1], weight[j]], axis=1) for j in range(4)], axis=0
    )
    total[pair * rows : (pair + 1) * rows, :] = jnp.dot(left, right, preferred_element_type=F32)


def half_of(total, p, rows):
    start = p % 2 * LN
    return total[p // 2 * rows : (p // 2 + 1) * rows, start : start + LN]


HOPS = (1, 12, 192, 64, 4, 48, 16, 2)


def path(code):
    mask = 0
    for k, hop in enumerate(HOPS):
        if code >> (7 - k) & 1:
            mask ^= hop
    return mask


def kernel_grad(turned, planes, shift, scale, result):
    def piece(k):
        a, b = k // 3, k % 3
        start = (shift + 1 - b) * 16
        return planes[shift + 1 - a : shift + 9 - a, start : start + 128, :].reshape(1024, LN)

    for k in range(0, 9, 2):
        right = jnp.concatenate([piece(k), piece(min(k + 1, 8))], axis=1)
        part = jnp.dot(turned[...], right, preferred_element_type=F32) * scale
        result[k * 288 : k * 288 + 288, :] = part[:, 0:LN]
        if k < 8:
            result[(k + 1) * 288 : (k + 1) * 288 + 288, :] = part[:, LN : 2 * LN]


def band(p, low, high):
    return int(p >= low) + int(p >= high)


def silu_parts(value):
    sigma = jax.nn.sigmoid(value)
    return (value * sigma).astype(BF16), sigma * (1.0 + value * (1.0 - sigma))


def inner_kernel(own_grid, side_grid, middle, fwd_one, hidden, slope, taps, total):
    for p in range(16):
        value = own_grid[p - 4] if 4 <= p < 12 else side_grid[p % 8]
        spread(taps, p, value.astype(F32), 96)
    left = jnp.concatenate(
        [taps[j // 2 : j // 2 + 7, j % 2, :, :].reshape(672, TAPS) for j in range(4)], axis=1
    )
    right = jnp.concatenate(
        [jnp.concatenate([fwd_one[j + 1], fwd_one[j]], axis=1) for j in range(4)], axis=0
    )
    total[...] = jnp.dot(left, right, preferred_element_type=F32)
    for p in range(14):
        parts = silu_parts(half_of(total, p, 96) * middle[band(p, 3, 11), 16:112, :])
        hidden[p] = parts[0]
        if 2 <= p < 12:
            slope[p - 2] = parts[1]


def level_kernel(
    scale,
    own_grid,
    side_grid,
    own_cot,
    side_cot,
    middle,
    south,
    north,
    fwd_one,
    fwd_two,
    back_two,
    turned_one,
    inner_hidden,
    inner_slope,
    activated,
    grad_one,
    masks,
    keep,
    send,
    taps_one,
    taps_two,
    taps_three,
    total_one,
    total_two,
    total_three,
    edge,
    upstream,
    slope_one,
    grad_two,
    turned_two,
    grad_one_sum,
    grad_two_sum,
    packed,
    rows,
):
    has = neighbours()
    for ref, flag, row in ((south, has[2], 0), (north, has[3], 192)):
        tile = ref[11 * CH : 11 * CH + 48, :].astype(F32) * flag
        turned = jnp.concatenate([tile, jnp.zeros((80, LN), F32)], axis=0).T[0:64]
        for bx in range(3):
            side = has[bx // 2] if bx != 1 else 1.0
            column = turned[:, 16 * bx : 16 * bx + 1] * side
            masks[bx, row : row + 64, :] = jnp.broadcast_to(column, (64, LN))
    masks[:, 64:192, :] = middle[...]

    for k in range(8):
        for ref, row in ((south, 0), (north, 64)):
            both = flip_pad(ref[k * CH : (k + 1) * CH, :])
            edge[k, row : row + 64, :] = both[0:64]
            edge[k + 8, row : row + 64, :] = both[64:128]
    for k in range(3):
        for ref, row in ((south, 0), (north, 160)):
            four = flip_pad(ref[(8 + k) * CH : (9 + k) * CH, :])
            for q in range(4):
                upstream[k + 3 * q, row : row + 32, :] = four[32 * q : 32 * q + 32]
    for k in range(2):
        upstream[k, 32:160, :] = side_cot[k].astype(F32)
        upstream[10 + k, 32:160, :] = side_cot[2 + k].astype(F32)
    for k in range(8):
        upstream[2 + k, 32:160, :] = own_cot[k].astype(F32)

    def begin(p):
        bx = band(p, 4, 12)
        value = own_grid[p - 4] if bx == 1 else side_grid[p % 8]
        low = edge[p, 0:64, :] * masks[bx, 0:64, :]
        high = edge[p, 64:128, :] * masks[bx, 192:256, :]
        value = value.astype(F32)
        spread(taps_one, p, jnp.concatenate([low, value[0:32]], axis=0), 64)
        spread(taps_one, p, jnp.concatenate([value[96:128], high], axis=0), 64, 64)

    def after_one(p):
        bx = band(p, 3, 11)
        mask = jnp.concatenate([masks[bx, 16:80, :], masks[bx, 176:240, :]], axis=0)
        hidden, slope = silu_parts(half_of(total_one, p, 128) * mask)
        if 2 <= p < 12:
            slope_one[p - 2, 0:32, :] = slope[32:64]
            slope_one[p - 2, 32:128, :] = inner_slope[p - 2]
            slope_one[p - 2, 128:160, :] = slope[64:96]
        hidden = jnp.concatenate([hidden[0:64], inner_hidden[p], hidden[64:128]], axis=0)
        hidden = hidden.astype(F32)
        spread(taps_two, p, hidden, 192)
        if 3 <= p < 11:
            turn_levels(hidden[48:176].T[0:CH], p - 3, turned_two)

    def after_two(p):
        mask = masks[band(p, 2, 10), 32:224, :]
        value = half_of(total_two, p, 192) * mask
        sigma = jax.nn.sigmoid(value)
        if 2 <= p < 10:
            rows[pl.ds(p - 2, CH, stride=8), :] = (value * sigma)[32:160].T[0:CH]
        slope = sigma * (1.0 + value * (1.0 - sigma))
        grad = upstream[p] * slope * mask
        grad_two[p] = grad.astype(BF16)
        spread(taps_three, p, grad, 160)

    def after_three(p):
        grad = half_of(total_three, p, 160) * slope_one[p] * masks[band(p, 1, 9), 48:208, :]
        grad_one[p] = grad.astype(BF16)

    for p in range(4):
        begin(p)
    for t in range(12):
        if t < 7:
            convolve(taps_one, fwd_one, total_one, t, 128)
        if t < 6:
            begin(2 * t + 4)
            begin(2 * t + 5)
        if 1 <= t < 8:
            after_one(2 * t - 2)
            after_one(2 * t - 1)
        if 3 <= t < 9:
            convolve(taps_two, fwd_two, total_two, t - 3, 192)
        if 4 <= t < 10:
            after_two(2 * t - 8)
            after_two(2 * t - 7)
        if 6 <= t < 11:
            convolve(taps_three, back_two, total_three, t - 6, 160)
        if 7 <= t < 12:
            after_three(2 * t - 14)
            after_three(2 * t - 13)
        if t == 10:
            kernel_grad(turned_two, grad_two, 2, scale, grad_two_sum)
    activated[...] = rows[...].reshape(CH, 8, LN).astype(BF16)
    kernel_grad(turned_one, grad_one, 1, scale, grad_one_sum)

    column, row = here()
    position = column * 16 + row
    spare = lanes(48) >= CH
    for grad, source in ((1, grad_two_sum), (0, grad_one_sum)):
        for code in range(256):
            owner = jnp.bitwise_xor(position, path(code))
            start = 81 * (owner >> 3) + 10 * (owner & 7)
            packed[24 * code + 12 * grad : 24 * code + 12 * grad + 12, :] = source[
                pl.ds(start, 12), :
            ]
    for code in range(0, 256, 8):
        block = [packed[24 * code + 48 * k : 24 * code + 48 * k + 48, :] for k in range(4)]
        out = keep if code < 128 else send
        first = 144 * (code // 8 % 4)
        for k in range(3):
            mixed = jnp.where(spare, pltpu.roll(block[3], CH - 32 * k, 1), block[k])
            out[code // 32 % 4, first + 48 * k : first + 48 * k + 48, :] = mixed.astype(BF16)


def final_kernel(grad_one, masks, back_one, feature_grad, token, taps, total, rows):
    token[...] = jnp.zeros_like(token)
    for p in range(10):
        spread(taps, p, grad_one[p].astype(F32), 128)

    def after_four(p):
        value = half_of(total, p, 128)
        rows[pl.ds(p, CH, stride=8), :] = (value * masks[1, 64:192, :]).T[0:CH]

    for t in range(5):
        if t < 4:
            convolve(taps, back_one, total, t, 128)
        if t > 0:
            after_four(2 * t - 2)
            after_four(2 * t - 1)
    feature_grad[...] = rows[...].reshape(CH, 8, LN).astype(BF16)


def gather_kernel(a0, a1, a2, a3, token, *outs):
    for k, out in enumerate(outs):
        piece = slice(144 * k, 144 * k + 144)
        out[...] = sum(ref[piece, :].astype(F32) for ref in (a0, a1, a2, a3)).astype(BF16)


def unpack_kernel(a0, a1, a2, a3, hold, give):
    lane = lanes(48)
    a, b, c = (
        sum(ref[48 * k : 48 * k + 48, :].astype(F32) for ref in (a0, a1, a2, a3))
        for k in range(3)
    )
    last = jnp.where(
        lane < 32,
        pltpu.roll(a, 32, 1),
        jnp.where(lane < 64, pltpu.roll(b, 64, 1), pltpu.roll(c, 96, 1)),
    )
    for out, pair in ((hold, (a, b)), (give, (c, last))):
        out[...] = jnp.concatenate(pair, axis=0).astype(BF16)


def step_kernel(held, got, hold, give):
    size = hold.shape[0]
    total = held[...].astype(F32) + got[...].astype(F32)
    hold[...] = total[0:size].astype(hold.dtype)
    give[...] = total[size : 2 * size].astype(give.dtype)


def finish_kernel(held, got, out_one, out_two):
    j = lax.axis_index("north") & 7
    lane = lanes(1)
    value = held[...] + got[...]
    for grad, out in ((0, out_one), (1, out_two)):
        flat = []
        for m in range(3):
            r = [value[12 * grad + 4 * m + q : 12 * grad + 4 * m + q + 1] for q in range(4)]
            flat.append(jnp.where(lane < 96, r[0], pltpu.roll(r[1], 96, 1)))
            flat.append(jnp.where(lane < 64, pltpu.roll(r[1], 96, 1), pltpu.roll(r[2], 64, 1)))
            flat.append(jnp.where(lane < 32, pltpu.roll(r[2], 64, 1), pltpu.roll(r[3], 32, 1)))
        low = jnp.concatenate(flat[0:8], axis=0)
        high = jnp.concatenate(flat[1:9], axis=0)
        turn = lax.rem(LN - 12 * j, LN)
        out[...] = jnp.where(
            lanes(8) < LN - 12 * j, pltpu.roll(low, turn, 1), pltpu.roll(high, turn, 1)
        )


def call(kernel, name, outs, scratch, limit, flops, specs, *args):
    return pl.pallas_call(
        kernel,
        out_shape=outs,
        in_specs=specs,
        out_specs=[VMEM] * len(outs),
        scratch_shapes=scratch,
        compiler_params=pltpu.CompilerParams(vmem_limit_bytes=limit << 20),
        cost_estimate=pl.CostEstimate(flops=flops, bytes_accessed=1 << 20, transcendentals=0),
        name=name,
    )(*args)


def shape(*dims, dtype=BF16):
    return jax.ShapeDtypeStruct(dims, dtype)


def shift_by(step, axis):
    count = lax.axis_size(axis)
    return [(i, (i + step) % count) for i in range(count)]


def swap(value, bits):
    count = lax.axis_size("east") * lax.axis_size("north")
    return lax.ppermute(value, BOTH, [(i, i ^ bits) for i in range(count)])


def local(features, occupancy, weight_first, weight_second, cotangent):
    scale = 1.0 / math.sqrt(128 * 128 * 16)
    occupied = occupancy.reshape(1, 2)
    wide = pltpu.VMEM((CH * 8, LN), F32)
    near = pltpu.VMEM((CH, 8, LN), BF16)

    to_west, to_east = call(
        strips_kernel,
        "strips",
        [shape(STRIP, LN), shape(STRIP, LN)],
        [near, near, pltpu.VMEM((1, 2), jnp.int32), wide, wide, pltpu.SemaphoreType.DMA((3,))],
        60,
        1 << 20,
        [pl.BlockSpec(memory_space=pltpu.HBM)] * 3,
        occupied,
        features,
        cotangent,
    )
    west = lax.ppermute(to_east, "east", shift_by(1, "east"))
    east = lax.ppermute(to_west, "east", shift_by(-1, "east"))

    weight = shape(5, TAPS, LN)
    tile = shape(8, LN, LN)
    image = shape(CH, 8, LN)
    planes = shape(8, CH, LN)
    fwd_one, fwd_two, back_two, back_one, turned_one, own_grid, own_cot, feat, cot, own_mask = call(
        prepare_kernel,
        "prepare",
        [weight] * 4 + [shape(288, 1024), tile, tile, planes, planes, shape(16, LN)],
        [wide, wide],
        12,
        1 << 33,
        [VMEM] * 5,
        weight_first,
        weight_second,
        features,
        cotangent,
        occupied,
    )
    to_south, to_north = call(
        rims_kernel,
        "rims",
        [shape(RIM, LN), shape(RIM, LN)],
        [],
        8,
        1 << 20,
        [VMEM] * 5,
        west,
        east,
        feat,
        cot,
        own_mask,
    )
    south = lax.ppermute(to_north, "north", shift_by(1, "north"))
    north = lax.ppermute(to_south, "north", shift_by(-1, "north"))
    side_grid, side_cot, middle = call(
        sides_kernel,
        "sides",
        [tile, shape(4, LN, LN), shape(3, LN, LN, dtype=F32)],
        [],
        8,
        1 << 31,
        [VMEM] * 3,
        own_mask,
        west,
        east,
    )

    inner_hidden, inner_slope = call(
        inner_kernel,
        "inner",
        [shape(14, 96, LN), shape(10, 96, LN, dtype=F32)],
        [pltpu.VMEM((8, 2, 96, TAPS), BF16), pltpu.VMEM((672, 2 * LN), F32)],
        16,
        1 << 32,
        [VMEM] * 4,
        own_grid,
        side_grid,
        middle,
        fwd_one,
    )
    activated, grad_one, masks, keep, send = call(
        lambda *refs: level_kernel(scale, *refs),
        "level",
        [
            image,
            shape(10, 160, LN),
            shape(3, 256, LN, dtype=F32),
            shape(4, 576, LN),
            shape(4, 576, LN),
        ],
        [
            pltpu.VMEM((8, 2, 128, TAPS), BF16),
            pltpu.VMEM((7, 2, 192, TAPS), BF16),
            pltpu.VMEM((6, 2, 160, TAPS), BF16),
            pltpu.VMEM((7 * 128, 2 * LN), F32),
            pltpu.VMEM((6 * 192, 2 * LN), F32),
            pltpu.VMEM((5 * 160, 2 * LN), F32),
            pltpu.VMEM((16, 128, LN), F32),
            pltpu.VMEM((12, 192, LN), F32),
            pltpu.VMEM((10, 160, LN), F32),
            pltpu.VMEM((12, 192, LN), BF16),
            pltpu.VMEM((288, 1024), BF16),
            pltpu.VMEM((2592 + 16, LN), F32),
            pltpu.VMEM((2592 + 16, LN), F32),
            pltpu.VMEM((256 * 24, LN), F32),
            wide,
        ],
        40,
        1 << 34,
        [VMEM] * 13,
        own_grid,
        side_grid,
        own_cot,
        side_cot,
        middle,
        south,
        north,
        fwd_one,
        fwd_two,
        back_two,
        turned_one,
        inner_hidden,
        inner_slope,
    )

    part = (keep.astype(F32) + swap(send, 1).astype(F32)).astype(BF16)
    others = [swap(part[k], bits) for k, bits in ((2, 12), (1, 192), (3, 204))]
    feature_grad, token = call(
        final_kernel,
        "final",
        [image, shape(8, LN, dtype=F32)],
        [pltpu.VMEM((5, 2, 128, TAPS), BF16), pltpu.VMEM((512, 2 * LN), F32), wide],
        12,
        1 << 32,
        [VMEM] * 3,
        grad_one,
        masks,
        back_one,
    )
    pieces = call(
        gather_kernel,
        "gather",
        [shape(144, LN)] * 4,
        [],
        8,
        1 << 20,
        [VMEM] * 5,
        part[0],
        *others,
        token,
    )
    others = [swap(pieces[k], bits) for k, bits in ((2, 64), (1, 4), (3, 68))]
    held, given = call(
        unpack_kernel,
        "unpack",
        [shape(96, LN), shape(96, LN)],
        [],
        8,
        1 << 20,
        [VMEM] * 4,
        pieces[0],
        *others,
    )
    for partner, size, kind in ((48, 48, BF16), (16, 24, F32)):
        held, given = call(
            step_kernel,
            "step",
            [shape(size, LN, dtype=kind)] * 2,
            [],
            8,
            1 << 20,
            [VMEM] * 2,
            held,
            swap(given, partner),
        )
    one, two = call(
        finish_kernel,
        "finish",
        [shape(8, LN, dtype=F32), shape(8, LN, dtype=F32)],
        [],
        8,
        1 << 20,
        [VMEM] * 2,
        held,
        swap(given, 2),
    )
    return activated, feature_grad, one.reshape(-1)[0:972], two.reshape(-1)[0:972]


def solution(mesh):
    return jax.shard_map(
        local,
        mesh=mesh,
        in_specs=(
            P(None, "east", "north"),
            P("east", "north", None),
            P(),
            P(),
            P(None, "east", "north"),
        ),
        out_specs=(
            P(None, "east", "north"),
            P(None, "east", "north"),
            P(BOTH),
            P(BOTH),
        ),
        check_vma=False,
    )
```

```python
import math

import jax
import jax.numpy as jnp
from jax import lax
from jax.experimental import pallas as pl
from jax.experimental.pallas import tpu as pltpu
from jax.sharding import PartitionSpec as P

BOTH = ("east", "north")
F32 = jnp.float32
BF16 = jnp.bfloat16
CH = 96
LN = 128
TAPS = 7 * LN
WHOLE = (0, 2, 3, 5, 6, 7, 8)
SPLIT = (1, 1, 1, 4, 4, 4)
STRIP = 6 * CH + 16
RIM = 11 * CH + 48
VMEM = pl.BlockSpec(memory_space=pltpu.VMEM)
SMEM = pl.BlockSpec(memory_space=pltpu.SMEM)


def lanes(rows):
    return lax.broadcasted_iota(jnp.int32, (rows, LN), 1)


def flip_pad(value):
    wide = jnp.concatenate(
        [value.astype(F32), jnp.zeros((LN - value.shape[0], value.shape[1]), F32)], axis=0
    )
    return wide.T


def mask_column(ref, row):
    tile = ref[row : row + 16, :].astype(F32)
    return jnp.concatenate([tile] * 8, axis=0).T


def here():
    return lax.axis_index("east"), lax.axis_index("north")


def as_float(flag):
    return flag.astype(jnp.int32).astype(F32)


def neighbours():
    column, row = here()
    last_column, last_row = lax.axis_size("east") - 1, lax.axis_size("north") - 1
    flags = (column > 0, column < last_column, row > 0, row < last_row)
    return [as_float(flag) for flag in flags]


def mask_tile(occupied):
    levels = occupied[...].astype(F32)
    return jnp.where((lanes(16) & 15) < 8, levels[:, 0:1], levels[:, 1:2]).astype(BF16)


def strips_kernel(
    occupied,
    features,
    cotangent,
    to_west,
    to_east,
    near_feat,
    near_cot,
    near_occupied,
    wide_feat,
    wide_cot,
    sems,
):
    copies = [
        pltpu.make_async_copy(features, near_feat, sems.at[0]),
        pltpu.make_async_copy(cotangent, near_cot, sems.at[1]),
        pltpu.make_async_copy(occupied, near_occupied, sems.at[2]),
    ]
    for copy in copies:
        copy.start()
    for copy, near, wide, start, count in (
        (copies[0], near_feat, wide_feat, 0, 4),
        (copies[1], near_cot, wide_cot, 4, 2),
    ):
        copy.wait()
        wide[...] = near[...].astype(F32).reshape(CH * 8, LN)
        for k in range(count):
            rows = slice((start + k) * CH, (start + k + 1) * CH)
            to_west[rows, :] = wide[pl.ds(k, CH, stride=8), :].astype(BF16)
            to_east[rows, :] = wide[pl.ds(8 - count + k, CH, stride=8), :].astype(BF16)
    copies[2].wait()
    mask = mask_tile(near_occupied)
    to_west[6 * CH : STRIP, :] = mask
    to_east[6 * CH : STRIP, :] = mask


def turn_levels(value, x, turned):
    lane = lanes(CH) & 15
    below = jnp.where(lane == 0, 0.0, pltpu.roll(value, 1, 1))
    above = jnp.where(lane == 15, 0.0, pltpu.roll(value, LN - 1, 1))
    start = x * LN if isinstance(x, int) else pl.multiple_of(x * LN, LN)
    for c, moved in enumerate((below, value, above)):
        turned[c * CH : (c + 1) * CH, pl.ds(start, LN)] = moved.astype(BF16)


def pack_weights(source, ahead, back):
    for out in (ahead, back):
        out[...] = jnp.zeros_like(out)

    def body(plane, carry):
        for k in range(9):
            straight = source[9 * plane + k]
            turned = jnp.pad(
                source[26 - 9 * plane - k].astype(F32), ((0, LN - CH), (0, LN - CH))
            ).T.astype(BF16)
            if k in WHOLE:
                row = WHOLE.index(k) * LN
                ahead[plane + 1, row : row + CH, 0:CH] = straight
                back[plane + 1, row : row + CH, :] = turned[0:CH]
            else:
                for q in range(3):
                    row = (SPLIT.index(k) + q) * LN + CH
                    ahead[plane + 1, row : row + 32, 0:CH] = straight[32 * q : 32 * q + 32]
                    back[plane + 1, row : row + 32, :] = turned[32 * q : 32 * q + 32]
        return carry

    lax.fori_loop(0, 3, body, 0)


def prepare_kernel(
    weight,
    features,
    cotangent,
    occupied,
    ahead,
    back,
    turned_one,
    own_grid,
    feat,
    cot,
    own_mask,
    wide_feat,
    wide_cot,
):
    wide_feat[...] = features[...].astype(F32).reshape(CH * 8, LN)
    wide_cot[...] = cotangent[...].astype(F32).reshape(CH * 8, LN)
    own_mask[...] = mask_tile(occupied)
    pack_weights(weight, ahead, back)
    mask = jnp.concatenate([own_mask[...].astype(F32)] * 6, axis=0)
    for x in range(8):
        plain = wide_feat[pl.ds(x, CH, stride=8), :]
        feat[x] = plain.astype(BF16)
        value = plain * mask
        turn_levels(value, x, turned_one)
        own_grid[x] = flip_pad(value).astype(BF16)
        cot[x] = wide_cot[pl.ds(x, CH, stride=8), :].astype(BF16)


def second_kernel(weight, cot, middle, ahead, back, own_cot):
    pack_weights(weight, ahead, back)
    for x in range(8):
        own_cot[x] = flip_pad(cot[x]).astype(BF16)


def rims_kernel(west, east, feat, cot, own_mask, to_south, to_north):
    half = lanes(CH) < 64
    quarter = lanes(CH) // 32

    def feat_plane(p):
        if p < 4:
            return west[p * CH : (p + 1) * CH, :].astype(F32)
        if p < 12:
            return feat[p - 4].astype(F32)
        return east[(p - 12) * CH : (p - 11) * CH, :].astype(F32)

    def cot_plane(p):
        if p < 2:
            return west[(4 + p) * CH : (5 + p) * CH, :].astype(F32)
        if p < 10:
            return cot[p - 2].astype(F32)
        return east[(p - 6) * CH : (p - 5) * CH, :].astype(F32)

    for k in range(8):
        one, two = feat_plane(k), feat_plane(k + 8)
        rows = slice(k * CH, (k + 1) * CH)
        to_south[rows, :] = jnp.where(half, one, pltpu.roll(two, 64, 1)).astype(BF16)
        to_north[rows, :] = jnp.where(half, pltpu.roll(one, 64, 1), two).astype(BF16)
    for k in range(3):
        four = [cot_plane(k + 3 * q) for q in range(4)]
        rows = slice((8 + k) * CH, (9 + k) * CH)
        for out, shift in ((to_south, 0), (to_north, 32)):
            moved = [
                pltpu.roll(four[q], (32 * q + shift) % LN, 1) if (32 * q + shift) % LN else four[q]
                for q in range(4)
            ]
            packed = jnp.where(
                quarter < 2,
                jnp.where(quarter == 0, moved[0], moved[1]),
                jnp.where(quarter == 2, moved[2], moved[3]),
            )
            out[rows, :] = packed.astype(BF16)
    for out in (to_south, to_north):
        out[11 * CH : 11 * CH + 16, :] = west[6 * CH : STRIP, :]
        out[11 * CH + 16 : 11 * CH + 32, :] = own_mask[...]
        out[11 * CH + 32 : RIM, :] = east[6 * CH : STRIP, :]


def sides_kernel(own_mask, west, east, side_grid, side_cot, middle):
    has = neighbours()
    middle[0] = mask_column(west, 6 * CH) * has[0]
    middle[1] = mask_column(own_mask, 0)
    middle[2] = mask_column(east, 6 * CH) * has[1]
    for side, ref in ((0, west), (1, east)):
        for k in range(4):
            block = flip_pad(ref[k * CH : (k + 1) * CH, :]) * middle[2 * side]
            side_grid[4 * side + k] = block.astype(BF16)
        for k in range(2):
            side_cot[2 * side + k] = flip_pad(ref[(4 + k) * CH : (5 + k) * CH, :]).astype(BF16)


def spread(taps, plane, value, rows, first=0):
    count = rows + 32
    level = lax.broadcasted_iota(jnp.int32, (count, LN), 0) & 15
    below = jnp.where(level == 0, 0.0, pltpu.roll(value, 1, 0))
    above = jnp.where(level == 15, 0.0, pltpu.roll(value, count - 1, 0))
    spare = lanes(count) >= CH
    short = [moved.astype(BF16) for moved in (below, value, above)]
    rest = [
        jnp.where(spare, pltpu.roll(short[1], CH - 32 * q, 1), jnp.bfloat16(0)) for q in range(3)
    ]
    for n, k in enumerate(WHOLE):
        start = 16 * (k // 3)
        block = short[k % 3][start : start + rows]
        if n < 6:
            start = 16 * (SPLIT[n] // 3)
            block = block + rest[n % 3][start : start + rows]
        taps[plane // 2, plane % 2, first : first + rows, n * LN : (n + 1) * LN] = block


def convolve(taps, weight, total, pair, rows):
    left = jnp.concatenate(
        [taps[pair + j // 2, j % 2, 0:rows, :] for j in range(4)], axis=1
    )
    right = jnp.concatenate(
        [jnp.concatenate([weight[j + 1], weight[j]], axis=1) for j in range(4)], axis=0
    )
    total[pair * rows : (pair + 1) * rows, :] = jnp.dot(left, right, preferred_element_type=F32)


def half_of(total, p, rows):
    start = p % 2 * LN
    return total[p // 2 * rows : (p // 2 + 1) * rows, start : start + LN]


HOPS = (1, 12, 192, 64, 4, 48, 16, 2)


def path(code):
    mask = 0
    for k, hop in enumerate(HOPS):
        if code >> (7 - k) & 1:
            mask ^= hop
    return mask


def kernel_grad(turned, planes, shift, scale, result):
    def piece(k):
        a, b = k // 3, k % 3
        start = (shift + 1 - b) * 16
        return planes[shift + 1 - a : shift + 9 - a, start : start + 128, :].reshape(1024, LN)

    for k in range(0, 9, 2):
        right = jnp.concatenate([piece(k), piece(min(k + 1, 8))], axis=1)
        part = jnp.dot(turned[...], right, preferred_element_type=F32) * scale
        result[k * 288 : k * 288 + 288, :] = part[:, 0:LN]
        if k < 8:
            result[(k + 1) * 288 : (k + 1) * 288 + 288, :] = part[:, LN : 2 * LN]


def band(p, low, high):
    return int(p >= low) + int(p >= high)


def silu_parts(value):
    sigma = jax.nn.sigmoid(value)
    return (value * sigma).astype(BF16), sigma * (1.0 + value * (1.0 - sigma))


def inner_kernel(own_grid, side_grid, middle, fwd_one, hidden, slope, taps, total):
    for p in range(16):
        value = own_grid[p - 4] if 4 <= p < 12 else side_grid[p % 8]
        spread(taps, p, value.astype(F32), 96)
    left = jnp.concatenate(
        [taps[j // 2 : j // 2 + 7, j % 2, :, :].reshape(672, TAPS) for j in range(4)], axis=1
    )
    right = jnp.concatenate(
        [jnp.concatenate([fwd_one[j + 1], fwd_one[j]], axis=1) for j in range(4)], axis=0
    )
    total[...] = jnp.dot(left, right, preferred_element_type=F32)
    for p in range(14):
        parts = silu_parts(half_of(total, p, 96) * middle[band(p, 3, 11), 16:112, :])
        hidden[p] = parts[0]
        if 2 <= p < 12:
            slope[p - 2] = parts[1]


def level_kernel(
    scale,
    own_grid,
    side_grid,
    own_cot,
    side_cot,
    middle,
    south,
    north,
    fwd_one,
    fwd_two,
    back_two,
    turned_one,
    inner_hidden,
    inner_slope,
    activated,
    grad_one,
    masks,
    keep,
    send,
    taps_one,
    taps_two,
    taps_three,
    total_one,
    total_two,
    total_three,
    edge,
    upstream,
    slope_one,
    grad_two,
    turned_two,
    grad_one_sum,
    grad_two_sum,
    packed,
    rows,
):
    has = neighbours()
    for ref, flag, row in ((south, has[2], 0), (north, has[3], 192)):
        tile = ref[11 * CH : 11 * CH + 48, :].astype(F32) * flag
        turned = jnp.concatenate([tile, jnp.zeros((80, LN), F32)], axis=0).T[0:64]
        for bx in range(3):
            side = has[bx // 2] if bx != 1 else 1.0
            column = turned[:, 16 * bx : 16 * bx + 1] * side
            masks[bx, row : row + 64, :] = jnp.broadcast_to(column, (64, LN))
    masks[:, 64:192, :] = middle[...]

    for k in range(8):
        for ref, row in ((south, 0), (north, 64)):
            both = flip_pad(ref[k * CH : (k + 1) * CH, :])
            edge[k, row : row + 64, :] = both[0:64]
            edge[k + 8, row : row + 64, :] = both[64:128]
    for k in range(3):
        for ref, row in ((south, 0), (north, 160)):
            four = flip_pad(ref[(8 + k) * CH : (9 + k) * CH, :])
            for q in range(4):
                upstream[k + 3 * q, row : row + 32, :] = four[32 * q : 32 * q + 32]
    for k in range(2):
        upstream[k, 32:160, :] = side_cot[k].astype(F32)
        upstream[10 + k, 32:160, :] = side_cot[2 + k].astype(F32)
    for k in range(8):
        upstream[2 + k, 32:160, :] = own_cot[k].astype(F32)

    def begin(p):
        bx = band(p, 4, 12)
        value = own_grid[p - 4] if bx == 1 else side_grid[p % 8]
        low = edge[p, 0:64, :] * masks[bx, 0:64, :]
        high = edge[p, 64:128, :] * masks[bx, 192:256, :]
        value = value.astype(F32)
        spread(taps_one, p, jnp.concatenate([low, value[0:32]], axis=0), 64)
        spread(taps_one, p, jnp.concatenate([value[96:128], high], axis=0), 64, 64)

    def after_one(p):
        bx = band(p, 3, 11)
        mask = jnp.concatenate([masks[bx, 16:80, :], masks[bx, 176:240, :]], axis=0)
        hidden, slope = silu_parts(half_of(total_one, p, 128) * mask)
        if 2 <= p < 12:
            slope_one[p - 2, 0:32, :] = slope[32:64]
            slope_one[p - 2, 32:128, :] = inner_slope[p - 2]
            slope_one[p - 2, 128:160, :] = slope[64:96]
        hidden = jnp.concatenate([hidden[0:64], inner_hidden[p], hidden[64:128]], axis=0)
        hidden = hidden.astype(F32)
        spread(taps_two, p, hidden, 192)
        if 3 <= p < 11:
            turn_levels(hidden[48:176].T[0:CH], p - 3, turned_two)

    def after_two(p):
        mask = masks[band(p, 2, 10), 32:224, :]
        value = half_of(total_two, p, 192) * mask
        sigma = jax.nn.sigmoid(value)
        if 2 <= p < 10:
            rows[pl.ds(p - 2, CH, stride=8), :] = (value * sigma)[32:160].T[0:CH]
        slope = sigma * (1.0 + value * (1.0 - sigma))
        grad = upstream[p] * slope * mask
        grad_two[p] = grad.astype(BF16)
        spread(taps_three, p, grad, 160)

    def after_three(p):
        grad = half_of(total_three, p, 160) * slope_one[p] * masks[band(p, 1, 9), 48:208, :]
        grad_one[p] = grad.astype(BF16)

    for p in range(4):
        begin(p)
    for t in range(12):
        if t < 7:
            convolve(taps_one, fwd_one, total_one, t, 128)
        if t < 6:
            begin(2 * t + 4)
            begin(2 * t + 5)
        if 1 <= t < 8:
            after_one(2 * t - 2)
            after_one(2 * t - 1)
        if 3 <= t < 9:
            convolve(taps_two, fwd_two, total_two, t - 3, 192)
        if 4 <= t < 10:
            after_two(2 * t - 8)
            after_two(2 * t - 7)
        if 6 <= t < 11:
            convolve(taps_three, back_two, total_three, t - 6, 160)
        if 7 <= t < 12:
            after_three(2 * t - 14)
            after_three(2 * t - 13)
        if t == 10:
            kernel_grad(turned_two, grad_two, 2, scale, grad_two_sum)
    activated[...] = rows[...].reshape(CH, 8, LN).astype(BF16)
    kernel_grad(turned_one, grad_one, 1, scale, grad_one_sum)

    column, row = here()
    position = column * 16 + row
    spare = lanes(48) >= CH
    for grad, source in ((1, grad_two_sum), (0, grad_one_sum)):
        for code in range(256):
            owner = jnp.bitwise_xor(position, path(code))
            start = 81 * (owner >> 3) + 10 * (owner & 7)
            packed[24 * code + 12 * grad : 24 * code + 12 * grad + 12, :] = source[
                pl.ds(start, 12), :
            ]
    for code in range(0, 256, 8):
        block = [packed[24 * code + 48 * k : 24 * code + 48 * k + 48, :] for k in range(4)]
        out = keep if code < 128 else send
        first = 144 * (code // 8 % 4)
        for k in range(3):
            mixed = jnp.where(spare, pltpu.roll(block[3], CH - 32 * k, 1), block[k])
            out[code // 32 % 4, first + 48 * k : first + 48 * k + 48, :] = mixed.astype(BF16)


def final_kernel(grad_one, masks, back_one, feature_grad, token, taps, total, rows):
    token[...] = jnp.zeros_like(token)
    for p in range(10):
        spread(taps, p, grad_one[p].astype(F32), 128)

    def after_four(p):
        value = half_of(total, p, 128)
        rows[pl.ds(p, CH, stride=8), :] = (value * masks[1, 64:192, :]).T[0:CH]

    for t in range(5):
        if t < 4:
            convolve(taps, back_one, total, t, 128)
        if t > 0:
            after_four(2 * t - 2)
            after_four(2 * t - 1)
    feature_grad[...] = rows[...].reshape(CH, 8, LN).astype(BF16)


def gather_kernel(a0, a1, a2, a3, token, *outs):
    for k, out in enumerate(outs):
        piece = slice(144 * k, 144 * k + 144)
        out[...] = sum(ref[piece, :].astype(F32) for ref in (a0, a1, a2, a3)).astype(BF16)


def unpack_kernel(a0, a1, a2, a3, hold, give):
    lane = lanes(48)
    a, b, c = (
        sum(ref[48 * k : 48 * k + 48, :].astype(F32) for ref in (a0, a1, a2, a3))
        for k in range(3)
    )
    last = jnp.where(
        lane < 32,
        pltpu.roll(a, 32, 1),
        jnp.where(lane < 64, pltpu.roll(b, 64, 1), pltpu.roll(c, 96, 1)),
    )
    for out, pair in ((hold, (a, b)), (give, (c, last))):
        out[...] = jnp.concatenate(pair, axis=0).astype(BF16)


def step_kernel(held, got, hold, give):
    size = hold.shape[0]
    total = held[...].astype(F32) + got[...].astype(F32)
    hold[...] = total[0:size].astype(hold.dtype)
    give[...] = total[size : 2 * size].astype(give.dtype)


def finish_kernel(held, got, out_one, out_two):
    j = lax.axis_index("north") & 7
    lane = lanes(1)
    value = held[...] + got[...]
    for grad, out in ((0, out_one), (1, out_two)):
        flat = []
        for m in range(3):
            r = [value[12 * grad + 4 * m + q : 12 * grad + 4 * m + q + 1] for q in range(4)]
            flat.append(jnp.where(lane < 96, r[0], pltpu.roll(r[1], 96, 1)))
            flat.append(jnp.where(lane < 64, pltpu.roll(r[1], 96, 1), pltpu.roll(r[2], 64, 1)))
            flat.append(jnp.where(lane < 32, pltpu.roll(r[2], 64, 1), pltpu.roll(r[3], 32, 1)))
        low = jnp.concatenate(flat[0:8], axis=0)
        high = jnp.concatenate(flat[1:9], axis=0)
        turn = lax.rem(LN - 12 * j, LN)
        out[...] = jnp.where(
            lanes(8) < LN - 12 * j, pltpu.roll(low, turn, 1), pltpu.roll(high, turn, 1)
        )


def call(kernel, name, outs, scratch, limit, flops, specs, *args):
    return pl.pallas_call(
        kernel,
        out_shape=outs,
        in_specs=specs,
        out_specs=[VMEM] * len(outs),
        scratch_shapes=scratch,
        compiler_params=pltpu.CompilerParams(vmem_limit_bytes=limit << 20),
        cost_estimate=pl.CostEstimate(flops=flops, bytes_accessed=1 << 20, transcendentals=0),
        name=name,
    )(*args)


def shape(*dims, dtype=BF16):
    return jax.ShapeDtypeStruct(dims, dtype)


def shift_by(step, axis):
    count = lax.axis_size(axis)
    return [(i, (i + step) % count) for i in range(count)]


def swap(value, bits):
    count = lax.axis_size("east") * lax.axis_size("north")
    return lax.ppermute(value, BOTH, [(i, i ^ bits) for i in range(count)])


def local(features, occupancy, weight_first, weight_second, cotangent):
    scale = 1.0 / math.sqrt(128 * 128 * 16)
    occupied = occupancy.reshape(1, 2)
    wide = pltpu.VMEM((CH * 8, LN), F32)
    near = pltpu.VMEM((CH, 8, LN), BF16)

    to_west, to_east = call(
        strips_kernel,
        "strips",
        [shape(STRIP, LN), shape(STRIP, LN)],
        [near, near, pltpu.VMEM((1, 2), jnp.int32), wide, wide, pltpu.SemaphoreType.DMA((3,))],
        60,
        1 << 20,
        [pl.BlockSpec(memory_space=pltpu.HBM)] * 3,
        occupied,
        features,
        cotangent,
    )
    west = lax.ppermute(to_east, "east", shift_by(1, "east"))
    east = lax.ppermute(to_west, "east", shift_by(-1, "east"))

    weight = shape(5, TAPS, LN)
    tile = shape(8, LN, LN)
    image = shape(CH, 8, LN)
    planes = shape(8, CH, LN)
    fwd_one, back_one, turned_one, own_grid, feat, cot, own_mask = call(
        prepare_kernel,
        "prepare",
        [weight] * 2 + [shape(288, 1024), tile, planes, planes, shape(16, LN)],
        [wide, wide],
        12,
        1 << 33,
        [VMEM] * 4,
        weight_first,
        features,
        cotangent,
        occupied,
    )
    to_south, to_north = call(
        rims_kernel,
        "rims",
        [shape(RIM, LN), shape(RIM, LN)],
        [],
        8,
        1 << 20,
        [VMEM] * 5,
        west,
        east,
        feat,
        cot,
        own_mask,
    )
    south = lax.ppermute(to_north, "north", shift_by(1, "north"))
    north = lax.ppermute(to_south, "north", shift_by(-1, "north"))
    side_grid, side_cot, middle = call(
        sides_kernel,
        "sides",
        [tile, shape(4, LN, LN), shape(3, LN, LN, dtype=F32)],
        [],
        8,
        1 << 31,
        [VMEM] * 3,
        own_mask,
        west,
        east,
    )

    inner_hidden, inner_slope = call(
        inner_kernel,
        "inner",
        [shape(14, 96, LN), shape(10, 96, LN, dtype=F32)],
        [pltpu.VMEM((8, 2, 96, TAPS), BF16), pltpu.VMEM((672, 2 * LN), F32)],
        16,
        1 << 32,
        [VMEM] * 4,
        own_grid,
        side_grid,
        middle,
        fwd_one,
    )
    fwd_two, back_two, own_cot = call(
        second_kernel,
        "second",
        [weight] * 2 + [tile],
        [],
        12,
        1 << 31,
        [VMEM] * 3,
        weight_second,
        cot,
        middle,
    )
    activated, grad_one, masks, keep, send = call(
        lambda *refs: level_kernel(scale, *refs),
        "level",
        [
            image,
            shape(10, 160, LN),
            shape(3, 256, LN, dtype=F32),
            shape(4, 576, LN),
            shape(4, 576, LN),
        ],
        [
            pltpu.VMEM((8, 2, 128, TAPS), BF16),
            pltpu.VMEM((7, 2, 192, TAPS), BF16),
            pltpu.VMEM((6, 2, 160, TAPS), BF16),
            pltpu.VMEM((7 * 128, 2 * LN), F32),
            pltpu.VMEM((6 * 192, 2 * LN), F32),
            pltpu.VMEM((5 * 160, 2 * LN), F32),
            pltpu.VMEM((16, 128, LN), F32),
            pltpu.VMEM((12, 192, LN), F32),
            pltpu.VMEM((10, 160, LN), F32),
            pltpu.VMEM((12, 192, LN), BF16),
            pltpu.VMEM((288, 1024), BF16),
            pltpu.VMEM((2592 + 16, LN), F32),
            pltpu.VMEM((2592 + 16, LN), F32),
            pltpu.VMEM((256 * 24, LN), F32),
            wide,
        ],
        40,
        1 << 34,
        [VMEM] * 13,
        own_grid,
        side_grid,
        own_cot,
        side_cot,
        middle,
        south,
        north,
        fwd_one,
        fwd_two,
        back_two,
        turned_one,
        inner_hidden,
        inner_slope,
    )

    part = (keep.astype(F32) + swap(send, 1).astype(F32)).astype(BF16)
    others = [swap(part[k], bits) for k, bits in ((2, 12), (1, 192), (3, 204))]
    feature_grad, token = call(
        final_kernel,
        "final",
        [image, shape(8, LN, dtype=F32)],
        [pltpu.VMEM((5, 2, 128, TAPS), BF16), pltpu.VMEM((512, 2 * LN), F32), wide],
        12,
        1 << 32,
        [VMEM] * 3,
        grad_one,
        masks,
        back_one,
    )
    pieces = call(
        gather_kernel,
        "gather",
        [shape(144, LN)] * 4,
        [],
        8,
        1 << 20,
        [VMEM] * 5,
        part[0],
        *others,
        token,
    )
    others = [swap(pieces[k], bits) for k, bits in ((2, 64), (1, 4), (3, 68))]
    held, given = call(
        unpack_kernel,
        "unpack",
        [shape(96, LN), shape(96, LN)],
        [],
        8,
        1 << 20,
        [VMEM] * 4,
        pieces[0],
        *others,
    )
    for partner, size, kind in ((48, 48, BF16), (16, 24, F32)):
        held, given = call(
            step_kernel,
            "step",
            [shape(size, LN, dtype=kind)] * 2,
            [],
            8,
            1 << 20,
            [VMEM] * 2,
            held,
            swap(given, partner),
        )
    one, two = call(
        finish_kernel,
        "finish",
        [shape(8, LN, dtype=F32), shape(8, LN, dtype=F32)],
        [],
        8,
        1 << 20,
        [VMEM] * 2,
        held,
        swap(given, 2),
    )
    return activated, feature_grad, one.reshape(-1)[0:972], two.reshape(-1)[0:972]


def solution(mesh):
    return jax.shard_map(
        local,
        mesh=mesh,
        in_specs=(
            P(None, "east", "north"),
            P("east", "north", None),
            P(),
            P(),
            P(None, "east", "north"),
        ),
        out_specs=(
            P(None, "east", "north"),
            P(None, "east", "north"),
            P(BOTH),
            P(BOTH),
        ),
        check_vma=False,
    )
```

```python
import math

import jax
import jax.numpy as jnp
from jax import lax
from jax.experimental import pallas as pl
from jax.experimental.pallas import tpu as pltpu
from jax.sharding import PartitionSpec as P

BOTH = ("east", "north")
F32 = jnp.float32
BF16 = jnp.bfloat16
CH = 96
LN = 128
TAPS = 7 * LN
WHOLE = (0, 2, 3, 5, 6, 7, 8)
SPLIT = (1, 1, 1, 4, 4, 4)
STRIP = 6 * CH + 16
RIM = 11 * CH + 48
VMEM = pl.BlockSpec(memory_space=pltpu.VMEM)
SMEM = pl.BlockSpec(memory_space=pltpu.SMEM)


def lanes(rows):
    return lax.broadcasted_iota(jnp.int32, (rows, LN), 1)


def flip_pad(value):
    wide = jnp.concatenate(
        [value.astype(F32), jnp.zeros((LN - value.shape[0], value.shape[1]), F32)], axis=0
    )
    return wide.T


def mask_column(ref, row):
    tile = ref[row : row + 16, :].astype(F32)
    return jnp.concatenate([tile] * 8, axis=0).T


def here():
    return lax.axis_index("east"), lax.axis_index("north")


def as_float(flag):
    return flag.astype(jnp.int32).astype(F32)


def neighbours():
    column, row = here()
    last_column, last_row = lax.axis_size("east") - 1, lax.axis_size("north") - 1
    flags = (column > 0, column < last_column, row > 0, row < last_row)
    return [as_float(flag) for flag in flags]


def mask_tile(occupied):
    levels = occupied[...].astype(F32)
    return jnp.where((lanes(16) & 15) < 8, levels[:, 0:1], levels[:, 1:2]).astype(BF16)


def cuts(rows, parts):
    tiles = rows // 16
    bounds = [16 * (tiles * k // parts) for k in range(parts + 1)]
    return list(zip(bounds, bounds[1:]))


def divide(whole, parts):
    for (low, high), part in zip(cuts(whole.shape[0], len(parts)), parts):
        part[...] = whole[low:high, :]


def unite(parts, whole):
    for (low, high), part in zip(cuts(whole.shape[0], len(parts)), parts):
        whole[low:high, :] = part[...]


def strips_parts(occupied, features, cotangent, *refs):
    to_west, to_east = refs[8:10]
    strips_kernel(occupied, features, cotangent, to_west, to_east, *refs[10:])
    divide(to_west, refs[0:4])
    divide(to_east, refs[4:8])


def rims_parts(*refs):
    west, east, to_south, to_north = refs[19:23]
    unite(refs[0:4], west)
    unite(refs[4:8], east)
    rims_kernel(west, east, *refs[8:11], to_south, to_north)
    divide(to_south, refs[11:15])
    divide(to_north, refs[15:19])


def sides_parts(own_mask, *refs):
    west, east = refs[11:13]
    unite(refs[0:4], west)
    unite(refs[4:8], east)
    sides_kernel(own_mask, west, east, *refs[8:11])


def level_parts(scale, *refs):
    south, north = refs[-2:]
    unite(refs[5:9], south)
    unite(refs[9:13], north)
    level_kernel(scale, *refs[0:5], south, north, *refs[13:-2])


def strips_kernel(
    occupied,
    features,
    cotangent,
    to_west,
    to_east,
    near_feat,
    near_cot,
    near_occupied,
    wide_feat,
    wide_cot,
    sems,
):
    copies = [
        pltpu.make_async_copy(features, near_feat, sems.at[0]),
        pltpu.make_async_copy(cotangent, near_cot, sems.at[1]),
        pltpu.make_async_copy(occupied, near_occupied, sems.at[2]),
    ]
    for copy in copies:
        copy.start()
    for copy, near, wide, start, count in (
        (copies[0], near_feat, wide_feat, 0, 4),
        (copies[1], near_cot, wide_cot, 4, 2),
    ):
        copy.wait()
        wide[...] = near[...].astype(F32).reshape(CH * 8, LN)
        for k in range(count):
            rows = slice((start + k) * CH, (start + k + 1) * CH)
            to_west[rows, :] = wide[pl.ds(k, CH, stride=8), :].astype(BF16)
            to_east[rows, :] = wide[pl.ds(8 - count + k, CH, stride=8), :].astype(BF16)
    copies[2].wait()
    mask = mask_tile(near_occupied)
    to_west[6 * CH : STRIP, :] = mask
    to_east[6 * CH : STRIP, :] = mask


def turn_levels(value, x, turned):
    lane = lanes(CH) & 15
    below = jnp.where(lane == 0, 0.0, pltpu.roll(value, 1, 1))
    above = jnp.where(lane == 15, 0.0, pltpu.roll(value, LN - 1, 1))
    start = x * LN if isinstance(x, int) else pl.multiple_of(x * LN, LN)
    for c, moved in enumerate((below, value, above)):
        turned[c * CH : (c + 1) * CH, pl.ds(start, LN)] = moved.astype(BF16)


def pack_weights(source, ahead, back):
    for out in (ahead, back):
        out[...] = jnp.zeros_like(out)

    def body(plane, carry):
        for k in range(9):
            straight = source[9 * plane + k]
            turned = jnp.pad(
                source[26 - 9 * plane - k].astype(F32), ((0, LN - CH), (0, LN - CH))
            ).T.astype(BF16)
            if k in WHOLE:
                row = WHOLE.index(k) * LN
                ahead[plane + 1, row : row + CH, 0:CH] = straight
                back[plane + 1, row : row + CH, :] = turned[0:CH]
            else:
                for q in range(3):
                    row = (SPLIT.index(k) + q) * LN + CH
                    ahead[plane + 1, row : row + 32, 0:CH] = straight[32 * q : 32 * q + 32]
                    back[plane + 1, row : row + 32, :] = turned[32 * q : 32 * q + 32]
        return carry

    lax.fori_loop(0, 3, body, 0)


def prepare_kernel(
    weight,
    features,
    cotangent,
    occupied,
    ahead,
    back,
    turned_one,
    own_grid,
    feat,
    cot,
    own_mask,
    wide_feat,
    wide_cot,
):
    wide_feat[...] = features[...].astype(F32).reshape(CH * 8, LN)
    wide_cot[...] = cotangent[...].astype(F32).reshape(CH * 8, LN)
    own_mask[...] = mask_tile(occupied)
    pack_weights(weight, ahead, back)
    mask = jnp.concatenate([own_mask[...].astype(F32)] * 6, axis=0)
    for x in range(8):
        plain = wide_feat[pl.ds(x, CH, stride=8), :]
        feat[x] = plain.astype(BF16)
        value = plain * mask
        turn_levels(value, x, turned_one)
        own_grid[x] = flip_pad(value).astype(BF16)
        cot[x] = wide_cot[pl.ds(x, CH, stride=8), :].astype(BF16)


def second_kernel(weight, cot, middle, ahead, back, own_cot):
    pack_weights(weight, ahead, back)
    for x in range(8):
        own_cot[x] = flip_pad(cot[x]).astype(BF16)


def rims_kernel(west, east, feat, cot, own_mask, to_south, to_north):
    half = lanes(CH) < 64
    quarter = lanes(CH) // 32

    def feat_plane(p):
        if p < 4:
            return west[p * CH : (p + 1) * CH, :].astype(F32)
        if p < 12:
            return feat[p - 4].astype(F32)
        return east[(p - 12) * CH : (p - 11) * CH, :].astype(F32)

    def cot_plane(p):
        if p < 2:
            return west[(4 + p) * CH : (5 + p) * CH, :].astype(F32)
        if p < 10:
            return cot[p - 2].astype(F32)
        return east[(p - 6) * CH : (p - 5) * CH, :].astype(F32)

    for k in range(8):
        one, two = feat_plane(k), feat_plane(k + 8)
        rows = slice(k * CH, (k + 1) * CH)
        to_south[rows, :] = jnp.where(half, one, pltpu.roll(two, 64, 1)).astype(BF16)
        to_north[rows, :] = jnp.where(half, pltpu.roll(one, 64, 1), two).astype(BF16)
    for k in range(3):
        four = [cot_plane(k + 3 * q) for q in range(4)]
        rows = slice((8 + k) * CH, (9 + k) * CH)
        for out, shift in ((to_south, 0), (to_north, 32)):
            moved = [
                pltpu.roll(four[q], (32 * q + shift) % LN, 1) if (32 * q + shift) % LN else four[q]
                for q in range(4)
            ]
            packed = jnp.where(
                quarter < 2,
                jnp.where(quarter == 0, moved[0], moved[1]),
                jnp.where(quarter == 2, moved[2], moved[3]),
            )
            out[rows, :] = packed.astype(BF16)
    for out in (to_south, to_north):
        out[11 * CH : 11 * CH + 16, :] = west[6 * CH : STRIP, :]
        out[11 * CH + 16 : 11 * CH + 32, :] = own_mask[...]
        out[11 * CH + 32 : RIM, :] = east[6 * CH : STRIP, :]


def sides_kernel(own_mask, west, east, side_grid, side_cot, middle):
    has = neighbours()
    middle[0] = mask_column(west, 6 * CH) * has[0]
    middle[1] = mask_column(own_mask, 0)
    middle[2] = mask_column(east, 6 * CH) * has[1]
    for side, ref in ((0, west), (1, east)):
        for k in range(4):
            block = flip_pad(ref[k * CH : (k + 1) * CH, :]) * middle[2 * side]
            side_grid[4 * side + k] = block.astype(BF16)
        for k in range(2):
            side_cot[2 * side + k] = flip_pad(ref[(4 + k) * CH : (5 + k) * CH, :]).astype(BF16)


def spread(taps, plane, value, rows, first=0):
    count = rows + 32
    level = lax.broadcasted_iota(jnp.int32, (count, LN), 0) & 15
    below = jnp.where(level == 0, 0.0, pltpu.roll(value, 1, 0))
    above = jnp.where(level == 15, 0.0, pltpu.roll(value, count - 1, 0))
    spare = lanes(count) >= CH
    short = [moved.astype(BF16) for moved in (below, value, above)]
    rest = [
        jnp.where(spare, pltpu.roll(short[1], CH - 32 * q, 1), jnp.bfloat16(0)) for q in range(3)
    ]
    for n, k in enumerate(WHOLE):
        start = 16 * (k // 3)
        block = short[k % 3][start : start + rows]
        if n < 6:
            start = 16 * (SPLIT[n] // 3)
            block = block + rest[n % 3][start : start + rows]
        taps[plane // 2, plane % 2, first : first + rows, n * LN : (n + 1) * LN] = block


def convolve(taps, weight, total, pair, rows):
    left = jnp.concatenate(
        [taps[pair + j // 2, j % 2, 0:rows, :] for j in range(4)], axis=1
    )
    right = jnp.concatenate(
        [jnp.concatenate([weight[j + 1], weight[j]], axis=1) for j in range(4)], axis=0
    )
    total[pair * rows : (pair + 1) * rows, :] = jnp.dot(left, right, preferred_element_type=F32)


def half_of(total, p, rows):
    start = p % 2 * LN
    return total[p // 2 * rows : (p // 2 + 1) * rows, start : start + LN]


HOPS = (1, 12, 192, 64, 4, 48, 16, 2)


def path(code):
    mask = 0
    for k, hop in enumerate(HOPS):
        if code >> (7 - k) & 1:
            mask ^= hop
    return mask


def kernel_grad(turned, planes, shift, scale, result):
    def piece(k):
        a, b = k // 3, k % 3
        start = (shift + 1 - b) * 16
        return planes[shift + 1 - a : shift + 9 - a, start : start + 128, :].reshape(1024, LN)

    for k in range(0, 9, 2):
        right = jnp.concatenate([piece(k), piece(min(k + 1, 8))], axis=1)
        part = jnp.dot(turned[...], right, preferred_element_type=F32) * scale
        result[k * 288 : k * 288 + 288, :] = part[:, 0:LN]
        if k < 8:
            result[(k + 1) * 288 : (k + 1) * 288 + 288, :] = part[:, LN : 2 * LN]


def band(p, low, high):
    return int(p >= low) + int(p >= high)


def silu_parts(value):
    sigma = jax.nn.sigmoid(value)
    return (value * sigma).astype(BF16), sigma * (1.0 + value * (1.0 - sigma))


def inner_kernel(own_grid, side_grid, middle, fwd_one, hidden, slope, taps, total):
    for p in range(16):
        value = own_grid[p - 4] if 4 <= p < 12 else side_grid[p % 8]
        spread(taps, p, value.astype(F32), 96)
    left = jnp.concatenate(
        [taps[j // 2 : j // 2 + 7, j % 2, :, :].reshape(672, TAPS) for j in range(4)], axis=1
    )
    right = jnp.concatenate(
        [jnp.concatenate([fwd_one[j + 1], fwd_one[j]], axis=1) for j in range(4)], axis=0
    )
    total[...] = jnp.dot(left, right, preferred_element_type=F32)
    for p in range(14):
        parts = silu_parts(half_of(total, p, 96) * middle[band(p, 3, 11), 16:112, :])
        hidden[p] = parts[0]
        if 2 <= p < 12:
            slope[p - 2] = parts[1]


def level_kernel(
    scale,
    own_grid,
    side_grid,
    own_cot,
    side_cot,
    middle,
    south,
    north,
    fwd_one,
    fwd_two,
    back_two,
    turned_one,
    inner_hidden,
    inner_slope,
    activated,
    grad_one,
    masks,
    keep,
    send,
    taps_one,
    taps_two,
    taps_three,
    total_one,
    total_two,
    total_three,
    edge,
    upstream,
    slope_one,
    grad_two,
    turned_two,
    grad_one_sum,
    grad_two_sum,
    packed,
    rows,
):
    has = neighbours()
    for ref, flag, row in ((south, has[2], 0), (north, has[3], 192)):
        tile = ref[11 * CH : 11 * CH + 48, :].astype(F32) * flag
        turned = jnp.concatenate([tile, jnp.zeros((80, LN), F32)], axis=0).T[0:64]
        for bx in range(3):
            side = has[bx // 2] if bx != 1 else 1.0
            column = turned[:, 16 * bx : 16 * bx + 1] * side
            masks[bx, row : row + 64, :] = jnp.broadcast_to(column, (64, LN))
    masks[:, 64:192, :] = middle[...]

    for k in range(8):
        for ref, row in ((south, 0), (north, 64)):
            both = flip_pad(ref[k * CH : (k + 1) * CH, :])
            edge[k, row : row + 64, :] = both[0:64]
            edge[k + 8, row : row + 64, :] = both[64:128]
    for k in range(3):
        for ref, row in ((south, 0), (north, 160)):
            four = flip_pad(ref[(8 + k) * CH : (9 + k) * CH, :])
            for q in range(4):
                upstream[k + 3 * q, row : row + 32, :] = four[32 * q : 32 * q + 32]
    for k in range(2):
        upstream[k, 32:160, :] = side_cot[k].astype(F32)
        upstream[10 + k, 32:160, :] = side_cot[2 + k].astype(F32)
    for k in range(8):
        upstream[2 + k, 32:160, :] = own_cot[k].astype(F32)

    def begin(p):
        bx = band(p, 4, 12)
        value = own_grid[p - 4] if bx == 1 else side_grid[p % 8]
        low = edge[p, 0:64, :] * masks[bx, 0:64, :]
        high = edge[p, 64:128, :] * masks[bx, 192:256, :]
        value = value.astype(F32)
        spread(taps_one, p, jnp.concatenate([low, value[0:32]], axis=0), 64)
        spread(taps_one, p, jnp.concatenate([value[96:128], high], axis=0), 64, 64)

    def after_one(p):
        bx = band(p, 3, 11)
        mask = jnp.concatenate([masks[bx, 16:80, :], masks[bx, 176:240, :]], axis=0)
        hidden, slope = silu_parts(half_of(total_one, p, 128) * mask)
        if 2 <= p < 12:
            slope_one[p - 2, 0:32, :] = slope[32:64]
            slope_one[p - 2, 32:128, :] = inner_slope[p - 2]
            slope_one[p - 2, 128:160, :] = slope[64:96]
        hidden = jnp.concatenate([hidden[0:64], inner_hidden[p], hidden[64:128]], axis=0)
        hidden = hidden.astype(F32)
        spread(taps_two, p, hidden, 192)
        if 3 <= p < 11:
            turn_levels(hidden[48:176].T[0:CH], p - 3, turned_two)

    def after_two(p):
        mask = masks[band(p, 2, 10), 32:224, :]
        value = half_of(total_two, p, 192) * mask
        sigma = jax.nn.sigmoid(value)
        if 2 <= p < 10:
            rows[pl.ds(p - 2, CH, stride=8), :] = (value * sigma)[32:160].T[0:CH]
        slope = sigma * (1.0 + value * (1.0 - sigma))
        grad = upstream[p] * slope * mask
        grad_two[p] = grad.astype(BF16)
        spread(taps_three, p, grad, 160)

    def after_three(p):
        grad = half_of(total_three, p, 160) * slope_one[p] * masks[band(p, 1, 9), 48:208, :]
        grad_one[p] = grad.astype(BF16)

    for p in range(4):
        begin(p)
    for t in range(12):
        if t < 7:
            convolve(taps_one, fwd_one, total_one, t, 128)
        if t < 6:
            begin(2 * t + 4)
            begin(2 * t + 5)
        if 1 <= t < 8:
            after_one(2 * t - 2)
            after_one(2 * t - 1)
        if 3 <= t < 9:
            convolve(taps_two, fwd_two, total_two, t - 3, 192)
        if 4 <= t < 10:
            after_two(2 * t - 8)
            after_two(2 * t - 7)
        if 6 <= t < 11:
            convolve(taps_three, back_two, total_three, t - 6, 160)
        if 7 <= t < 12:
            after_three(2 * t - 14)
            after_three(2 * t - 13)
        if t == 10:
            kernel_grad(turned_two, grad_two, 2, scale, grad_two_sum)
    activated[...] = rows[...].reshape(CH, 8, LN).astype(BF16)
    kernel_grad(turned_one, grad_one, 1, scale, grad_one_sum)

    column, row = here()
    position = column * 16 + row
    spare = lanes(48) >= CH
    for grad, source in ((1, grad_two_sum), (0, grad_one_sum)):
        for code in range(256):
            owner = jnp.bitwise_xor(position, path(code))
            start = 81 * (owner >> 3) + 10 * (owner & 7)
            packed[24 * code + 12 * grad : 24 * code + 12 * grad + 12, :] = source[
                pl.ds(start, 12), :
            ]
    for code in range(0, 256, 8):
        block = [packed[24 * code + 48 * k : 24 * code + 48 * k + 48, :] for k in range(4)]
        out = keep if code < 128 else send
        first = 144 * (code // 8 % 4)
        for k in range(3):
            mixed = jnp.where(spare, pltpu.roll(block[3], CH - 32 * k, 1), block[k])
            out[code // 32 % 4, first + 48 * k : first + 48 * k + 48, :] = mixed.astype(BF16)


def final_kernel(grad_one, masks, back_one, feature_grad, token, taps, total, rows):
    token[...] = jnp.zeros_like(token)
    for p in range(10):
        spread(taps, p, grad_one[p].astype(F32), 128)

    def after_four(p):
        value = half_of(total, p, 128)
        rows[pl.ds(p, CH, stride=8), :] = (value * masks[1, 64:192, :]).T[0:CH]

    for t in range(5):
        if t < 4:
            convolve(taps, back_one, total, t, 128)
        if t > 0:
            after_four(2 * t - 2)
            after_four(2 * t - 1)
    feature_grad[...] = rows[...].reshape(CH, 8, LN).astype(BF16)


def gather_kernel(own, *refs):
    others, outs = refs[0:6], refs[7:11]
    for k, out in enumerate(outs):
        total = own[144 * k : 144 * k + 144, :].astype(F32)
        start = 144 * (k % 2)
        for ref in others[k // 2 :: 2]:
            total = total + ref[start : start + 144, :].astype(F32)
        out[...] = total.astype(BF16)


def unpack_kernel(a0, a1, a2, a3, hold, give):
    lane = lanes(48)
    a, b, c = (
        sum(ref[48 * k : 48 * k + 48, :].astype(F32) for ref in (a0, a1, a2, a3))
        for k in range(3)
    )
    last = jnp.where(
        lane < 32,
        pltpu.roll(a, 32, 1),
        jnp.where(lane < 64, pltpu.roll(b, 64, 1), pltpu.roll(c, 96, 1)),
    )
    for out, pair in ((hold, (a, b)), (give, (c, last))):
        out[...] = jnp.concatenate(pair, axis=0).astype(BF16)


def step_kernel(held, got, hold, give):
    size = hold.shape[0]
    total = held[...].astype(F32) + got[...].astype(F32)
    hold[...] = total[0:size].astype(hold.dtype)
    give[...] = total[size : 2 * size].astype(give.dtype)


def finish_kernel(held, got, out_one, out_two):
    j = lax.axis_index("north") & 7
    lane = lanes(1)
    value = held[...] + got[...]
    for grad, out in ((0, out_one), (1, out_two)):
        flat = []
        for m in range(3):
            r = [value[12 * grad + 4 * m + q : 12 * grad + 4 * m + q + 1] for q in range(4)]
            flat.append(jnp.where(lane < 96, r[0], pltpu.roll(r[1], 96, 1)))
            flat.append(jnp.where(lane < 64, pltpu.roll(r[1], 96, 1), pltpu.roll(r[2], 64, 1)))
            flat.append(jnp.where(lane < 32, pltpu.roll(r[2], 64, 1), pltpu.roll(r[3], 32, 1)))
        low = jnp.concatenate(flat[0:8], axis=0)
        high = jnp.concatenate(flat[1:9], axis=0)
        turn = lax.rem(LN - 12 * j, LN)
        out[...] = jnp.where(
            lanes(8) < LN - 12 * j, pltpu.roll(low, turn, 1), pltpu.roll(high, turn, 1)
        )


def call(kernel, name, outs, scratch, limit, flops, specs, *args):
    return pl.pallas_call(
        kernel,
        out_shape=outs,
        in_specs=specs,
        out_specs=[VMEM] * len(outs),
        scratch_shapes=scratch,
        compiler_params=pltpu.CompilerParams(vmem_limit_bytes=limit << 20),
        cost_estimate=pl.CostEstimate(flops=flops, bytes_accessed=1 << 20, transcendentals=0),
        name=name,
    )(*args)


def shape(*dims, dtype=BF16):
    return jax.ShapeDtypeStruct(dims, dtype)


def shift_by(step, axis):
    count = lax.axis_size(axis)
    return [(i, (i + step) % count) for i in range(count)]


def swap(value, bits):
    count = lax.axis_size("east") * lax.axis_size("north")
    return lax.ppermute(value, BOTH, [(i, i ^ bits) for i in range(count)])


def local(features, occupancy, weight_first, weight_second, cotangent):
    scale = 1.0 / math.sqrt(128 * 128 * 16)
    occupied = occupancy.reshape(1, 2)
    wide = pltpu.VMEM((CH * 8, LN), F32)
    near = pltpu.VMEM((CH, 8, LN), BF16)

    strip_parts = [shape(high - low, LN) for low, high in cuts(STRIP, 4)]
    rim_parts = [shape(high - low, LN) for low, high in cuts(RIM, 4)]
    strip = pltpu.VMEM((STRIP, LN), BF16)
    rim = pltpu.VMEM((RIM, LN), BF16)
    moving = call(
        strips_parts,
        "strips",
        strip_parts * 2,
        [strip, strip, near, near, pltpu.VMEM((1, 2), jnp.int32), wide, wide, pltpu.SemaphoreType.DMA((3,))],
        60,
        1 << 20,
        [pl.BlockSpec(memory_space=pltpu.HBM)] * 3,
        occupied,
        features,
        cotangent,
    )
    west, east = [], []
    for k in range(4):
        west.append(lax.ppermute(moving[4 + k], "east", shift_by(1, "east")))
        east.append(lax.ppermute(moving[k], "east", shift_by(-1, "east")))

    weight = shape(5, TAPS, LN)
    tile = shape(8, LN, LN)
    image = shape(CH, 8, LN)
    planes = shape(8, CH, LN)
    fwd_one, back_one, turned_one, own_grid, feat, cot, own_mask = call(
        prepare_kernel,
        "prepare",
        [weight] * 2 + [shape(288, 1024), tile, planes, planes, shape(16, LN)],
        [wide, wide],
        12,
        1 << 33,
        [VMEM] * 4,
        weight_first,
        features,
        cotangent,
        occupied,
    )
    moving = call(
        rims_parts,
        "rims",
        rim_parts * 2,
        [strip, strip, rim, rim],
        8,
        1 << 20,
        [VMEM] * 11,
        *west,
        *east,
        feat,
        cot,
        own_mask,
    )
    south, north = [], []
    for k in range(4):
        south.append(lax.ppermute(moving[4 + k], "north", shift_by(1, "north")))
        north.append(lax.ppermute(moving[k], "north", shift_by(-1, "north")))
    side_grid, side_cot, middle = call(
        sides_parts,
        "sides",
        [tile, shape(4, LN, LN), shape(3, LN, LN, dtype=F32)],
        [strip, strip],
        8,
        1 << 31,
        [VMEM] * 9,
        own_mask,
        *west,
        *east,
    )

    inner_hidden, inner_slope = call(
        inner_kernel,
        "inner",
        [shape(14, 96, LN), shape(10, 96, LN, dtype=F32)],
        [pltpu.VMEM((8, 2, 96, TAPS), BF16), pltpu.VMEM((672, 2 * LN), F32)],
        16,
        1 << 32,
        [VMEM] * 4,
        own_grid,
        side_grid,
        middle,
        fwd_one,
    )
    fwd_two, back_two, own_cot = call(
        second_kernel,
        "second",
        [weight] * 2 + [tile],
        [],
        12,
        1 << 31,
        [VMEM] * 3,
        weight_second,
        cot,
        middle,
    )
    activated, grad_one, masks, keep, send = call(
        lambda *refs: level_parts(scale, *refs),
        "level",
        [
            image,
            shape(10, 160, LN),
            shape(3, 256, LN, dtype=F32),
            shape(4, 576, LN),
            shape(4, 576, LN),
        ],
        [
            pltpu.VMEM((8, 2, 128, TAPS), BF16),
            pltpu.VMEM((7, 2, 192, TAPS), BF16),
            pltpu.VMEM((6, 2, 160, TAPS), BF16),
            pltpu.VMEM((7 * 128, 2 * LN), F32),
            pltpu.VMEM((6 * 192, 2 * LN), F32),
            pltpu.VMEM((5 * 160, 2 * LN), F32),
            pltpu.VMEM((16, 128, LN), F32),
            pltpu.VMEM((12, 192, LN), F32),
            pltpu.VMEM((10, 160, LN), F32),
            pltpu.VMEM((12, 192, LN), BF16),
            pltpu.VMEM((288, 1024), BF16),
            pltpu.VMEM((2592 + 16, LN), F32),
            pltpu.VMEM((2592 + 16, LN), F32),
            pltpu.VMEM((256 * 24, LN), F32),
            wide,
            rim,
            rim,
        ],
        40,
        1 << 34,
        [VMEM] * 19,
        own_grid,
        side_grid,
        own_cot,
        side_cot,
        middle,
        *south,
        *north,
        fwd_one,
        fwd_two,
        back_two,
        turned_one,
        inner_hidden,
        inner_slope,
    )

    part = (keep.astype(F32) + swap(send, 1).astype(F32)).astype(BF16)
    halves = {
        (k, half): swap(part[k, 288 * half : 288 * half + 288], bits)
        for half in range(2)
        for k, bits in ((2, 12), (1, 192), (3, 204))
    }
    others = [halves[k, half] for k in (2, 1, 3) for half in range(2)]
    feature_grad, token = call(
        final_kernel,
        "final",
        [image, shape(8, LN, dtype=F32)],
        [pltpu.VMEM((5, 2, 128, TAPS), BF16), pltpu.VMEM((512, 2 * LN), F32), wide],
        12,
        1 << 32,
        [VMEM] * 3,
        grad_one,
        masks,
        back_one,
    )
    pieces = call(
        gather_kernel,
        "gather",
        [shape(144, LN)] * 4,
        [],
        8,
        1 << 20,
        [VMEM] * 8,
        part[0],
        *others,
        token,
    )
    others = [swap(pieces[k], bits) for k, bits in ((2, 64), (1, 4), (3, 68))]
    held, given = call(
        unpack_kernel,
        "unpack",
        [shape(96, LN), shape(96, LN)],
        [],
        8,
        1 << 20,
        [VMEM] * 4,
        pieces[0],
        *others,
    )
    for partner, size, kind in ((48, 48, BF16), (16, 24, F32)):
        held, given = call(
            step_kernel,
            "step",
            [shape(size, LN, dtype=kind)] * 2,
            [],
            8,
            1 << 20,
            [VMEM] * 2,
            held,
            swap(given, partner),
        )
    one, two = call(
        finish_kernel,
        "finish",
        [shape(8, LN, dtype=F32), shape(8, LN, dtype=F32)],
        [],
        8,
        1 << 20,
        [VMEM] * 2,
        held,
        swap(given, 2),
    )
    return activated, feature_grad, one.reshape(-1)[0:972], two.reshape(-1)[0:972]


def solution(mesh):
    return jax.shard_map(
        local,
        mesh=mesh,
        in_specs=(
            P(None, "east", "north"),
            P("east", "north", None),
            P(),
            P(),
            P(None, "east", "north"),
        ),
        out_specs=(
            P(None, "east", "north"),
            P(None, "east", "north"),
            P(BOTH),
            P(BOTH),
        ),
        check_vma=False,
    )
```
